32 devices in a mesh: gx: 2 (over x), gy: 16 (over z, y, core).
Axes of the slice: x: 2, y: 2, z: 4, core: 2. Of those that a mesh axis runs over, the one named last changes fastest.
Arguments:
- pressure: float32 [8, 8, 2048], P('gx', None, 'gy'), may hold values from -6 to 6
- saturation: float32 [2, 8, 8, 2048], P(None, 'gx', None, 'gy'), may hold values from 0.05 to 0.45
- saturation_old: float32 [2, 8, 8, 2048], P(None, 'gx', None, 'gy'), may hold values from 0.05 to 0.45
- pore_volume: float32 [8, 8, 2048], P('gx', None, 'gy'), may hold values from 0.4 to 25.6
- permeability: float32 [8, 8, 2048], P('gx', None, 'gy'), may hold values from 0.1 to 10
- jac_diag: float32 [3, 3, 8, 8, 2048], P(None, None, 'gx', None, 'gy'), may hold values from -0.2 to 1, as said below
- jac_off: float32 [6, 3, 3, 8, 8, 2048], P(None, None, None, 'gx', None, 'gy'), may hold values from -0.05 to 0.05
- perf_cell: int32 [2, 2048], P('gx', 'gy'), may hold values from 0 to 4095
- perf_well: int32 [2, 2048], P('gx', 'gy'), may hold values from 0 to 127, as said below
- perf_index: float32 [2, 2048], P('gx', 'gy'), may hold values from 0.5 to 4
- well_rate: float32 [2, 128], P('gx', 'gy'), may hold values from 1 to 8
Outputs:
- residual: float32 [3, 8, 8, 2048], P(None, 'gx', None, 'gy')
- update: float32 [3, 8, 8, 2048], P(None, 'gx', None, 'gy')
The draws below stay inside these ranges and needn't reach their ends.
Inputs may be any that keep to these rules, and one draw needn't show every extreme that they name: `perf_well`: every one of the 128 wells of a row (one index of gx) has at least one perforation in that row. `jac_diag`: in every 3 x 3 block each diagonal entry exceeds the sum of the magnitudes of the other entries of its row.
All inputs are finite; a program needn't handle non-finite values.
Results may differ from the reference program's by a relative error of at most 0.0003.
Values sent between devices are 32-bit elements; how exact they have to be, the bound alone decides.
No kernel may reach another device: no remote copies, remote signals or barrier semaphores. Data moves between devices by JAX's collectives and lax.ppermute only.
A program may use at most 64 MiB of HBM per device.

```python
import math
import jax
import jax.numpy as jnp
from jax import lax

CX = 4
CY = 128
NZL = 8
PERF_DEV = 128
SWEEPS = 4
NX = 8
NY = 2048
ROW_WELLS = 128
ROW_PERFS = 2048
N_GX = 2


def draw_pore_volume(key, part):
    shape_all = (NX, NZL, NY)
    first_pos = (jnp.arange(NX, dtype=jnp.float32) / max(NX - 1, 1))[:, None, None]
    second_pos = (jnp.arange(NY, dtype=jnp.float32) / max(NY - 1, 1))[None, None, :]
    rough = jnp.exp(jax.random.uniform(jax.random.fold_in(key, 11), shape_all, jnp.float32, jnp.log(0.5), jnp.log(2.0)))
    trend = 8.0 ** (0.7 * first_pos + 0.3 * second_pos)
    return (rough * trend).astype(jnp.float32)


def draw_jac_diag(key, part):
    spread = jax.random.uniform(jax.random.fold_in(key, 21), (3, 3, NX, NZL, NY), jnp.float32, -0.2, 0.2)
    leading = jax.random.uniform(jax.random.fold_in(key, 22), (3, NX, NZL, NY), jnp.float32, 0.6, 1.0)
    column = jax.random.uniform(jax.random.fold_in(key, 23), (2, NX, NZL, NY), jnp.float32, 0.0, 0.2)
    identity = jnp.eye(3, dtype=jnp.float32)[:, :, None, None, None]
    blocks = spread * (1.0 - identity) + identity * leading[None]
    blocks = blocks.at[1:, 0].set(column)
    return blocks.astype(jnp.float32)


def draw_jac_off(key, part):
    spread = jax.random.uniform(jax.random.fold_in(key, 31), (6, 3, 3, NX, NZL, NY), jnp.float32, -0.05, 0.05)
    column = -jax.random.uniform(jax.random.fold_in(key, 32), (6, 3, NX, NZL, NY), jnp.float32, 0.005, 0.045)
    return spread.at[:, :, 0].set(column).astype(jnp.float32)


def draw_perf_well(key, part):

    def one_row(row_key):
        slots = jnp.arange(ROW_PERFS, dtype=jnp.int32)
        first_pick = jax.random.randint(jax.random.fold_in(row_key, 1), (ROW_PERFS,), 0, ROW_WELLS, dtype=jnp.int32)
        second_pick = jax.random.randint(jax.random.fold_in(row_key, 2), (ROW_PERFS,), 0, ROW_WELLS, dtype=jnp.int32)
        chosen = jnp.where(slots < ROW_WELLS, slots, jnp.minimum(first_pick, second_pick))
        relabel = jax.random.permutation(jax.random.fold_in(row_key, 3), jnp.arange(ROW_WELLS, dtype=jnp.int32))
        chosen = relabel[chosen]
        order = jax.random.permutation(jax.random.fold_in(row_key, 4), jnp.arange(ROW_PERFS, dtype=jnp.int32))
        return chosen[order]
    row_keys = jax.vmap(lambda row_at: jax.random.fold_in(jax.random.fold_in(key, 41), row_at))(jnp.arange(N_GX, dtype=jnp.int32))
    return jax.vmap(one_row)(row_keys).astype(jnp.int32)


def plant(result, rng, low, high):
    place = [jax.random.randint(jax.random.fold_in(rng, axis), (), 0, length) for axis, length in enumerate(result.shape)]
    main_axis = result.shape.index(max(result.shape))
    next_to = place[:main_axis] + [(place[main_axis] + 1) % result.shape[main_axis]] + place[main_axis + 1:]
    return result.at[tuple(place)].set(low).at[tuple(next_to)].set(high)


def level_of(stream_key, shape, pieces, least, high):
    factor_of, own = 1.0, jax.random.fold_in(stream_key, 6)
    for position, parts in pieces:
        heights = jnp.exp(jax.random.uniform(jax.random.fold_in(own, position), (parts,), jnp.float32, least / len(pieces), high / len(pieces)))
        factor_of = factor_of * jnp.repeat(heights, shape[position] // parts).reshape([-1 if axis == position else 1 for axis in range(len(shape))])
    return factor_of


def noise(stream_key, extent, width, bound, pieces=(), kind=jnp.bfloat16):
    result = jax.random.normal(stream_key, extent, jnp.float32) * width
    if len(pieces) > 0:
        result = level_of(stream_key, extent, pieces, -0.22, 0.18) * result
    return jnp.clip(result, min=-bound, max=bound).astype(kind)


def setup_inputs(seed: int = 0) -> dict:
    splits = jax.random.split(jax.random.key(seed), 12)
    return {
        "pressure": noise(splits[0], (NX, NZL, NY), 1.0, 6.0, ((0, 2), (2, 16)), jnp.float32),
        "saturation": jnp.clip(0.05 + 0.39999999 * jax.random.uniform(splits[1], (2, NX, NZL, NY), jnp.float32) ** level_of(splits[1], (2, NX, NZL, NY), ((1, 2), (3, 16)), -0.2, 0.2), 0.05, 0.45),
        "saturation_old": jnp.clip(0.05 + 0.39999999 * jax.random.uniform(splits[2], (2, NX, NZL, NY), jnp.float32) ** level_of(splits[2], (2, NX, NZL, NY), ((1, 2), (3, 16)), -0.2, 0.2), 0.05, 0.45),
        "pore_volume": draw_pore_volume(jax.random.fold_in(splits[11], 71), 0),
        "permeability": jnp.clip(jnp.exp(math.log(10.0) - 4.6051702 * jax.random.uniform(splits[4], (NX, NZL, NY), jnp.float32) ** level_of(splits[4], (NX, NZL, NY), ((0, 2), (2, 16)), -0.2, 0.2)), 0.1, 10.0),
        "jac_diag": draw_jac_diag(jax.random.fold_in(splits[11], 71), 0),
        "jac_off": draw_jac_off(jax.random.fold_in(splits[11], 71), 0),
        "perf_cell": plant(jax.random.randint(splits[7], (N_GX, ROW_PERFS), 0, CX * NZL * CY), jax.random.fold_in(splits[7], 1), 0, (CX * NZL * CY) - 1).astype(jnp.int32),
        "perf_well": draw_perf_well(jax.random.fold_in(splits[11], 71), 0),
        "perf_index": jnp.clip(jnp.exp(math.log(4.0) - 2.0794415 * jax.random.uniform(splits[9], (N_GX, ROW_PERFS), jnp.float32) ** level_of(splits[9], (N_GX, ROW_PERFS), ((0, 2), (1, 16)), -0.2, 0.2)), 0.5, 4.0),
        "well_rate": jnp.clip(jnp.exp(math.log(8.0) - 2.0794415 * jax.random.uniform(splits[10], (N_GX, ROW_WELLS), jnp.float32) ** level_of(splits[10], (N_GX, ROW_WELLS), ((0, 2), (1, 16)), -0.2, 0.2)), 1.0, 8.0),
    }


viscosity = (1.0, 2.0, 0.2)
vertical_ratio = 0.1
highest = lax.Precision.HIGHEST

def beside_all(padded):
    return [padded[..., :-2, 1:-1, 1:-1], padded[..., 2:, 1:-1, 1:-1], padded[..., 1:-1, 1:-1, :-2], padded[..., 1:-1, 1:-1, 2:], padded[..., 1:-1, :-2, 1:-1], padded[..., 1:-1, 2:, 1:-1]]

def phases(sat):
    return jnp.stack([sat[0], 1.0 - sat[0] - sat[1], sat[1]])

def mobilities(water_sat, gas_sat):
    oil_sat = 1.0 - water_sat - gas_sat
    return jnp.stack([water_sat * water_sat / viscosity[0], oil_sat * oil_sat / viscosity[1], gas_sat * gas_sat / viscosity[2]])

def flux_terms(center, padded):
    nearby = beside_all(padded)
    pressure_here = center[0]
    mobile = center[1:4]
    perm_here = center[4]
    summed = jnp.zeros_like(mobile)
    for facing in range(6):
        beyond = nearby[facing]
        conduct = 2.0 * perm_here * beyond[4] / (perm_here + beyond[4])
        if facing >= 4:
            conduct = vertical_ratio * conduct
        pressure_drop = pressure_here - beyond[0]
        upwind = jnp.where(pressure_drop >= 0.0, mobile, beyond[1:4])
        summed = summed + conduct * upwind * pressure_drop
    return summed

def block_solve(matrix, target):

    def cofactor(row_at, col_at):
        return matrix[(row_at + 1) % 3, (col_at + 1) % 3] * matrix[(row_at + 2) % 3, (col_at + 2) % 3] - matrix[(row_at + 1) % 3, (col_at + 2) % 3] * matrix[(row_at + 2) % 3, (col_at + 1) % 3]
    cofactors = [[cofactor(row_at, col_at) for col_at in range(3)] for row_at in range(3)]
    determinant = matrix[0, 0] * cofactors[0][0] + matrix[0, 1] * cofactors[0][1] + matrix[0, 2] * cofactors[0][2]
    solved = [(cofactors[0][col_at] * target[0] + cofactors[1][col_at] * target[1] + cofactors[2][col_at] * target[2]) / determinant for col_at in range(3)]
    return jnp.stack(solved)

def jacobian_times(jac_diag, jac_off, values, nearby):
    local_part = jnp.einsum('abxzy,bxzy->axzy', jac_diag, values, precision=highest)
    return local_part + jnp.einsum('qabxzy,qbxzy->axzy', jac_off, nearby, precision=highest)

def precondition(vector, jac_diag, jac_off, near_fn):
    press_diag = jac_diag[0, 0] + jac_diag[1, 0] + jac_diag[2, 0]
    press_off = jac_off[:, 0, 0] + jac_off[:, 1, 0] + jac_off[:, 2, 0]
    restricted = vector[0] + vector[1] + vector[2]
    pressure_part = restricted / press_diag
    for sweep_index in range(1, SWEEPS):
        nearby = near_fn(pressure_part[None])[:, 0]
        pressure_part = (restricted - lax.optimization_barrier(jnp.sum(press_off * nearby, axis=0))) / press_diag
    nearby = near_fn(pressure_part[None])[:, 0]
    coupled = jac_diag[:, 0] * pressure_part + lax.optimization_barrier(jnp.sum(jac_off[:, :, 0] * nearby[:, None], axis=0))
    correction = block_solve(jac_diag, vector - coupled)
    empty = jnp.zeros_like(pressure_part)
    return correction + jnp.stack([pressure_part, empty, empty])

def near_global(stack):
    return jnp.stack(beside_all(jnp.pad(stack, ((0, 0), (1, 1), (1, 1), (1, 1)))))

def reference(pressure, saturation, saturation_old, pore_volume, permeability, jac_diag, jac_off, perf_cell, perf_well, perf_index, well_rate):
    mobile = mobilities(saturation[0], saturation[1])
    center = jnp.concatenate([pressure[None], mobile, permeability[None]])
    padded = jnp.pad(center, ((0, 0), (1, 1), (1, 1), (1, 1)))
    residual = pore_volume * (phases(saturation) - phases(saturation_old)) + flux_terms(center, padded)
    row_ids = jnp.arange(N_GX, dtype=jnp.int32)[:, None]
    owner_col = (jnp.arange(ROW_PERFS, dtype=jnp.int32) // PERF_DEV)[None, :]
    row_local = perf_cell // (NZL * CY)
    layer_local = perf_cell // CY % NZL
    col_local = perf_cell % CY
    flat_cells = ((row_ids * CX + row_local) * NZL + layer_local) * NY + owner_col * CY + col_local
    flat_cells = flat_cells.reshape(-1).astype(jnp.int32)
    pressure_at = pressure.reshape(-1)[flat_cells]
    mobile_at = mobile.reshape(3, -1)[:, flat_cells]
    index_vals = perf_index.reshape(-1)
    strength = index_vals * lax.optimization_barrier(jnp.sum(mobile_at, axis=0))
    weighted = strength * pressure_at
    well_ids = (row_ids * ROW_WELLS + perf_well).reshape(-1).astype(jnp.int32)
    well_count = N_GX * ROW_WELLS
    sum_strength = jax.ops.segment_sum(strength, well_ids, num_segments=well_count)
    sum_weighted = jax.ops.segment_sum(weighted, well_ids, num_segments=well_count)
    bottom = (sum_weighted - well_rate.reshape(-1)) / sum_strength
    perf_rates = index_vals * mobile_at * (pressure_at - bottom[well_ids])
    residual = residual.reshape(3, -1).at[:, flat_cells].add(perf_rates).reshape(residual.shape)
    initial = -residual
    norm_start = jnp.sqrt(jnp.sum(initial * initial))
    basis_vector = initial / norm_start
    direction = precondition(basis_vector, jac_diag, jac_off, near_global)
    mapped = jacobian_times(jac_diag, jac_off, direction, near_global(direction))
    projection_coef = jnp.sum(mapped * basis_vector)
    remainder = mapped - projection_coef * basis_vector
    remainder_norm = jnp.sqrt(jnp.sum(remainder * remainder))
    step_length = norm_start * projection_coef / (projection_coef * projection_coef + remainder_norm * remainder_norm)
    update = step_length * direction
    return (residual, update)
```

```python
import functools

import jax
import jax.numpy as jnp
from jax import lax
from jax.experimental import pallas as pl
from jax.experimental.pallas import tpu as pltpu
from jax.sharding import PartitionSpec as P

SWEEPS = 4
WIDE = SWEEPS + 2

viscosity = (1.0, 2.0, 0.2)
vertical_ratio = 0.1
highest = lax.Precision.HIGHEST
f32 = jnp.float32

PRESS, MOB, PERM, ACC, INV, COEF = 0, 1, 4, 5, 8, 9
BULK = 15
DINV, DCOL, OFFC = 0, 9, 12
EDGE = 30
EDGE_AT = BULK * WIDE
NT = (((1,), (1,)), ((), ()))
NN = (((1,), (0,)), ((), ()))


def iota(shape, axis):
    return lax.broadcasted_iota(jnp.int32, shape, axis)


def split_dot(values, hot, dims):
    rows = values.shape[0]
    high = values.astype(jnp.bfloat16)
    rest = values - high.astype(f32)
    mid = rest.astype(jnp.bfloat16)
    low = (rest - mid.astype(f32)).astype(jnp.bfloat16)
    parts = jnp.concatenate([high, mid, low], axis=0)
    out = lax.dot_general(parts, hot, dims, preferred_element_type=f32)
    return out[:rows] + (out[rows : 2 * rows] + out[2 * rows :])


def hot_of(condition):
    return jnp.where(condition, 1.0, 0.0).astype(jnp.bfloat16)


def window(count, cx):
    reach = -(-WIDE // cx)
    if count <= 2 * reach + 1:
        return list(range(count))
    return list(range(reach + 1)) + list(range(-reach, 0))


def before_kernel(
    count_x,
    count_y,
    press_ref,
    sat_ref,
    old_ref,
    pore_ref,
    perm_ref,
    diag_ref,
    off_ref,
    cell_ref,
    well_ref,
    index_ref,
    rate_ref,
    wells_out,
    block_out,
    ya_out,
    yb_out,
    dinv_out,
):
    cx, nz, cy = press_ref.shape
    at_x = lax.axis_index("gx")
    at_y = lax.axis_index("gy")
    layers = 1 if count_x == 2 else 2
    last = block_out.shape[0] - 1

    press = press_ref[...]
    water, gas = sat_ref[0], sat_ref[1]
    oil = 1.0 - water - gas
    mobile = [
        water * water / viscosity[0],
        oil * oil / viscosity[1],
        gas * gas / viscosity[2],
    ]

    cells = cell_ref[...]
    perfs = cells.shape[1]
    spot_xz = lax.div(cells, cy)
    spot_y = lax.rem(cells, cy)
    stacked = jnp.concatenate([m.reshape(cx * nz, cy) for m in mobile + [press]], axis=0)
    hot_y = hot_of(iota((cy, perfs), 0) == spot_y)
    picked = split_dot(stacked, hot_y, NN).reshape(4, cx * nz, perfs)
    on_xz = iota((cx * nz, perfs), 0) == spot_xz
    at_perf = [
        jnp.sum(jnp.where(on_xz, picked[i], 0.0), axis=0, keepdims=True) for i in range(4)
    ]
    index_vals = index_ref[...]
    parts = [index_vals * at_perf[i] for i in range(3)]
    strength = index_vals * (at_perf[0] + at_perf[1] + at_perf[2])
    weighted = strength * at_perf[3]
    row = iota((8, perfs), 0)
    both = jnp.where(row == 0, strength, jnp.where(row == 1, weighted, 0.0))
    wells = wells_out.shape[2]
    member = jnp.where(iota((wells, perfs), 0) == well_ref[...], 1.0, 0.0)
    sums = lax.dot_general(both, member, NT, precision=highest, preferred_element_type=f32)
    owned = rate_ref.shape[1]
    square = jnp.broadcast_to(rate_ref[...], (owned, owned))
    column = jnp.sum(
        jnp.where(iota((owned, owned), 0) == iota((owned, owned), 1), square, 0.0),
        axis=1,
        keepdims=True,
    )
    mine = iota((owned, wells), 1) == at_y * owned + iota((owned, wells), 0)
    rates = jnp.sum(jnp.where(mine, column, 0.0), axis=0, keepdims=True)
    pair = sums[:2] - jnp.where(iota((2, wells), 0) == 1, rates, 0.0)
    wells_out[...] = jnp.broadcast_to(pair[None], wells_out.shape)

    perf_rows = [
        spot_xz.astype(f32),
        spot_y.astype(f32),
        well_ref[...].astype(f32),
        *parts,
        at_perf[3],
        jnp.zeros_like(at_perf[3]),
    ]
    for r, values in enumerate(perf_rows):
        block_out[last, r : r + 1, :] = values
        ya_out[cx, r : r + 1, :] = values
        yb_out[cx, r : r + 1, :] = values

    old_water, old_gas = old_ref[0], old_ref[1]
    old_oil = 1.0 - old_water - old_gas
    pore = pore_ref[...]
    accumulated = [pore * (water - old_water), pore * (oil - old_oil), pore * (gas - old_gas)]
    layer_at = iota((cx, nz, cy), 1)
    columns = [[off_ref[q, c, 0] for c in range(3)] for q in range(6)]
    columns[4] = [jnp.where(layer_at > 0, v, 0.0) for v in columns[4]]
    columns[5] = [jnp.where(layer_at < nz - 1, v, 0.0) for v in columns[5]]
    diag = [[diag_ref[a, b] for b in range(3)] for a in range(3)]
    inverse = 1.0 / (diag[0][0] + diag[1][0] + diag[2][0])
    coefs = [(columns[q][0] + columns[q][1] + columns[q][2]) * inverse for q in range(6)]
    bulk = [press, *mobile, perm_ref[...], *accumulated, inverse, *coefs]

    def cofactor(a, b):
        return (
            diag[(a + 1) % 3][(b + 1) % 3] * diag[(a + 2) % 3][(b + 2) % 3]
            - diag[(a + 1) % 3][(b + 2) % 3] * diag[(a + 2) % 3][(b + 1) % 3]
        )

    cofactors = [[cofactor(a, b) for b in range(3)] for a in range(3)]
    over = 1.0 / (
        diag[0][0] * cofactors[0][0] + diag[0][1] * cofactors[0][1] + diag[0][2] * cofactors[0][2]
    )
    solve = [cofactors[b][a] * over for a in range(3) for b in range(3)]
    for i in range(9):
        dinv_out[i] = solve[i]
    edge = solve + [diag[c][0] for c in range(3)] + [columns[q][c] for q in range(6) for c in range(3)]

    for f in range(BULK):
        block_out[f * cx : (f + 1) * cx] = bulk[f]
    base = BULK * cx
    for e in range(EDGE):
        if layers == 1:
            block_out[base + e] = jnp.where(at_x == 0, edge[e][cx - 1], edge[e][0])
        else:
            block_out[base + e] = edge[e][0]
            block_out[base + EDGE + e] = edge[e][cx - 1]

    lane = iota((nz, cy), 1)
    to_left = [jnp.zeros((nz, cy), f32) for _ in range(cx)]
    to_right = [jnp.zeros((nz, cy), f32) for _ in range(cx)]
    for f in range(BULK + EDGE):
        wide = WIDE if f < BULK else 1
        shift = f * WIDE if f < BULK else EDGE_AT + f - BULK
        on_left = (lane >= shift) & (lane < shift + wide)
        start = (shift - wide) % cy
        on_right = (lane >= start) & (lane < start + wide)
        values = bulk[f] if f < BULK else edge[f - BULK]
        for x in range(cx):
            turned = pltpu.roll(values[x], shift, 1) if shift else values[x]
            to_left[x] = jnp.where(on_left, turned, to_left[x])
            to_right[x] = jnp.where(on_right, turned, to_right[x])
    even = lax.rem(at_y, 2) == 0
    for x in range(cx):
        ya_out[x] = jnp.where(even, to_right[x], to_left[x])
        yb_out[x] = jnp.where(even, to_left[x], to_right[x])


def main_kernel(count_x, count_y, offsets, *refs):
    width = len(offsets)
    (wells_ref, diag_ref, off_ref, dinv_ref), refs = refs[:4], refs[4:]
    blocks, refs = refs[:width], refs[width:]
    ya_refs, refs = refs[:width], refs[width:]
    yb_refs, refs = refs[:width], refs[width:]
    residual_out, z_out, sums_out = refs

    cx, nz, cy = residual_out.shape[1:]
    total = width * cx
    at_x = lax.axis_index("gx")
    at_y = lax.axis_index("gy")
    even = lax.rem(at_y, 2) == 0
    has_left = jnp.where(at_y > 0, 1.0, 0.0).astype(f32)
    has_right = jnp.where(at_y < count_y - 1, 1.0, 0.0).astype(f32)
    layers = 1 if count_x == 2 else 2
    last = BULK * cx + layers * EDGE
    index_x = [lax.rem(at_x + (o % count_x), count_x) for o in offsets]
    joined = [
        jnp.where(index_x[(j + 1) % width] == index_x[j] + 1, 1.0, 0.0).astype(f32)
        for j in range(width)
    ]

    from_left, from_right = [], []
    for j in range(width):
        first, second = ya_refs[j][...], yb_refs[j][...]
        from_right.append(jnp.where(even, first, second) * has_right)
        from_left.append(jnp.where(even, second, first) * has_left)
    lane = iota((nz, cy), 1)

    def halo(tiles_l, tiles_r, x, shift, wide):
        back = (cy - shift) % cy
        left, right = tiles_l[x], tiles_r[x]
        if back:
            left, right = pltpu.roll(left, back, 1), pltpu.roll(right, back, 1)
        return jnp.where(lane < wide, right, jnp.where(lane >= cy - wide, left, 0.0))

    def extended(f):
        own = jnp.concatenate([blocks[j][f * cx : (f + 1) * cx] for j in range(width)], axis=0)
        side = jnp.stack(
            [
                halo(from_left[j], from_right[j], x, f * WIDE, WIDE)
                for j in range(width)
                for x in range(cx)
            ]
        )
        return jnp.concatenate([own, side], axis=2)

    lanes = 2 * cy
    level = iota((total, nz, lanes), 1)

    def next_x(v):
        return jnp.concatenate([v[1:], v[:1]], axis=0)

    def last_x(v):
        return jnp.concatenate([v[-1:], v[:-1]], axis=0)

    def next_y(v):
        return pltpu.roll(v, v.shape[2] - 1, 2)

    def last_y(v):
        return pltpu.roll(v, 1, 2)

    def next_z(v):
        return pltpu.roll(v, nz - 1, 1)

    def last_z(v):
        return pltpu.roll(v, 1, 1)

    def seam_after(v):
        rows = [v[i] for i in range(total)]
        for j in range(width):
            rows[j * cx + cx - 1] = rows[j * cx + cx - 1] * joined[j]
        return jnp.stack(rows)

    def seam_before(v):
        rows = [v[i] for i in range(total)]
        for j in range(width):
            at = ((j + 1) % width) * cx
            rows[at] = rows[at] * joined[j]
        return jnp.stack(rows)

    press = extended(PRESS)
    mobile = [extended(MOB + c) for c in range(3)]
    perm = extended(PERM)
    resid = [extended(ACC + c) for c in range(3)]

    for forward, backward, kind in ((next_x, last_x, 0), (next_y, last_y, 1), (next_z, last_z, 2)):
        beyond = forward(perm)
        bottom = perm + beyond
        conduct = 2.0 * perm * beyond / jnp.where(bottom > 0.0, bottom, 1.0)
        if kind == 0:
            conduct = seam_after(conduct)
        if kind == 2:
            conduct = jnp.where(level < nz - 1, vertical_ratio * conduct, 0.0)
        drop = press - forward(press)
        flow = conduct * drop
        for c in range(3):
            passing = flow * jnp.where(drop >= 0.0, mobile[c], forward(mobile[c]))
            resid[c] = resid[c] + passing - backward(passing)

    wells = wells_ref.shape[2]
    perfs = blocks[0].shape[2]
    added = [[] for _ in range(3)]
    for j in range(width):
        pair = jnp.sum(wells_ref[pl.ds(index_x[j] * count_y, count_y)], axis=0)
        hole = pair[1:2] / pair[0:1]
        tiles = jnp.concatenate(
            [blocks[j][last], from_left[j][cx], from_right[j][cx]], axis=1
        )
        spot_xz, spot_y, well = tiles[0:1], tiles[1:2], tiles[2:3]
        member = jnp.where(iota((wells, 3 * perfs), 0).astype(f32) == well, 1.0, 0.0)
        hole_at = lax.dot_general(
            jnp.broadcast_to(hole, (8, wells)),
            member,
            NN,
            precision=highest,
            preferred_element_type=f32,
        )[0:1]
        fall = tiles[6:7] - hole_at
        on_xz = iota((cx * nz, 3 * perfs), 0).astype(f32) == spot_xz
        spread = jnp.concatenate(
            [jnp.where(on_xz, tiles[3 + c : 4 + c] * fall, 0.0) for c in range(3)], axis=0
        )
        hot_y = iota((cy, 3 * perfs), 0).astype(f32) == spot_y
        nearby = iota((cy, 3 * perfs), 0)
        source = iota((cy, 3 * perfs), 1)
        kept = jnp.where(
            source < 2 * perfs, jnp.where(nearby >= cy - WIDE, 1, 0), jnp.where(nearby < WIDE, 1, 0)
        )
        hot_side = hot_of(hot_y & (kept == 1))
        inner = split_dot(spread[:, :perfs], hot_of(hot_y[:, :perfs]), NT)
        outer = split_dot(spread[:, perfs:], hot_side[:, perfs:], NT)
        both = jnp.concatenate([inner, outer], axis=1).reshape(3, cx, nz, lanes)
        for c in range(3):
            added[c].append(both[c])
    start = [-(resid[c] + jnp.concatenate(added[c], axis=0)) for c in range(3)]
    for c in range(3):
        residual_out[c] = -start[c][:cx, :, :cy]

    coefs = [extended(COEF + q) for q in range(6)]
    coefs[0] = seam_before(coefs[0])
    coefs[1] = seam_after(coefs[1])
    scaled = (start[0] + start[1] + start[2]) * extended(INV)
    steps = (last_x, next_x, last_y, next_y, last_z, next_z)
    part = scaled
    for _ in range(1, SWEEPS):
        gathered = coefs[0] * steps[0](part)
        for q in range(1, 6):
            gathered = gathered + coefs[q] * steps[q](part)
        part = scaled - gathered

    near = [step(part) for step in steps]
    near[0] = seam_before(near[0])
    near[1] = seam_after(near[1])
    near[4] = jnp.where(level > 0, near[4], 0.0)
    near[5] = jnp.where(level < nz - 1, near[5], 0.0)

    def direction(edge_of, where):
        here = where(part)
        rest = []
        for c in range(3):
            coupled = edge_of(DCOL + c) * here
            for q in range(6):
                coupled = coupled + edge_of(OFFC + 3 * q + c) * where(near[q])
            rest.append(where(start[c]) - coupled)
        solved = []
        for a in range(3):
            value = edge_of(DINV + 3 * a) * rest[0]
            value = value + edge_of(DINV + 3 * a + 1) * rest[1]
            solved.append(value + edge_of(DINV + 3 * a + 2) * rest[2])
        solved[0] = solved[0] + here
        return solved

    def edge_own(e):
        if e < DCOL:
            return dinv_ref[e]
        if e < OFFC:
            return diag_ref[e - DCOL, 0]
        return off_ref[(e - OFFC) // 3, (e - OFFC) % 3, 0]

    def edge_side(e):
        return jnp.stack(
            [halo(from_left[0], from_right[0], x, EDGE_AT + e, 1) for x in range(cx)]
        )

    base = BULK * cx
    after, before = 1 % width, width - 1
    z_own = direction(edge_own, lambda v: v[:cx, :, :cy])
    z_side = direction(edge_side, lambda v: v[:cx, :, cy:])
    z_next = direction(
        lambda e: blocks[after][base + e], lambda v: v[after * cx, :, :cy]
    )
    z_last = direction(
        lambda e: blocks[before][base + (layers - 1) * EDGE + e],
        lambda v: v[before * cx + cx - 1, :, :cy],
    )
    level_own = iota((cx, nz, cy), 1)
    around = []
    for k in range(3):
        z_out[k] = z_own[k]
        ext = jnp.concatenate([z_own[k], z_side[k]], axis=2)
        around.append(
            [
                jnp.concatenate([(z_last[k] * joined[width - 1])[None], z_own[k][:-1]], axis=0),
                jnp.concatenate([z_own[k][1:], (z_next[k] * joined[0])[None]], axis=0),
                last_y(ext)[:, :, :cy],
                next_y(ext)[:, :, :cy],
                jnp.where(level_own > 0, last_z(z_own[k]), 0.0),
                jnp.where(level_own < nz - 1, next_z(z_own[k]), 0.0),
            ]
        )
    along = jnp.zeros((nz, cy), f32)
    square = jnp.zeros((nz, cy), f32)
    for c in range(3):
        mapped = diag_ref[c, 0] * z_own[0]
        for k in range(1, 3):
            mapped = mapped + diag_ref[c, k] * z_own[k]
        for q in range(6):
            for k in range(3):
                mapped = mapped + off_ref[q, c, k] * around[k][q]
        along = along + jnp.sum(mapped * start[c][:cx, :, :cy], axis=0)
        square = square + jnp.sum(mapped * mapped, axis=0)
    along = jnp.sum(along, axis=0, keepdims=True)
    square = jnp.sum(square, axis=0, keepdims=True)
    pair = jnp.where(iota((2, cy), 0) == 0, along, square)
    sums_out[...] = jnp.broadcast_to(pair[None], sums_out.shape)


def after_kernel(sums_ref, z_ref, update_out):
    pair = jnp.sum(sums_ref[...], axis=0)
    both = jnp.sum(pair, axis=1, keepdims=True)
    step = both[0:1] / both[1:2]
    update_out[...] = z_ref[...] * step[None, None]


def body(
    pressure,
    saturation,
    saturation_old,
    pore_volume,
    permeability,
    jac_diag,
    jac_off,
    perf_cell,
    perf_well,
    perf_index,
    well_rate,
):
    count_x, count_y = lax.axis_size("gx"), lax.axis_size("gy")
    devices = count_x * count_y
    cx, nz, cy = pressure.shape
    wells = well_rate.shape[1] * count_y
    layers = 1 if count_x == 2 else 2
    tiles = BULK * cx + layers * EDGE + 1
    offsets = window(count_x, cx)
    width = len(offsets)
    shape = jax.ShapeDtypeStruct
    whole = pl.BlockSpec(memory_space=pltpu.VMEM)
    params = pltpu.CompilerParams(vmem_limit_bytes=40 * 1024 * 1024)

    wells_part, block, ya, yb, dinv = pl.pallas_call(
        functools.partial(before_kernel, count_x, count_y),
        grid=(1,),
        in_specs=[
            *[whole] * 6,
            pl.BlockSpec((6, 3, 1, cx, nz, cy), lambda i: (0, 0, 0, 0, 0, 0)),
            *[whole] * 4,
        ],
        out_specs=[whole] * 5,
        out_shape=[
            shape((devices, 2, wells), f32),
            shape((tiles, nz, cy), f32),
            shape((cx + 1, nz, cy), f32),
            shape((cx + 1, nz, cy), f32),
            shape((9, cx, nz, cy), f32),
        ],
        compiler_params=params,
        name="before",
    )(
        pressure,
        saturation,
        saturation_old,
        pore_volume,
        permeability,
        jac_diag,
        jac_off,
        perf_cell,
        perf_well,
        perf_index,
        well_rate,
    )

    pairs = [(i, i ^ 1) for i in range(count_y)]
    others = [(i, (i + 1) % count_y if i % 2 else (i - 1) % count_y) for i in range(count_y)]

    def from_x(values, offset):
        return lax.ppermute(
            values, "gx", [((i + offset) % count_x, i) for i in range(count_x)]
        )

    ya_got = lax.ppermute(ya, "gy", pairs)
    yb_got = lax.ppermute(yb, "gy", others)
    blocks = [block] + [from_x(block, o) for o in offsets[1:]]
    wells_all = lax.all_to_all(wells_part, ("gx", "gy"), 0, 0)
    forward = jnp.stack([ya_got, yb_got])
    passed = [from_x(forward, o) for o in offsets[1:]]
    ya_all = [ya_got] + [p[0] for p in passed]
    yb_all = [yb_got] + [p[1] for p in passed]

    residual, direction, sums = pl.pallas_call(
        functools.partial(main_kernel, count_x, count_y, tuple(offsets)),
        in_specs=[whole] * (4 + 3 * width),
        out_specs=[whole] * 3,
        out_shape=[
            shape((3, cx, nz, cy), f32),
            shape((3, cx, nz, cy), f32),
            shape((devices, 2, cy), f32),
        ],
        compiler_params=params,
        name="main",
    )(wells_all, jac_diag, jac_off, dinv, *blocks, *ya_all, *yb_all)

    sums_all = lax.all_to_all(sums, ("gx", "gy"), 0, 0)
    update = pl.pallas_call(
        after_kernel,
        in_specs=[whole] * 2,
        out_specs=whole,
        out_shape=shape((3, cx, nz, cy), f32),
        compiler_params=params,
        name="after",
    )(sums_all, direction)
    return (residual, update)


def solution(mesh):
    placed = (
        P("gx", None, "gy"),
        P(None, "gx", None, "gy"),
        P(None, "gx", None, "gy"),
        P("gx", None, "gy"),
        P("gx", None, "gy"),
        P(None, None, "gx", None, "gy"),
        P(None, None, None, "gx", None, "gy"),
        P("gx", "gy"),
        P("gx", "gy"),
        P("gx", "gy"),
        P("gx", "gy"),
    )
    return jax.shard_map(
        body,
        mesh=mesh,
        in_specs=placed,
        out_specs=(P(None, "gx", None, "gy"), P(None, "gx", None, "gy")),
        check_vma=False,
    )
```

```python
import functools

import jax
import jax.numpy as jnp
from jax import lax
from jax.experimental import pallas as pl
from jax.experimental.pallas import tpu as pltpu
from jax.sharding import PartitionSpec as P

SWEEPS = 4
WIDE = SWEEPS + 2

viscosity = (1.0, 2.0, 0.2)
vertical_ratio = 0.1
highest = lax.Precision.HIGHEST
f32 = jnp.float32

PRESS, MOB, PERM, ACC, INV, COEF = 0, 1, 4, 5, 8, 9
BULK = 15
DINV, DCOL, OFFC = 0, 9, 12
EDGE = 30
EDGE_AT = BULK * WIDE
NT = (((1,), (1,)), ((), ()))
NN = (((1,), (0,)), ((), ()))


def iota(shape, axis):
    return lax.broadcasted_iota(jnp.int32, shape, axis)


def split_dot(values, hot, dims):
    rows = values.shape[0]
    high = values.astype(jnp.bfloat16)
    rest = values - high.astype(f32)
    mid = rest.astype(jnp.bfloat16)
    low = (rest - mid.astype(f32)).astype(jnp.bfloat16)
    parts = jnp.concatenate([high, mid, low], axis=0)
    out = lax.dot_general(parts, hot, dims, preferred_element_type=f32)
    return out[:rows] + (out[rows : 2 * rows] + out[2 * rows :])


def hot_of(condition):
    return jnp.where(condition, 1.0, 0.0).astype(jnp.bfloat16)


def window(count, cx):
    reach = -(-WIDE // cx)
    if count <= 2 * reach + 1:
        return list(range(count))
    return list(range(reach + 1)) + list(range(-reach, 0))


def before_kernel(
    count_x,
    count_y,
    *refs,
):
    sources, (wells_out, block_out, ya_out, yb_out, dinv_out) = refs[:11], refs[11:16]
    diag_ref, off_ref = refs[16:18]
    press_ref, sat_ref, old_ref, pore_ref, perm_ref = refs[18:23]
    cell_ref, well_ref, index_ref, rate_ref, sems = refs[23:]
    targets = (*refs[18:23], diag_ref, off_ref, *refs[23:27])
    copies = []
    for i in (7, 8, 9, 10, 0, 1, 4, 2, 3, 5, 6):
        copies.append(pltpu.make_async_copy(sources[i], targets[i], sems.at[i]))
        copies[-1].start()
    for copy in copies[:6]:
        copy.wait()
    cx, nz, cy = press_ref.shape
    at_x = lax.axis_index("gx")
    at_y = lax.axis_index("gy")
    layers = 1 if count_x == 2 else 2
    last = block_out.shape[0] - 1

    press = press_ref[...]
    water, gas = sat_ref[0], sat_ref[1]
    oil = 1.0 - water - gas
    mobile = [
        water * water / viscosity[0],
        oil * oil / viscosity[1],
        gas * gas / viscosity[2],
    ]

    cells = cell_ref[...]
    perfs = cells.shape[1]
    spot_xz = lax.div(cells, cy)
    spot_y = lax.rem(cells, cy)
    stacked = jnp.concatenate([m.reshape(cx * nz, cy) for m in mobile + [press]], axis=0)
    hot_y = hot_of(iota((cy, perfs), 0) == spot_y)
    picked = split_dot(stacked, hot_y, NN).reshape(4, cx * nz, perfs)
    on_xz = iota((cx * nz, perfs), 0) == spot_xz
    at_perf = [
        jnp.sum(jnp.where(on_xz, picked[i], 0.0), axis=0, keepdims=True) for i in range(4)
    ]
    index_vals = index_ref[...]
    parts = [index_vals * at_perf[i] for i in range(3)]
    strength = index_vals * (at_perf[0] + at_perf[1] + at_perf[2])
    weighted = strength * at_perf[3]
    row = iota((8, perfs), 0)
    both = jnp.where(row == 0, strength, jnp.where(row == 1, weighted, 0.0))
    wells = wells_out.shape[2]
    member = jnp.where(iota((wells, perfs), 0) == well_ref[...], 1.0, 0.0)
    sums = lax.dot_general(both, member, NT, precision=highest, preferred_element_type=f32)
    owned = rate_ref.shape[1]
    square = jnp.broadcast_to(rate_ref[...], (owned, owned))
    column = jnp.sum(
        jnp.where(iota((owned, owned), 0) == iota((owned, owned), 1), square, 0.0),
        axis=1,
        keepdims=True,
    )
    mine = iota((owned, wells), 1) == at_y * owned + iota((owned, wells), 0)
    rates = jnp.sum(jnp.where(mine, column, 0.0), axis=0, keepdims=True)
    pair = sums[:2] - jnp.where(iota((2, wells), 0) == 1, rates, 0.0)
    wells_out[...] = jnp.broadcast_to(pair[None], wells_out.shape)

    perf_rows = [
        spot_xz.astype(f32),
        spot_y.astype(f32),
        well_ref[...].astype(f32),
        *parts,
        at_perf[3],
        jnp.zeros_like(at_perf[3]),
    ]
    for r, values in enumerate(perf_rows):
        block_out[last, r : r + 1, :] = values
        ya_out[cx, r : r + 1, :] = values
        yb_out[cx, r : r + 1, :] = values

    for copy in copies[6:]:
        copy.wait()
    old_water, old_gas = old_ref[0], old_ref[1]
    old_oil = 1.0 - old_water - old_gas
    pore = pore_ref[...]
    accumulated = [pore * (water - old_water), pore * (oil - old_oil), pore * (gas - old_gas)]
    layer_at = iota((cx, nz, cy), 1)
    columns = [[off_ref[q, c, 0] for c in range(3)] for q in range(6)]
    columns[4] = [jnp.where(layer_at > 0, v, 0.0) for v in columns[4]]
    columns[5] = [jnp.where(layer_at < nz - 1, v, 0.0) for v in columns[5]]
    diag = [[diag_ref[a, b] for b in range(3)] for a in range(3)]
    inverse = 1.0 / (diag[0][0] + diag[1][0] + diag[2][0])
    coefs = [(columns[q][0] + columns[q][1] + columns[q][2]) * inverse for q in range(6)]
    bulk = [press, *mobile, perm_ref[...], *accumulated, inverse, *coefs]

    def cofactor(a, b):
        return (
            diag[(a + 1) % 3][(b + 1) % 3] * diag[(a + 2) % 3][(b + 2) % 3]
            - diag[(a + 1) % 3][(b + 2) % 3] * diag[(a + 2) % 3][(b + 1) % 3]
        )

    cofactors = [[cofactor(a, b) for b in range(3)] for a in range(3)]
    over = 1.0 / (
        diag[0][0] * cofactors[0][0] + diag[0][1] * cofactors[0][1] + diag[0][2] * cofactors[0][2]
    )
    solve = [cofactors[b][a] * over for a in range(3) for b in range(3)]
    for i in range(9):
        dinv_out[i] = solve[i]
    edge = solve + [diag[c][0] for c in range(3)] + [columns[q][c] for q in range(6) for c in range(3)]

    for f in range(BULK):
        block_out[f * cx : (f + 1) * cx] = bulk[f]
    base = BULK * cx
    for e in range(EDGE):
        if layers == 1:
            block_out[base + e] = jnp.where(at_x == 0, edge[e][cx - 1], edge[e][0])
        else:
            block_out[base + e] = edge[e][0]
            block_out[base + EDGE + e] = edge[e][cx - 1]

    lane = iota((nz, cy), 1)
    to_left = [jnp.zeros((nz, cy), f32) for _ in range(cx)]
    to_right = [jnp.zeros((nz, cy), f32) for _ in range(cx)]
    for f in range(BULK + EDGE):
        wide = WIDE if f < BULK else 1
        shift = f * WIDE if f < BULK else EDGE_AT + f - BULK
        on_left = (lane >= shift) & (lane < shift + wide)
        start = (shift - wide) % cy
        on_right = (lane >= start) & (lane < start + wide)
        values = bulk[f] if f < BULK else edge[f - BULK]
        for x in range(cx):
            turned = pltpu.roll(values[x], shift, 1) if shift else values[x]
            to_left[x] = jnp.where(on_left, turned, to_left[x])
            to_right[x] = jnp.where(on_right, turned, to_right[x])
    for spare in range(cx + 1, 2 * cx):
        ya_out[spare] = jnp.zeros((nz, cy), f32)
        yb_out[spare] = jnp.zeros((nz, cy), f32)
    even = lax.rem(at_y, 2) == 0
    for x in range(cx):
        ya_out[x] = jnp.where(even, to_right[x], to_left[x])
        yb_out[x] = jnp.where(even, to_left[x], to_right[x])


def main_kernel(count_x, count_y, offsets, *refs):
    width = len(offsets)
    (wells_ref, diag_ref, off_ref, dinv_ref), refs = refs[:4], refs[4:]
    blocks, refs = refs[:width], refs[width:]
    ya_refs, refs = refs[:width], refs[width:]
    yb_refs, refs = refs[:width], refs[width:]
    residual_out, z_out, sums_out = refs

    cx, nz, cy = residual_out.shape[1:]
    total = width * cx
    at_x = lax.axis_index("gx")
    at_y = lax.axis_index("gy")
    even = lax.rem(at_y, 2) == 0
    has_left = jnp.where(at_y > 0, 1.0, 0.0).astype(f32)
    has_right = jnp.where(at_y < count_y - 1, 1.0, 0.0).astype(f32)
    layers = 1 if count_x == 2 else 2
    last = BULK * cx + layers * EDGE
    index_x = [lax.rem(at_x + (o % count_x), count_x) for o in offsets]
    joined = [
        jnp.where(index_x[(j + 1) % width] == index_x[j] + 1, 1.0, 0.0).astype(f32)
        for j in range(width)
    ]

    from_left, from_right = [], []
    for j in range(width):
        first, second = ya_refs[j][...], yb_refs[j][...]
        from_right.append(jnp.where(even, first, second) * has_right)
        from_left.append(jnp.where(even, second, first) * has_left)
    lane = iota((nz, cy), 1)

    def halo(tiles_l, tiles_r, x, shift, wide):
        back = (cy - shift) % cy
        left, right = tiles_l[x], tiles_r[x]
        if back:
            left, right = pltpu.roll(left, back, 1), pltpu.roll(right, back, 1)
        return jnp.where(lane < wide, right, jnp.where(lane >= cy - wide, left, 0.0))

    def extended(f):
        own = jnp.concatenate([blocks[j][f * cx : (f + 1) * cx] for j in range(width)], axis=0)
        side = jnp.stack(
            [
                halo(from_left[j], from_right[j], x, f * WIDE, WIDE)
                for j in range(width)
                for x in range(cx)
            ]
        )
        return jnp.concatenate([own, side], axis=2)

    lanes = 2 * cy
    level = iota((total, nz, lanes), 1)

    def next_x(v):
        return jnp.concatenate([v[1:], v[:1]], axis=0)

    def last_x(v):
        return jnp.concatenate([v[-1:], v[:-1]], axis=0)

    def next_y(v):
        return pltpu.roll(v, v.shape[2] - 1, 2)

    def last_y(v):
        return pltpu.roll(v, 1, 2)

    def next_z(v):
        return pltpu.roll(v, nz - 1, 1)

    def last_z(v):
        return pltpu.roll(v, 1, 1)

    def seam_after(v):
        rows = [v[i] for i in range(total)]
        for j in range(width):
            rows[j * cx + cx - 1] = rows[j * cx + cx - 1] * joined[j]
        return jnp.stack(rows)

    def seam_before(v):
        rows = [v[i] for i in range(total)]
        for j in range(width):
            at = ((j + 1) % width) * cx
            rows[at] = rows[at] * joined[j]
        return jnp.stack(rows)

    press = extended(PRESS)
    mobile = [extended(MOB + c) for c in range(3)]
    perm = extended(PERM)
    resid = [extended(ACC + c) for c in range(3)]

    for forward, backward, kind in ((next_x, last_x, 0), (next_y, last_y, 1), (next_z, last_z, 2)):
        beyond = forward(perm)
        bottom = perm + beyond
        conduct = 2.0 * perm * beyond / jnp.where(bottom > 0.0, bottom, 1.0)
        if kind == 0:
            conduct = seam_after(conduct)
        if kind == 2:
            conduct = jnp.where(level < nz - 1, vertical_ratio * conduct, 0.0)
        drop = press - forward(press)
        flow = conduct * drop
        for c in range(3):
            passing = flow * jnp.where(drop >= 0.0, mobile[c], forward(mobile[c]))
            resid[c] = resid[c] + passing - backward(passing)

    wells = wells_ref.shape[2]
    perfs = blocks[0].shape[2]
    added = [[] for _ in range(3)]
    for j in range(width):
        pair = jnp.sum(wells_ref[pl.ds(index_x[j] * count_y, count_y)], axis=0)
        hole = pair[1:2] / pair[0:1]
        tiles = jnp.concatenate(
            [blocks[j][last], from_left[j][cx], from_right[j][cx]], axis=1
        )
        spot_xz, spot_y, well = tiles[0:1], tiles[1:2], tiles[2:3]
        member = jnp.where(iota((wells, 3 * perfs), 0).astype(f32) == well, 1.0, 0.0)
        hole_at = lax.dot_general(
            jnp.broadcast_to(hole, (8, wells)),
            member,
            NN,
            precision=highest,
            preferred_element_type=f32,
        )[0:1]
        fall = tiles[6:7] - hole_at
        on_xz = iota((cx * nz, 3 * perfs), 0).astype(f32) == spot_xz
        spread = jnp.concatenate(
            [jnp.where(on_xz, tiles[3 + c : 4 + c] * fall, 0.0) for c in range(3)], axis=0
        )
        hot_y = iota((cy, 3 * perfs), 0).astype(f32) == spot_y
        nearby = iota((cy, 3 * perfs), 0)
        source = iota((cy, 3 * perfs), 1)
        kept = jnp.where(
            source < 2 * perfs, jnp.where(nearby >= cy - WIDE, 1, 0), jnp.where(nearby < WIDE, 1, 0)
        )
        hot_side = hot_of(hot_y & (kept == 1))
        inner = split_dot(spread[:, :perfs], hot_of(hot_y[:, :perfs]), NT)
        outer = split_dot(spread[:, perfs:], hot_side[:, perfs:], NT)
        both = jnp.concatenate([inner, outer], axis=1).reshape(3, cx, nz, lanes)
        for c in range(3):
            added[c].append(both[c])
    start = [-(resid[c] + jnp.concatenate(added[c], axis=0)) for c in range(3)]
    for c in range(3):
        residual_out[c] = -start[c][:cx, :, :cy]

    coefs = [extended(COEF + q) for q in range(6)]
    coefs[0] = seam_before(coefs[0])
    coefs[1] = seam_after(coefs[1])
    scaled = (start[0] + start[1] + start[2]) * extended(INV)
    steps = (last_x, next_x, last_y, next_y, last_z, next_z)
    part = scaled
    for _ in range(1, SWEEPS):
        gathered = coefs[0] * steps[0](part)
        for q in range(1, 6):
            gathered = gathered + coefs[q] * steps[q](part)
        part = scaled - gathered

    near = [step(part) for step in steps]
    near[0] = seam_before(near[0])
    near[1] = seam_after(near[1])
    near[4] = jnp.where(level > 0, near[4], 0.0)
    near[5] = jnp.where(level < nz - 1, near[5], 0.0)

    def direction(edge_of, where):
        here = where(part)
        rest = []
        for c in range(3):
            coupled = edge_of(DCOL + c) * here
            for q in range(6):
                coupled = coupled + edge_of(OFFC + 3 * q + c) * where(near[q])
            rest.append(where(start[c]) - coupled)
        solved = []
        for a in range(3):
            value = edge_of(DINV + 3 * a) * rest[0]
            value = value + edge_of(DINV + 3 * a + 1) * rest[1]
            solved.append(value + edge_of(DINV + 3 * a + 2) * rest[2])
        solved[0] = solved[0] + here
        return solved

    def edge_own(e):
        if e < DCOL:
            return dinv_ref[e]
        if e < OFFC:
            return diag_ref[e - DCOL, 0]
        return off_ref[(e - OFFC) // 3, (e - OFFC) % 3, 0]

    def edge_side(e):
        return jnp.stack(
            [halo(from_left[0], from_right[0], x, EDGE_AT + e, 1) for x in range(cx)]
        )

    base = BULK * cx
    after, before = 1 % width, width - 1
    z_own = direction(edge_own, lambda v: v[:cx, :, :cy])
    z_side = direction(edge_side, lambda v: v[:cx, :, cy:])
    z_next = direction(
        lambda e: blocks[after][base + e], lambda v: v[after * cx, :, :cy]
    )
    z_last = direction(
        lambda e: blocks[before][base + (layers - 1) * EDGE + e],
        lambda v: v[before * cx + cx - 1, :, :cy],
    )
    level_own = iota((cx, nz, cy), 1)
    around = []
    for k in range(3):
        z_out[k] = z_own[k]
        ext = jnp.concatenate([z_own[k], z_side[k]], axis=2)
        around.append(
            [
                jnp.concatenate([(z_last[k] * joined[width - 1])[None], z_own[k][:-1]], axis=0),
                jnp.concatenate([z_own[k][1:], (z_next[k] * joined[0])[None]], axis=0),
                last_y(ext)[:, :, :cy],
                next_y(ext)[:, :, :cy],
                jnp.where(level_own > 0, last_z(z_own[k]), 0.0),
                jnp.where(level_own < nz - 1, next_z(z_own[k]), 0.0),
            ]
        )
    along = jnp.zeros((nz, cy), f32)
    square = jnp.zeros((nz, cy), f32)
    for c in range(3):
        mapped = diag_ref[c, 0] * z_own[0]
        for k in range(1, 3):
            mapped = mapped + diag_ref[c, k] * z_own[k]
        for q in range(6):
            for k in range(3):
                mapped = mapped + off_ref[q, c, k] * around[k][q]
        along = along + jnp.sum(mapped * start[c][:cx, :, :cy], axis=0)
        square = square + jnp.sum(mapped * mapped, axis=0)
    along = jnp.sum(along, axis=0, keepdims=True)
    square = jnp.sum(square, axis=0, keepdims=True)
    pair = jnp.where(iota((2, cy), 0) == 0, along, square)
    sums_out[...] = jnp.broadcast_to(pair[None], sums_out.shape)


def after_kernel(sums_ref, z_ref, update_out):
    pair = jnp.sum(sums_ref[...], axis=0)
    both = jnp.sum(pair, axis=1, keepdims=True)
    step = both[0:1] / both[1:2]
    update_out[...] = z_ref[...] * step[None, None]


def body(
    pressure,
    saturation,
    saturation_old,
    pore_volume,
    permeability,
    jac_diag,
    jac_off,
    perf_cell,
    perf_well,
    perf_index,
    well_rate,
):
    count_x, count_y = lax.axis_size("gx"), lax.axis_size("gy")
    devices = count_x * count_y
    cx, nz, cy = pressure.shape
    wells = well_rate.shape[1] * count_y
    layers = 1 if count_x == 2 else 2
    tiles = BULK * cx + layers * EDGE + 1
    offsets = window(count_x, cx)
    width = len(offsets)
    shape = jax.ShapeDtypeStruct
    whole = pl.BlockSpec(memory_space=pltpu.VMEM)
    anywhere = pl.BlockSpec(memory_space=pltpu.HBM)
    params = pltpu.CompilerParams(vmem_limit_bytes=32 * 1024 * 1024)

    fields = (pressure, saturation, saturation_old, pore_volume, permeability, jac_diag)
    perforations = (perf_cell, perf_well, perf_index, well_rate)
    wells_part, block, ya, yb, dinv, diag, off = pl.pallas_call(
        functools.partial(before_kernel, count_x, count_y),
        in_specs=[anywhere] * 11,
        out_specs=[whole] * 7,
        out_shape=[
            shape((devices, 2, wells), f32),
            shape((tiles, nz, cy), f32),
            shape((2 * cx, nz, cy), f32),
            shape((2 * cx, nz, cy), f32),
            shape((9, cx, nz, cy), f32),
            shape(jac_diag.shape, f32),
            shape(jac_off.shape, f32),
        ],
        scratch_shapes=[
            *[pltpu.VMEM(v.shape, v.dtype) for v in fields[:5]],
            *[pltpu.VMEM(v.shape, v.dtype) for v in perforations],
            pltpu.SemaphoreType.DMA((11,)),
        ],
        compiler_params=params,
        name="before",
    )(*[pltpu.with_memory_space_constraint(v, pltpu.HBM) for v in (*fields, jac_off, *perforations)])

    pairs = [(i, i ^ 1) for i in range(count_y)]
    others = [(i, min(i + 1, count_y - 1) if i % 2 else max(i - 1, 0)) for i in range(count_y)]

    def from_x(values, offset):
        return lax.ppermute(
            values, "gx", [((i + offset) % count_x, i) for i in range(count_x)]
        )

    ya_got = lax.ppermute(ya, "gy", pairs)
    yb_got = lax.ppermute(yb, "gy", others)
    blocks = [block] + [from_x(block, o) for o in offsets[1:]]
    wells_all = lax.all_to_all(wells_part, ("gx", "gy"), 0, 0)
    ya_all = [ya_got] + [from_x(ya_got, o) for o in offsets[1:]]
    yb_all = [yb_got] + [from_x(yb_got, o) for o in offsets[1:]]

    residual, direction, sums = pl.pallas_call(
        functools.partial(main_kernel, count_x, count_y, tuple(offsets)),
        in_specs=[whole] * (4 + 3 * width),
        out_specs=[whole] * 3,
        out_shape=[
            shape((3, cx, nz, cy), f32),
            shape((3, cx, nz, cy), f32),
            shape((devices, 2, cy), f32),
        ],
        compiler_params=params,
        name="main",
    )(wells_all, diag, off, dinv, *blocks, *ya_all, *yb_all)

    sums_all = lax.all_to_all(sums, ("gx", "gy"), 0, 0)
    update = pl.pallas_call(
        after_kernel,
        in_specs=[whole] * 2,
        out_specs=whole,
        out_shape=shape((3, cx, nz, cy), f32),
        compiler_params=params,
        name="after",
    )(sums_all, direction)
    return (residual, update)


def solution(mesh):
    placed = (
        P("gx", None, "gy"),
        P(None, "gx", None, "gy"),
        P(None, "gx", None, "gy"),
        P("gx", None, "gy"),
        P("gx", None, "gy"),
        P(None, None, "gx", None, "gy"),
        P(None, None, None, "gx", None, "gy"),
        P("gx", "gy"),
        P("gx", "gy"),
        P("gx", "gy"),
        P("gx", "gy"),
    )
    return jax.shard_map(
        body,
        mesh=mesh,
        in_specs=placed,
        out_specs=(P(None, "gx", None, "gy"), P(None, "gx", None, "gy")),
        check_vma=False,
    )
```

```python
import functools

import jax
import jax.numpy as jnp
from jax import lax
from jax.experimental import pallas as pl
from jax.experimental.pallas import tpu as pltpu
from jax.sharding import PartitionSpec as P

SWEEPS = 4
WIDE = SWEEPS + 2

viscosity = (1.0, 2.0, 0.2)
vertical_ratio = 0.1
highest = lax.Precision.HIGHEST
f32 = jnp.float32

PRESS, MOB, PERM, ACC, INV, COEF = 0, 1, 4, 5, 8, 9
BULK = 15
DINV, DCOL, OFFC, EACC = 0, 9, 12, 30
EDGE = 33
EDGE_AT = BULK * WIDE
WATER, GAS, SENT = 2, 3, 4
SUM, INNER = 7, 8
NT = (((1,), (1,)), ((), ()))
NN = (((1,), (0,)), ((), ()))


def iota(shape, axis):
    return lax.broadcasted_iota(jnp.int32, shape, axis)


def split_dot(values, hot, dims):
    rows = values.shape[0]
    high = values.astype(jnp.bfloat16)
    rest = values - high.astype(f32)
    mid = rest.astype(jnp.bfloat16)
    low = (rest - mid.astype(f32)).astype(jnp.bfloat16)
    parts = jnp.concatenate([high, mid, low], axis=0)
    out = lax.dot_general(parts, hot, dims, preferred_element_type=f32)
    return out[:rows] + (out[rows : 2 * rows] + out[2 * rows :])


def hot_of(condition):
    return jnp.where(condition, 1.0, 0.0).astype(jnp.bfloat16)


def sent_tiles(cx, layers):
    inner = SENT * cx
    edges = inner + INNER * (cx - layers)
    return inner, edges, edges + EDGE * layers, edges + EDGE * layers + 1


def window(count, cx):
    reach = -(-WIDE // cx)
    if count <= 2 * reach + 1:
        return list(range(count))
    return list(range(reach + 1)) + list(range(-reach, 0))


def before_kernel(
    count_x,
    count_y,
    *refs,
):
    sources, (wells_hbm, block_out, own_out, ya_out, yb_out, dinv_out) = refs[:11], refs[11:17]
    diag_ref, off_ref = refs[17:19]
    press_ref, sat_ref, old_ref, pore_ref, perm_ref = refs[19:24]
    cell_ref, well_ref, index_ref, rate_ref, wells_out, sems = refs[24:]
    targets = (*refs[19:24], diag_ref, off_ref, *refs[24:28])
    copies = []
    for i in (7, 8, 9, 10, 0, 1, 4, 2, 3, 5, 6):
        copies.append(pltpu.make_async_copy(sources[i], targets[i], sems.at[i]))
        copies[-1].start()
    for copy in copies[:6]:
        copy.wait()
    cx, nz, cy = press_ref.shape
    at_x = lax.axis_index("gx")
    at_y = lax.axis_index("gy")
    layers = 1 if count_x == 2 else 2
    inner_at, edge_at, last, _ = sent_tiles(cx, layers)

    press = press_ref[...]
    water, gas = sat_ref[0], sat_ref[1]
    oil = 1.0 - water - gas
    mobile = [
        water * water / viscosity[0],
        oil * oil / viscosity[1],
        gas * gas / viscosity[2],
    ]

    cells = cell_ref[...]
    perfs = cells.shape[1]
    spot_xz = lax.div(cells, cy)
    spot_y = lax.rem(cells, cy)
    stacked = jnp.concatenate([m.reshape(cx * nz, cy) for m in mobile + [press]], axis=0)
    hot_y = hot_of(iota((cy, perfs), 0) == spot_y)
    picked = split_dot(stacked, hot_y, NN).reshape(4, cx * nz, perfs)
    on_xz = iota((cx * nz, perfs), 0) == spot_xz
    at_perf = [
        jnp.sum(jnp.where(on_xz, picked[i], 0.0), axis=0, keepdims=True) for i in range(4)
    ]
    index_vals = index_ref[...]
    parts = [index_vals * at_perf[i] for i in range(3)]
    strength = index_vals * (at_perf[0] + at_perf[1] + at_perf[2])
    weighted = strength * at_perf[3]
    row = iota((8, perfs), 0)
    both = jnp.where(row == 0, strength, jnp.where(row == 1, weighted, 0.0))
    wells = wells_out.shape[2]
    member = jnp.where(iota((wells, perfs), 0) == well_ref[...], 1.0, 0.0)
    sums = lax.dot_general(both, member, NT, precision=highest, preferred_element_type=f32)
    owned = rate_ref.shape[1]
    square = jnp.broadcast_to(rate_ref[...], (owned, owned))
    column = jnp.sum(
        jnp.where(iota((owned, owned), 0) == iota((owned, owned), 1), square, 0.0),
        axis=1,
        keepdims=True,
    )
    mine = iota((owned, wells), 1) == at_y * owned + iota((owned, wells), 0)
    rates = jnp.sum(jnp.where(mine, column, 0.0), axis=0, keepdims=True)
    pair = sums[:2] - jnp.where(iota((2, wells), 0) == 1, rates, 0.0)
    wells_out[...] = jnp.broadcast_to(pair[None], wells_out.shape)
    wells_copy = pltpu.make_async_copy(wells_out, wells_hbm, sems.at[11])
    wells_copy.start()

    perf_rows = [
        spot_xz.astype(f32),
        spot_y.astype(f32),
        well_ref[...].astype(f32),
        *parts,
        at_perf[3],
        jnp.zeros_like(at_perf[3]),
    ]
    for r, values in enumerate(perf_rows):
        block_out[last, r : r + 1, :] = values
        own_out[BULK * cx, r : r + 1, :] = values
        ya_out[cx, r : r + 1, :] = values
        yb_out[cx, r : r + 1, :] = values

    for copy in copies[6:]:
        copy.wait()
    old_water, old_gas = old_ref[0], old_ref[1]
    old_oil = 1.0 - old_water - old_gas
    pore = pore_ref[...]
    accumulated = [pore * (water - old_water), pore * (oil - old_oil), pore * (gas - old_gas)]
    layer_at = iota((cx, nz, cy), 1)
    columns = [[off_ref[q, c, 0] for c in range(3)] for q in range(6)]
    columns[4] = [jnp.where(layer_at > 0, v, 0.0) for v in columns[4]]
    columns[5] = [jnp.where(layer_at < nz - 1, v, 0.0) for v in columns[5]]
    diag = [[diag_ref[a, b] for b in range(3)] for a in range(3)]
    inverse = 1.0 / (diag[0][0] + diag[1][0] + diag[2][0])
    coefs = [(columns[q][0] + columns[q][1] + columns[q][2]) * inverse for q in range(6)]
    bulk = [press, *mobile, perm_ref[...], *accumulated, inverse, *coefs]

    def cofactor(a, b):
        return (
            diag[(a + 1) % 3][(b + 1) % 3] * diag[(a + 2) % 3][(b + 2) % 3]
            - diag[(a + 1) % 3][(b + 2) % 3] * diag[(a + 2) % 3][(b + 1) % 3]
        )

    cofactors = [[cofactor(a, b) for b in range(3)] for a in range(3)]
    over = 1.0 / (
        diag[0][0] * cofactors[0][0] + diag[0][1] * cofactors[0][1] + diag[0][2] * cofactors[0][2]
    )
    solve = [cofactors[b][a] * over for a in range(3) for b in range(3)]
    for i in range(9):
        dinv_out[i] = solve[i]
    edge = solve + [diag[c][0] for c in range(3)] + [columns[q][c] for q in range(6) for c in range(3)]

    for f in range(BULK):
        own_out[f * cx : (f + 1) * cx] = bulk[f]
    for i, values in enumerate((press, perm_ref[...], water, gas)):
        block_out[i * cx : (i + 1) * cx] = values
    inner = [*coefs, inverse, accumulated[0] + accumulated[1] + accumulated[2]]
    for i in range(INNER):
        for x in range(cx - layers):
            at = inner_at + i * (cx - layers) + x
            if layers == 1:
                block_out[at] = jnp.where(at_x == 0, inner[i][x], inner[i][x + 1])
            else:
                block_out[at] = inner[i][x + 1]
    for e, values in enumerate(edge + accumulated):
        if layers == 1:
            block_out[edge_at + e] = jnp.where(at_x == 0, values[cx - 1], values[0])
        else:
            block_out[edge_at + e] = values[0]
            block_out[edge_at + EDGE + e] = values[cx - 1]

    lane = iota((nz, cy), 1)
    to_left = [jnp.zeros((nz, cy), f32) for _ in range(cx)]
    to_right = [jnp.zeros((nz, cy), f32) for _ in range(cx)]
    for f in range(BULK + EACC):
        wide = WIDE if f < BULK else 1
        shift = f * WIDE if f < BULK else EDGE_AT + f - BULK
        on_left = (lane >= shift) & (lane < shift + wide)
        start = (shift - wide) % cy
        on_right = (lane >= start) & (lane < start + wide)
        values = bulk[f] if f < BULK else edge[f - BULK]
        for x in range(cx):
            turned = pltpu.roll(values[x], shift, 1) if shift else values[x]
            to_left[x] = jnp.where(on_left, turned, to_left[x])
            to_right[x] = jnp.where(on_right, turned, to_right[x])
    for spare in range(cx + 1, 2 * cx):
        yb_out[spare] = jnp.zeros((nz, cy), f32)
    even = lax.rem(at_y, 2) == 0
    for x in range(cx):
        ya_out[x] = jnp.where(even, to_right[x], to_left[x])
        yb_out[x] = jnp.where(even, to_left[x], to_right[x])
    wells_copy.wait()


def main_kernel(count_x, count_y, offsets, *refs):
    width = len(offsets)
    (wells_ref, diag_ref, off_ref, dinv_ref, own_ref), refs = refs[:5], refs[5:]
    blocks, refs = (None, *refs[: width - 1]), refs[width - 1 :]
    ya_refs, refs = refs[:width], refs[width:]
    yb_refs, refs = refs[:width], refs[width:]
    residual_hbm, z_out, sums_out, residual_out, sem = refs

    cx, nz, cy = residual_out.shape[1:]
    total = width * cx
    at_x = lax.axis_index("gx")
    at_y = lax.axis_index("gy")
    even = lax.rem(at_y, 2) == 0
    has_left = jnp.where(at_y > 0, 1.0, 0.0).astype(f32)
    has_right = jnp.where(at_y < count_y - 1, 1.0, 0.0).astype(f32)
    layers = 1 if count_x == 2 else 2
    inner_at, edge_at, last, _ = sent_tiles(cx, layers)
    index_x = [lax.rem(at_x + (o % count_x), count_x) for o in offsets]
    joined = [
        jnp.where(index_x[(j + 1) % width] == index_x[j] + 1, 1.0, 0.0).astype(f32)
        for j in range(width)
    ]

    from_left, from_right = [], []
    for j in range(width):
        first, second = ya_refs[j][: cx + 1], yb_refs[j][: cx + 1]
        from_right.append(jnp.where(even, first, second) * has_right)
        from_left.append(jnp.where(even, second, first) * has_left)
    lane = iota((nz, cy), 1)

    def halo(tiles_l, tiles_r, x, shift, wide):
        back = (cy - shift) % cy
        left, right = tiles_l[x], tiles_r[x]
        if back:
            left, right = pltpu.roll(left, back, 1), pltpu.roll(right, back, 1)
        return jnp.where(lane < wide, right, jnp.where(lane >= cy - wide, left, 0.0))

    def arranged(edges, inner):
        if layers == 2:
            return jnp.stack([edges[0], *inner, edges[1]])
        first = [edges[0], *inner]
        second = [*inner, edges[0]]
        return jnp.stack([jnp.where(at_x == 0, a, b) for a, b in zip(first, second)])

    def received(j):
        block = blocks[j]
        press, perm, water, gas = (block[i * cx : (i + 1) * cx] for i in range(SENT))
        oil = 1.0 - water - gas
        edges = [
            [block[edge_at + side * EDGE + e] for e in range(EDGE)] for side in range(layers)
        ]
        inner = [
            [block[inner_at + i * (cx - layers) + x] for x in range(cx - layers)]
            for i in range(INNER)
        ]
        zero = jnp.zeros((nz, cy), f32)
        acc = [
            arranged(
                [edge[EACC + c] for edge in edges], inner[SUM] if c == 0 else [zero] * (cx - layers)
            )
            for c in range(3)
        ]
        scale = [1.0 / (edge[DCOL] + edge[DCOL + 1] + edge[DCOL + 2]) for edge in edges]
        coefs = [
            arranged(
                [
                    (edge[OFFC + 3 * q] + edge[OFFC + 3 * q + 1] + edge[OFFC + 3 * q + 2]) * by
                    for edge, by in zip(edges, scale)
                ],
                inner[q],
            )
            for q in range(6)
        ]
        mobile = [
            water * water / viscosity[0],
            oil * oil / viscosity[1],
            gas * gas / viscosity[2],
        ]
        return [press, *mobile, perm, *acc, arranged(scale, inner[6]), *coefs]

    others = [received(j) for j in range(1, width)]

    def extended(f):
        own = jnp.concatenate(
            [own_ref[f * cx : (f + 1) * cx], *[other[f] for other in others]], axis=0
        )
        side = jnp.stack(
            [
                halo(from_left[j], from_right[j], x, f * WIDE, WIDE)
                for j in range(width)
                for x in range(cx)
            ]
        )
        return jnp.concatenate([own, side], axis=2)

    lanes = 2 * cy
    level = iota((total, nz, lanes), 1)

    def next_x(v):
        return jnp.concatenate([v[1:], v[:1]], axis=0)

    def last_x(v):
        return jnp.concatenate([v[-1:], v[:-1]], axis=0)

    def next_y(v):
        return pltpu.roll(v, v.shape[2] - 1, 2)

    def last_y(v):
        return pltpu.roll(v, 1, 2)

    def next_z(v):
        return pltpu.roll(v, nz - 1, 1)

    def last_z(v):
        return pltpu.roll(v, 1, 1)

    def seam_after(v):
        rows = [v[i] for i in range(total)]
        for j in range(width):
            rows[j * cx + cx - 1] = rows[j * cx + cx - 1] * joined[j]
        return jnp.stack(rows)

    def seam_before(v):
        rows = [v[i] for i in range(total)]
        for j in range(width):
            at = ((j + 1) % width) * cx
            rows[at] = rows[at] * joined[j]
        return jnp.stack(rows)

    press = extended(PRESS)
    mobile = [extended(MOB + c) for c in range(3)]
    perm = extended(PERM)
    resid = [extended(ACC + c) for c in range(3)]

    for forward, backward, kind in ((next_x, last_x, 0), (next_y, last_y, 1), (next_z, last_z, 2)):
        beyond = forward(perm)
        bottom = perm + beyond
        conduct = 2.0 * perm * beyond / jnp.where(bottom > 0.0, bottom, 1.0)
        if kind == 0:
            conduct = seam_after(conduct)
        if kind == 2:
            conduct = jnp.where(level < nz - 1, vertical_ratio * conduct, 0.0)
        drop = press - forward(press)
        flow = conduct * drop
        for c in range(3):
            passing = flow * jnp.where(drop >= 0.0, mobile[c], forward(mobile[c]))
            resid[c] = resid[c] + passing - backward(passing)

    wells = wells_ref.shape[2]
    perfs = own_ref.shape[2]
    added = [[] for _ in range(3)]
    for j in range(width):
        pair = jnp.sum(wells_ref[pl.ds(index_x[j] * count_y, count_y)], axis=0)
        hole = pair[1:2] / pair[0:1]
        tiles = jnp.concatenate(
            [
                blocks[j][last] if j else own_ref[BULK * cx],
                from_left[j][cx],
                from_right[j][cx],
            ],
            axis=1,
        )
        spot_xz, spot_y, well = tiles[0:1], tiles[1:2], tiles[2:3]
        member = jnp.where(iota((wells, 3 * perfs), 0).astype(f32) == well, 1.0, 0.0)
        hole_at = lax.dot_general(
            jnp.broadcast_to(hole, (8, wells)),
            member,
            NN,
            precision=highest,
            preferred_element_type=f32,
        )[0:1]
        fall = tiles[6:7] - hole_at
        on_xz = iota((cx * nz, 3 * perfs), 0).astype(f32) == spot_xz
        spread = jnp.concatenate(
            [jnp.where(on_xz, tiles[3 + c : 4 + c] * fall, 0.0) for c in range(3)], axis=0
        )
        hot_y = iota((cy, 3 * perfs), 0).astype(f32) == spot_y
        nearby = iota((cy, 3 * perfs), 0)
        source = iota((cy, 3 * perfs), 1)
        kept = jnp.where(
            source < 2 * perfs, jnp.where(nearby >= cy - WIDE, 1, 0), jnp.where(nearby < WIDE, 1, 0)
        )
        hot_side = hot_of(hot_y & (kept == 1))
        inner = split_dot(spread[:, :perfs], hot_of(hot_y[:, :perfs]), NT)
        outer = split_dot(spread[:, perfs:], hot_side[:, perfs:], NT)
        both = jnp.concatenate([inner, outer], axis=1).reshape(3, cx, nz, lanes)
        for c in range(3):
            added[c].append(both[c])
    start = [-(resid[c] + jnp.concatenate(added[c], axis=0)) for c in range(3)]
    for c in range(3):
        residual_out[c] = -start[c][:cx, :, :cy]
    residual_copy = pltpu.make_async_copy(residual_out, residual_hbm, sem)
    residual_copy.start()

    coefs = [extended(COEF + q) for q in range(6)]
    coefs[0] = seam_before(coefs[0])
    coefs[1] = seam_after(coefs[1])
    scaled = (start[0] + start[1] + start[2]) * extended(INV)
    steps = (last_x, next_x, last_y, next_y, last_z, next_z)
    part = scaled
    for _ in range(1, SWEEPS):
        gathered = coefs[0] * steps[0](part)
        for q in range(1, 6):
            gathered = gathered + coefs[q] * steps[q](part)
        part = scaled - gathered

    near = [step(part) for step in steps]
    near[0] = seam_before(near[0])
    near[1] = seam_after(near[1])
    near[4] = jnp.where(level > 0, near[4], 0.0)
    near[5] = jnp.where(level < nz - 1, near[5], 0.0)

    def direction(edge_of, where):
        here = where(part)
        rest = []
        for c in range(3):
            coupled = edge_of(DCOL + c) * here
            for q in range(6):
                coupled = coupled + edge_of(OFFC + 3 * q + c) * where(near[q])
            rest.append(where(start[c]) - coupled)
        solved = []
        for a in range(3):
            value = edge_of(DINV + 3 * a) * rest[0]
            value = value + edge_of(DINV + 3 * a + 1) * rest[1]
            solved.append(value + edge_of(DINV + 3 * a + 2) * rest[2])
        solved[0] = solved[0] + here
        return solved

    def edge_own(e):
        if e < DCOL:
            return dinv_ref[e]
        if e < OFFC:
            return diag_ref[e - DCOL, 0]
        return off_ref[(e - OFFC) // 3, (e - OFFC) % 3, 0]

    def edge_side(e):
        return jnp.stack(
            [halo(from_left[0], from_right[0], x, EDGE_AT + e, 1) for x in range(cx)]
        )

    after, before = 1 % width, width - 1
    z_own = direction(edge_own, lambda v: v[:cx, :, :cy])
    z_side = direction(edge_side, lambda v: v[:cx, :, cy:])
    z_next = direction(
        lambda e: blocks[after][edge_at + e], lambda v: v[after * cx, :, :cy]
    )
    z_last = direction(
        lambda e: blocks[before][edge_at + (layers - 1) * EDGE + e],
        lambda v: v[before * cx + cx - 1, :, :cy],
    )
    level_own = iota((cx, nz, cy), 1)
    around = []
    for k in range(3):
        z_out[k] = z_own[k]
        ext = jnp.concatenate([z_own[k], z_side[k]], axis=2)
        around.append(
            [
                jnp.concatenate([(z_last[k] * joined[width - 1])[None], z_own[k][:-1]], axis=0),
                jnp.concatenate([z_own[k][1:], (z_next[k] * joined[0])[None]], axis=0),
                last_y(ext)[:, :, :cy],
                next_y(ext)[:, :, :cy],
                jnp.where(level_own > 0, last_z(z_own[k]), 0.0),
                jnp.where(level_own < nz - 1, next_z(z_own[k]), 0.0),
            ]
        )
    along = jnp.zeros((nz, cy), f32)
    square = jnp.zeros((nz, cy), f32)
    for c in range(3):
        mapped = diag_ref[c, 0] * z_own[0]
        for k in range(1, 3):
            mapped = mapped + diag_ref[c, k] * z_own[k]
        for q in range(6):
            for k in range(3):
                mapped = mapped + off_ref[q, c, k] * around[k][q]
        along = along + jnp.sum(mapped * start[c][:cx, :, :cy], axis=0)
        square = square + jnp.sum(mapped * mapped, axis=0)
    along = jnp.sum(along, axis=0, keepdims=True)
    square = jnp.sum(square, axis=0, keepdims=True)
    pair = jnp.where(iota((2, cy), 0) == 0, along, square)
    sums_out[...] = jnp.broadcast_to(pair[None], sums_out.shape)
    residual_copy.wait()


def after_kernel(sums_ref, z_ref, update_out):
    pair = jnp.sum(sums_ref[...], axis=0)
    both = jnp.sum(pair, axis=1, keepdims=True)
    step = both[0:1] / both[1:2]
    update_out[...] = z_ref[...] * step[None, None]


def other_pair(device, count_x, count_y):
    x, y = divmod(device, count_y)
    near = y + 1 if y % 2 else y - 1
    if 0 <= near < count_y:
        return x * count_y + near
    return (x ^ 1) * count_y + y if count_x % 2 == 0 else device


def body(
    pressure,
    saturation,
    saturation_old,
    pore_volume,
    permeability,
    jac_diag,
    jac_off,
    perf_cell,
    perf_well,
    perf_index,
    well_rate,
):
    count_x, count_y = lax.axis_size("gx"), lax.axis_size("gy")
    devices = count_x * count_y
    cx, nz, cy = pressure.shape
    wells = well_rate.shape[1] * count_y
    layers = 1 if count_x == 2 else 2
    tiles = sent_tiles(cx, layers)[-1]
    offsets = window(count_x, cx)
    width = len(offsets)
    shape = jax.ShapeDtypeStruct
    whole = pl.BlockSpec(memory_space=pltpu.VMEM)
    anywhere = pl.BlockSpec(memory_space=pltpu.HBM)
    params = pltpu.CompilerParams(vmem_limit_bytes=32 * 1024 * 1024)

    fields = (pressure, saturation, saturation_old, pore_volume, permeability, jac_diag)
    perforations = (perf_cell, perf_well, perf_index, well_rate)
    wells_part, block, own, ya, yb, dinv, diag, off = pl.pallas_call(
        functools.partial(before_kernel, count_x, count_y),
        in_specs=[anywhere] * 11,
        out_specs=[anywhere, *[whole] * 7],
        out_shape=[
            pltpu.HBM((devices, 2, wells), f32),
            shape((tiles, nz, cy), f32),
            shape((BULK * cx + 1, nz, cy), f32),
            shape((cx + 1, nz, cy), f32),
            shape((2 * cx, nz, cy), f32),
            shape((9, cx, nz, cy), f32),
            shape(jac_diag.shape, f32),
            shape(jac_off.shape, f32),
        ],
        scratch_shapes=[
            *[pltpu.VMEM(v.shape, v.dtype) for v in fields[:5]],
            *[pltpu.VMEM(v.shape, v.dtype) for v in perforations],
            pltpu.VMEM((devices, 2, wells), f32),
            pltpu.SemaphoreType.DMA((12,)),
        ],
        compiler_params=params,
        name="before",
    )(*[pltpu.with_memory_space_constraint(v, pltpu.HBM) for v in (*fields, jac_off, *perforations)])

    pairs = [(i, i ^ 1) for i in range(count_y)]
    others = [(i, other_pair(i, count_x, count_y)) for i in range(devices)]

    def from_x(values, offset):
        return lax.ppermute(
            values, "gx", [((i + offset) % count_x, i) for i in range(count_x)]
        )

    ya_got = lax.ppermute(ya, "gy", pairs)
    yb_got = lax.ppermute(yb, ("gx", "gy"), others)
    blocks = [from_x(block, o) for o in offsets[1:]]
    wells_all = lax.all_to_all(wells_part, ("gx", "gy"), 0, 0)
    ya_all = [ya_got] + [from_x(ya_got, o) for o in offsets[1:]]
    yb_all = [yb_got] + [from_x(yb_got, o) for o in offsets[1:]]

    residual, direction, sums = pl.pallas_call(
        functools.partial(main_kernel, count_x, count_y, tuple(offsets)),
        in_specs=[whole] * (4 + 3 * width),
        out_specs=[anywhere, whole, whole],
        out_shape=[
            pltpu.HBM((3, cx, nz, cy), f32),
            shape((3, cx, nz, cy), f32),
            shape((devices, 2, cy), f32),
        ],
        scratch_shapes=[pltpu.VMEM((3, cx, nz, cy), f32), pltpu.SemaphoreType.DMA],
        compiler_params=params,
        name="main",
    )(wells_all, diag, off, dinv, own, *blocks, *ya_all, *yb_all)

    sums_all = lax.all_to_all(sums, ("gx", "gy"), 0, 0)
    update = pl.pallas_call(
        after_kernel,
        in_specs=[whole] * 2,
        out_specs=whole,
        out_shape=shape((3, cx, nz, cy), f32),
        compiler_params=params,
        name="after",
    )(sums_all, direction)
    return (residual, update)


def solution(mesh):
    placed = (
        P("gx", None, "gy"),
        P(None, "gx", None, "gy"),
        P(None, "gx", None, "gy"),
        P("gx", None, "gy"),
        P("gx", None, "gy"),
        P(None, None, "gx", None, "gy"),
        P(None, None, None, "gx", None, "gy"),
        P("gx", "gy"),
        P("gx", "gy"),
        P("gx", "gy"),
        P("gx", "gy"),
    )
    return jax.shard_map(
        body,
        mesh=mesh,
        in_specs=placed,
        out_specs=(P(None, "gx", None, "gy"), P(None, "gx", None, "gy")),
        check_vma=False,
    )
```

```python
import functools

import jax
import jax.numpy as jnp
from jax import lax
from jax.experimental import pallas as pl
from jax.experimental.pallas import tpu as pltpu
from jax.sharding import PartitionSpec as P

SWEEPS = 4
WIDE = SWEEPS + 1

viscosity = (1.0, 2.0, 0.2)
vertical_ratio = 0.1
highest = lax.Precision.HIGHEST
f32 = jnp.float32

PRESS, MOB, PERM, PART, INV, COEF = 0, 1, 4, 5, 8, 9
BULK = 15
FACE = 5
DINV, DCOL, OFFC, EPART, EPRESS, EPERM, EWATER, EGAS = 0, 9, 12, 30, 33, 34, 35, 36
EDGE = 37
SEAM = 30
BORDER_AT = (BULK * WIDE + 1) // 2 * 2
SUM, INNER = 7, 8
TINY = 1e-30
NT = (((1,), (1,)), ((), ()))
NN = (((1,), (0,)), ((), ()))


def iota(shape, axis):
    return lax.broadcasted_iota(jnp.int32, shape, axis)


def split_dot(values, hot, dims):
    rows = values.shape[0]
    high = values.astype(jnp.bfloat16)
    rest = values - high.astype(f32)
    mid = rest.astype(jnp.bfloat16)
    low = (rest - mid.astype(f32)).astype(jnp.bfloat16)
    parts = jnp.concatenate([high, mid, low], axis=0)
    out = lax.dot_general(parts, hot, dims, preferred_element_type=f32)
    return out[:rows] + (out[rows : 2 * rows] + out[2 * rows :])


def hot_of(condition):
    return jnp.where(condition, 1.0, 0.0).astype(jnp.bfloat16)


def sent_tiles(cx, layers):
    edges = INNER * (cx - layers)
    borders = edges + EDGE * layers
    return edges, borders, borders + 1, borders + 2, borders + 3 + cx


def mobilities(water, gas):
    oil = 1.0 - water - gas
    return [
        water * water / viscosity[0],
        oil * oil / viscosity[1],
        gas * gas / viscosity[2],
    ]


def face_flows(here, there, weight):
    conduct = weight * here[PERM] * there[PERM] / (here[PERM] + there[PERM] + TINY)
    drop = here[PRESS] - there[PRESS]
    flow = conduct * drop
    return [
        flow * jnp.where(drop >= 0.0, here[MOB + c], there[MOB + c]) for c in range(3)
    ]


def window(count, cx):
    reach = -(-WIDE // cx)
    if count <= 2 * reach + 1:
        return list(range(count))
    return list(range(reach + 1)) + list(range(-reach, 0))


def before_kernel(
    count_x,
    count_y,
    *refs,
):
    sources, (wells_hbm, block_out, own_out, ya_out, yb_out, dinv_out) = refs[:11], refs[11:17]
    diag_ref, off_ref = refs[17:19]
    press_ref, sat_ref, old_ref, pore_ref, perm_ref = refs[19:24]
    cell_ref, well_ref, index_ref, rate_ref, wells_out, sems = refs[24:]
    targets = (*refs[19:24], diag_ref, off_ref, *refs[24:28])
    copies = []
    for i in (7, 8, 9, 10, 0, 1, 4, 2, 3, 5, 6):
        copies.append(pltpu.make_async_copy(sources[i], targets[i], sems.at[i]))
        copies[-1].start()
    for copy in copies[:6]:
        copy.wait()
    cx, nz, cy = press_ref.shape
    at_x = lax.axis_index("gx")
    at_y = lax.axis_index("gy")
    layers = 1 if count_x == 2 else 2
    edge_at, border_at, last, columns_at, _ = sent_tiles(cx, layers)

    press = press_ref[...]
    water, gas = sat_ref[0], sat_ref[1]
    mobile = mobilities(water, gas)

    cells = cell_ref[...]
    perfs = cells.shape[1]
    spot_xz = lax.div(cells, cy)
    spot_y = lax.rem(cells, cy)
    stacked = jnp.concatenate([m.reshape(cx * nz, cy) for m in mobile + [press]], axis=0)
    hot_y = hot_of(iota((cy, perfs), 0) == spot_y)
    picked = split_dot(stacked, hot_y, NN).reshape(4, cx * nz, perfs)
    on_xz = iota((cx * nz, perfs), 0) == spot_xz
    at_perf = [
        jnp.sum(jnp.where(on_xz, picked[i], 0.0), axis=0, keepdims=True) for i in range(4)
    ]
    index_vals = index_ref[...]
    parts = [index_vals * at_perf[i] for i in range(3)]
    strength = index_vals * (at_perf[0] + at_perf[1] + at_perf[2])
    weighted = strength * at_perf[3]
    row = iota((8, perfs), 0)
    both = jnp.where(row == 0, strength, jnp.where(row == 1, weighted, 0.0))
    wells = wells_out.shape[2]
    member = jnp.where(iota((wells, perfs), 0) == well_ref[...], 1.0, 0.0)
    sums = lax.dot_general(both, member, NT, precision=highest, preferred_element_type=f32)
    owned = rate_ref.shape[1]
    square = jnp.broadcast_to(rate_ref[...], (owned, owned))
    column = jnp.sum(
        jnp.where(iota((owned, owned), 0) == iota((owned, owned), 1), square, 0.0),
        axis=1,
        keepdims=True,
    )
    mine = iota((owned, wells), 1) == at_y * owned + iota((owned, wells), 0)
    rates = jnp.sum(jnp.where(mine, column, 0.0), axis=0, keepdims=True)
    pair = sums[:2] - jnp.where(iota((2, wells), 0) == 1, rates, 0.0)
    wells_out[...] = jnp.broadcast_to(pair[None], wells_out.shape)
    wells_copy = pltpu.make_async_copy(wells_out, wells_hbm, sems.at[11])
    wells_copy.start()

    perf_rows = [
        spot_xz.astype(f32),
        spot_y.astype(f32),
        well_ref[...].astype(f32),
        *parts,
        at_perf[3],
        jnp.zeros_like(at_perf[3]),
    ]
    for r, values in enumerate(perf_rows):
        block_out[last, r : r + 1, :] = values
        block_out[columns_at + cx, r : r + 1, :] = values
        own_out[BULK * cx, r : r + 1, :] = values
        ya_out[cx, r : r + 1, :] = values
        yb_out[cx, r : r + 1, :] = values

    for copy in copies[6:9]:
        copy.wait()
    perm = perm_ref[...]
    old_water, old_gas = old_ref[0], old_ref[1]
    oil, old_oil = 1.0 - water - gas, 1.0 - old_water - old_gas
    pore = pore_ref[...]
    part = [pore * (water - old_water), pore * (oil - old_oil), pore * (gas - old_gas)]
    layer_at = iota((cx, nz, cy), 1)
    lane_at = iota((cx, nz, cy), 2)
    cells_here = [press, *mobile, perm]
    flows = face_flows([v[:-1] for v in cells_here], [v[1:] for v in cells_here], 2.0)
    none = jnp.zeros((1, nz, cy), f32)
    for c in range(3):
        part[c] = part[c] + jnp.concatenate([flows[c], none], axis=0)
        part[c] = part[c] - jnp.concatenate([none, flows[c]], axis=0)
    for axis, weight, inside in (
        (2, 2.0, lane_at < cy - 1),
        (1, 2.0 * vertical_ratio, layer_at < nz - 1),
    ):
        size = cells_here[0].shape[axis]
        flows = face_flows(
            cells_here, [pltpu.roll(v, size - 1, axis) for v in cells_here], weight
        )
        for c in range(3):
            flow = jnp.where(inside, flows[c], 0.0)
            part[c] = part[c] + flow - pltpu.roll(flow, 1, axis)

    for copy in copies[9:]:
        copy.wait()
    columns = [[off_ref[q, c, 0] for c in range(3)] for q in range(6)]
    columns[4] = [jnp.where(layer_at > 0, v, 0.0) for v in columns[4]]
    columns[5] = [jnp.where(layer_at < nz - 1, v, 0.0) for v in columns[5]]
    diag = [[diag_ref[a, b] for b in range(3)] for a in range(3)]
    inverse = 1.0 / (diag[0][0] + diag[1][0] + diag[2][0])
    coefs = [(columns[q][0] + columns[q][1] + columns[q][2]) * inverse for q in range(6)]
    bulk = [press, *mobile, perm, *part, inverse, *coefs]

    def cofactor(a, b):
        return (
            diag[(a + 1) % 3][(b + 1) % 3] * diag[(a + 2) % 3][(b + 2) % 3]
            - diag[(a + 1) % 3][(b + 2) % 3] * diag[(a + 2) % 3][(b + 1) % 3]
        )

    cofactors = [[cofactor(a, b) for b in range(3)] for a in range(3)]
    over = 1.0 / (
        diag[0][0] * cofactors[0][0] + diag[0][1] * cofactors[0][1] + diag[0][2] * cofactors[0][2]
    )
    solve = [cofactors[b][a] * over for a in range(3) for b in range(3)]
    for i in range(9):
        dinv_out[i] = solve[i]
    edge = solve + [diag[c][0] for c in range(3)] + [columns[q][c] for q in range(6) for c in range(3)]

    for f in range(BULK):
        own_out[f * cx : (f + 1) * cx] = bulk[f]
    inner = [*coefs, inverse, part[0] + part[1] + part[2]]
    for i in range(INNER):
        for x in range(cx - layers):
            at = i * (cx - layers) + x
            if layers == 1:
                block_out[at] = jnp.where(at_x == 0, inner[i][x], inner[i][x + 1])
            else:
                block_out[at] = inner[i][x + 1]
    for e, values in enumerate([*edge, *part, press, perm, water, gas]):
        if layers == 1:
            block_out[edge_at + e] = jnp.where(at_x == 0, values[cx - 1], values[0])
        else:
            block_out[edge_at + e] = values[0]
            block_out[edge_at + EDGE + e] = values[cx - 1]

    lane = iota((nz, cy), 1)
    border = jnp.zeros((nz, cy), f32)
    for f in range(FACE):
        for x in range(cx):
            at = BORDER_AT + 2 * (f * cx + x) + 1
            first = pltpu.roll(bulk[f][x], at - 1, 1)
            second = pltpu.roll(bulk[f][x], at + 1, 1)
            border = jnp.where(lane == at - 1, first, jnp.where(lane == at, second, border))
    block_out[border_at] = border
    own_out[BULK * cx + 1] = border

    to_left = [jnp.zeros((nz, cy), f32) for _ in range(cx)]
    to_right = [jnp.zeros((nz, cy), f32) for _ in range(cx)]
    to_left[0] = to_right[0] = border
    for f in range(BULK):
        shift = f * WIDE
        on_left = (lane >= shift) & (lane < shift + WIDE)
        start = (shift - WIDE) % cy
        on_right = (lane >= start) & (lane < start + WIDE)
        for x in range(cx):
            turned = pltpu.roll(bulk[f][x], shift, 1) if shift else bulk[f][x]
            to_left[x] = jnp.where(on_left, turned, to_left[x])
            to_right[x] = jnp.where(on_right, turned, to_right[x])
    for group in range(0, SEAM, cy // (2 * cx)):
        left, right = jnp.zeros((nz, cy), f32), jnp.zeros((nz, cy), f32)
        for e in range(group, min(group + cy // (2 * cx), SEAM)):
            for x in range(cx):
                at = 2 * ((e - group) * cx + x) + 1
                turned = pltpu.roll(edge[e][x], at, 1)
                left = jnp.where(lane == at, turned, left)
                right = jnp.where(lane == at - 1, turned, right)
        to_left.append(left)
        to_right.append(right)
    even = lax.rem(at_y, 2) == 0
    for x in range(cx):
        block_out[columns_at + x] = jnp.where(even, to_right[x], to_left[x])
    for t, (left, right) in enumerate(zip(to_left, to_right)):
        at = t if t < cx else t + 1
        ya_out[at] = jnp.where(even, right, left)
        yb_out[at] = jnp.where(even, left, right)
    for spare in range(len(to_left) + 1, yb_out.shape[0]):
        yb_out[spare] = jnp.zeros((nz, cy), f32)
    wells_copy.wait()


def main_kernel(count_x, count_y, offsets, *refs):
    width = len(offsets)
    (wells_ref, diag_ref, off_ref, dinv_ref, own_ref), refs = refs[:5], refs[5:]
    blocks, refs = (None, *refs[: width - 1]), refs[width - 1 :]
    ya_refs, refs = refs[:width], refs[width:]
    yb_refs, refs = refs[:width], refs[width:]
    residual_hbm, z_out, sums_out, residual_out, sem = refs

    cx, nz, cy = residual_out.shape[1:]
    total = width * cx
    at_x = lax.axis_index("gx")
    at_y = lax.axis_index("gy")
    even = lax.rem(at_y, 2) == 0
    has_left = jnp.where(at_y > 0, 1.0, 0.0).astype(f32)
    has_right = jnp.where(at_y < count_y - 1, 1.0, 0.0).astype(f32)
    layers = 1 if count_x == 2 else 2
    edge_at, border_at, last, columns_at, _ = sent_tiles(cx, layers)
    index_x = [lax.rem(at_x + (o % count_x), count_x) for o in offsets]
    joined = [
        jnp.where(index_x[(j + 1) % width] == index_x[j] + 1, 1.0, 0.0).astype(f32)
        for j in range(width)
    ]

    from_left, from_right = [], []
    for j in range(width):
        first, second = ya_refs[j][: cx + 1], yb_refs[j][: cx + 1]
        from_right.append(jnp.where(even, first, second) * has_right)
        from_left.append(jnp.where(even, second, first) * has_left)
    lane = iota((nz, cy), 1)

    def halo(tiles_l, tiles_r, x, shift, wide):
        back = (cy - shift) % cy
        left, right = tiles_l[x], tiles_r[x]
        if back:
            left, right = pltpu.roll(left, back, 1), pltpu.roll(right, back, 1)
        return jnp.where(lane < wide, right, jnp.where(lane >= cy - wide, left, 0.0))

    def arranged(edges, inner):
        if layers == 2:
            return jnp.stack([edges[0], *inner, edges[1]])
        first = [edges[0], *inner]
        second = [*inner, edges[0]]
        return jnp.stack([jnp.where(at_x == 0, a, b) for a, b in zip(first, second)])

    def received(j):
        block = blocks[j]
        edges = [
            [block[edge_at + side * EDGE + e] for e in range(EDGE)] for side in range(layers)
        ]
        inner = [
            [block[i * (cx - layers) + x] for x in range(cx - layers)] for i in range(INNER)
        ]
        zero = jnp.zeros((nz, cy), f32)
        part = [
            arranged(
                [edge[EPART + c] for edge in edges], inner[SUM] if c == 0 else [zero] * (cx - layers)
            )
            for c in range(3)
        ]
        scale = [1.0 / (edge[DCOL] + edge[DCOL + 1] + edge[DCOL + 2]) for edge in edges]
        coefs = [
            arranged(
                [
                    (edge[OFFC + 3 * q] + edge[OFFC + 3 * q + 1] + edge[OFFC + 3 * q + 2]) * by
                    for edge, by in zip(edges, scale)
                ],
                inner[q],
            )
            for q in range(6)
        ]
        return dict(enumerate([*part, arranged(scale, inner[6]), *coefs], start=PART))

    others = [received(j) for j in range(1, width)]

    def extended(f):
        own = jnp.concatenate(
            [own_ref[f * cx : (f + 1) * cx], *[other[f] for other in others]], axis=0
        )
        side = jnp.stack(
            [
                halo(from_left[j], from_right[j], x, f * WIDE, WIDE)
                for j in range(width)
                for x in range(cx)
            ]
        )
        return jnp.concatenate([own, side], axis=2)

    lanes = 2 * cy
    level = iota((total, nz, lanes), 1)

    def next_x(v):
        return jnp.concatenate([v[1:], v[:1]], axis=0)

    def last_x(v):
        return jnp.concatenate([v[-1:], v[:-1]], axis=0)

    def next_y(v):
        return pltpu.roll(v, v.shape[2] - 1, 2)

    def last_y(v):
        return pltpu.roll(v, 1, 2)

    def next_z(v):
        return pltpu.roll(v, nz - 1, 1)

    def last_z(v):
        return pltpu.roll(v, 1, 1)

    def seam_after(v):
        rows = [v[i] for i in range(total)]
        for j in range(width):
            rows[j * cx + cx - 1] = rows[j * cx + cx - 1] * joined[j]
        return jnp.stack(rows)

    def seam_before(v):
        rows = [v[i] for i in range(total)]
        for j in range(width):
            at = ((j + 1) % width) * cx
            rows[at] = rows[at] * joined[j]
        return jnp.stack(rows)

    resid = [extended(PART + c) for c in range(3)]
    rows = [[resid[c][x] for x in range(total)] for c in range(3)]
    sides = {}

    def side_of(f, x):
        if (f, x) not in sides:
            j = x // cx
            sides[f, x] = halo(from_left[j], from_right[j], x % cx, f * WIDE, WIDE)
        return sides[f, x]

    even_lane = lane % 2 == 0
    ends = (lane == 0) | (lane == cy - 1)
    for j in range(width):
        border = blocks[j][border_at] if j else own_ref[BULK * cx + 1]
        beyond = jnp.where(
            even_lane, pltpu.roll(from_left[j][0], cy - 1, 1), pltpu.roll(from_right[j][0], 1, 1)
        )
        backs = [cy - BORDER_AT - 2 * f * cx for f in range(FACE)]
        flows = face_flows(
            [pltpu.roll(beyond, back, 1) for back in backs],
            [pltpu.roll(border, back, 1) for back in backs],
            2.0,
        )
        for c in range(3):
            flow = jnp.where(lane < 2 * cx, flows[c], 0.0)
            swapped = jnp.where(even_lane, pltpu.roll(flow, cy - 1, 1), pltpu.roll(flow, 1, 1))
            for x in range(cx):
                back = cy - 2 * x - 1
                inward = jnp.where(ends, pltpu.roll(swapped, back, 1), 0.0)
                outward = jnp.where(ends, pltpu.roll(flow, back, 1), 0.0)
                at = j * cx + x
                rows[c][at] = rows[c][at] + jnp.concatenate([-inward, outward], axis=1)

    def edge_cells(j, last_layer):
        x = cx - 1 if last_layer else 0
        if j == 0:
            inside = [own_ref[f * cx + x] for f in range(FACE)]
        else:
            at = edge_at + (EDGE if last_layer and layers == 2 else 0)
            water, gas = blocks[j][at + EWATER], blocks[j][at + EGAS]
            inside = [
                blocks[j][at + EPRESS],
                *mobilities(water, gas),
                blocks[j][at + EPERM],
            ]
        return [
            jnp.concatenate([inside[f], side_of(f, j * cx + x)], axis=1) for f in range(FACE)
        ]

    for j in range(width):
        after = (j + 1) % width
        flows = face_flows(edge_cells(j, True), edge_cells(after, False), 2.0 * joined[j])
        for c in range(3):
            near_x, far_x = j * cx + cx - 1, after * cx
            rows[c][near_x] = rows[c][near_x] + flows[c]
            rows[c][far_x] = rows[c][far_x] - flows[c]
    resid = [jnp.stack(rows[c]) for c in range(3)]

    wells = wells_ref.shape[2]
    perfs = own_ref.shape[2]
    added = [[] for _ in range(3)]
    for j in range(width):
        pair = jnp.sum(wells_ref[pl.ds(index_x[j] * count_y, count_y)], axis=0)
        hole = pair[1:2] / pair[0:1]
        tiles = jnp.concatenate(
            [
                blocks[j][last] if j else own_ref[BULK * cx],
                from_left[j][cx],
                from_right[j][cx],
            ],
            axis=1,
        )
        spot_xz, spot_y, well = tiles[0:1], tiles[1:2], tiles[2:3]
        member = hot_of(iota((wells, 3 * perfs), 0).astype(f32) == well)
        hole_at = split_dot(jnp.broadcast_to(hole, (16, wells)), member, NN)[0:1]
        fall = tiles[6:7] - hole_at
        on_xz = iota((cx * nz, 3 * perfs), 0).astype(f32) == spot_xz
        spread = jnp.concatenate(
            [jnp.where(on_xz, tiles[3 + c : 4 + c] * fall, 0.0) for c in range(3)], axis=0
        )
        hot_y = iota((cy, 3 * perfs), 0).astype(f32) == spot_y
        nearby = iota((cy, 3 * perfs), 0)
        source = iota((cy, 3 * perfs), 1)
        kept = jnp.where(
            source < 2 * perfs, jnp.where(nearby >= cy - WIDE, 1, 0), jnp.where(nearby < WIDE, 1, 0)
        )
        hot_side = hot_of(hot_y & (kept == 1))
        inner = split_dot(spread[:, :perfs], hot_of(hot_y[:, :perfs]), NT)
        outer = split_dot(spread[:, perfs:], hot_side[:, perfs:], NT)
        both = jnp.concatenate([inner, outer], axis=1).reshape(3, cx, nz, lanes)
        for c in range(3):
            added[c].append(both[c])
    start = [-(resid[c] + jnp.concatenate(added[c], axis=0)) for c in range(3)]
    for c in range(3):
        residual_out[c] = -start[c][:cx, :, :cy]
    residual_copy = pltpu.make_async_copy(residual_out, residual_hbm, sem)
    residual_copy.start()

    coefs = [extended(COEF + q) for q in range(6)]
    coefs[0] = seam_before(coefs[0])
    coefs[1] = seam_after(coefs[1])
    scaled = (start[0] + start[1] + start[2]) * extended(INV)
    steps = (last_x, next_x, last_y, next_y, last_z, next_z)
    part = scaled
    for _ in range(1, SWEEPS):
        gathered = coefs[0] * steps[0](part)
        for q in range(1, 6):
            gathered = gathered + coefs[q] * steps[q](part)
        part = scaled - gathered

    near = [step(part) for step in steps]
    near[0] = seam_before(near[0])
    near[1] = seam_after(near[1])
    near[4] = jnp.where(level > 0, near[4], 0.0)
    near[5] = jnp.where(level < nz - 1, near[5], 0.0)

    def direction(edge_of, where):
        here = where(part)
        rest = []
        for c in range(3):
            coupled = edge_of(DCOL + c) * here
            for q in range(6):
                coupled = coupled + edge_of(OFFC + 3 * q + c) * where(near[q])
            rest.append(where(start[c]) - coupled)
        solved = []
        for a in range(3):
            value = edge_of(DINV + 3 * a) * rest[0]
            value = value + edge_of(DINV + 3 * a + 1) * rest[1]
            solved.append(value + edge_of(DINV + 3 * a + 2) * rest[2])
        solved[0] = solved[0] + here
        return solved

    def edge_own(e):
        if e < DCOL:
            return dinv_ref[e]
        if e < OFFC:
            return diag_ref[e - DCOL, 0]
        return off_ref[(e - OFFC) // 3, (e - OFFC) % 3, 0]

    beside = []
    for t in range(cx + 1, cx + 1 - (-SEAM * 2 * cx // cy)):
        one, two = ya_refs[0][t], yb_refs[0][t]
        left, right = jnp.where(even, two, one), jnp.where(even, one, two)
        beside.append(jnp.where(even_lane, left, right))

    def edge_side(e):
        tile, place = divmod(2 * cx * e, cy)
        return pltpu.roll(beside[tile], cy - place, 1) if place else beside[tile]

    def gathered_side(v):
        packed = jnp.zeros((nz, cy), f32)
        for x in range(cx):
            turned = pltpu.roll(v[x, :, cy:], 2 * x + 1, 1)
            packed = jnp.where((lane >= 2 * x) & (lane < 2 * x + 2), turned, packed)
        return packed

    after, before = 1 % width, width - 1
    z_own = direction(edge_own, lambda v: v[:cx, :, :cy])
    z_side = [
        jnp.stack([pltpu.roll(v, cy - 2 * x - 1, 1) for x in range(cx)])
        for v in direction(edge_side, gathered_side)
    ]
    if layers == 1:
        z_next = z_last = direction(
            lambda e: blocks[after][edge_at + e],
            lambda v: jnp.where(at_x == 0, v[cx, :, :cy], v[total - 1, :, :cy]),
        )
    else:
        z_next = direction(
            lambda e: blocks[after][edge_at + e], lambda v: v[after * cx, :, :cy]
        )
        z_last = direction(
            lambda e: blocks[before][edge_at + EDGE + e],
            lambda v: v[before * cx + cx - 1, :, :cy],
        )
    level_own = iota((cx, nz, cy), 1)
    around = []
    for k in range(3):
        z_out[k] = z_own[k]
        ext = jnp.concatenate([z_own[k], z_side[k]], axis=2)
        around.append(
            [
                jnp.concatenate([(z_last[k] * joined[width - 1])[None], z_own[k][:-1]], axis=0),
                jnp.concatenate([z_own[k][1:], (z_next[k] * joined[0])[None]], axis=0),
                last_y(ext)[:, :, :cy],
                next_y(ext)[:, :, :cy],
                jnp.where(level_own > 0, last_z(z_own[k]), 0.0),
                jnp.where(level_own < nz - 1, next_z(z_own[k]), 0.0),
            ]
        )
    along = jnp.zeros((nz, cy), f32)
    square = jnp.zeros((nz, cy), f32)
    for c in range(3):
        mapped = diag_ref[c, 0] * z_own[0]
        for k in range(1, 3):
            mapped = mapped + diag_ref[c, k] * z_own[k]
        for q in range(6):
            for k in range(3):
                mapped = mapped + off_ref[q, c, k] * around[k][q]
        along = along + jnp.sum(mapped * start[c][:cx, :, :cy], axis=0)
        square = square + jnp.sum(mapped * mapped, axis=0)
    along = jnp.sum(along, axis=0, keepdims=True)
    square = jnp.sum(square, axis=0, keepdims=True)
    pair = jnp.where(iota((2, cy), 0) == 0, along, square)
    sums_out[...] = jnp.broadcast_to(pair[None], sums_out.shape)
    residual_copy.wait()


def after_kernel(sums_ref, z_ref, update_out):
    pair = jnp.sum(sums_ref[...], axis=0)
    both = jnp.sum(pair, axis=1, keepdims=True)
    step = both[0:1] / both[1:2]
    update_out[...] = z_ref[...] * step[None, None]


def other_pair(device, count_x, count_y):
    x, y = divmod(device, count_y)
    near = y + 1 if y % 2 else y - 1
    if 0 <= near < count_y:
        return x * count_y + near
    return (x ^ 1) * count_y + y if count_x % 2 == 0 else device


def body(
    pressure,
    saturation,
    saturation_old,
    pore_volume,
    permeability,
    jac_diag,
    jac_off,
    perf_cell,
    perf_well,
    perf_index,
    well_rate,
):
    count_x, count_y = lax.axis_size("gx"), lax.axis_size("gy")
    devices = count_x * count_y
    cx, nz, cy = pressure.shape
    wells = well_rate.shape[1] * count_y
    layers = 1 if count_x == 2 else 2
    columns_at, tiles = sent_tiles(cx, layers)[-2:]
    groups = -(-SEAM * 2 * cx // cy)
    offsets = window(count_x, cx)
    width = len(offsets)
    shape = jax.ShapeDtypeStruct
    whole = pl.BlockSpec(memory_space=pltpu.VMEM)
    anywhere = pl.BlockSpec(memory_space=pltpu.HBM)
    params = pltpu.CompilerParams(vmem_limit_bytes=32 * 1024 * 1024)

    fields = (pressure, saturation, saturation_old, pore_volume, permeability, jac_diag)
    perforations = (perf_cell, perf_well, perf_index, well_rate)
    wells_part, block, own, ya, yb, dinv, diag, off = pl.pallas_call(
        functools.partial(before_kernel, count_x, count_y),
        in_specs=[anywhere] * 11,
        out_specs=[anywhere, *[whole] * 7],
        out_shape=[
            pltpu.HBM((devices, 2, wells), f32),
            shape((tiles, nz, cy), f32),
            shape((BULK * cx + 2, nz, cy), f32),
            shape((cx + 1 + groups, nz, cy), f32),
            shape((max(cx + 1 + groups, 2 * cx), nz, cy), f32),
            shape((9, cx, nz, cy), f32),
            shape(jac_diag.shape, f32),
            shape(jac_off.shape, f32),
        ],
        scratch_shapes=[
            *[pltpu.VMEM(v.shape, v.dtype) for v in fields[:5]],
            *[pltpu.VMEM(v.shape, v.dtype) for v in perforations],
            pltpu.VMEM((devices, 2, wells), f32),
            pltpu.SemaphoreType.DMA((12,)),
        ],
        compiler_params=params,
        name="before",
    )(*[pltpu.with_memory_space_constraint(v, pltpu.HBM) for v in (*fields, jac_off, *perforations)])

    pairs = [(i, i ^ 1) for i in range(count_y)]
    others = [(i, other_pair(i, count_x, count_y)) for i in range(devices)]

    def from_x(values, offset):
        return lax.ppermute(
            values, "gx", [((i + offset) % count_x, i) for i in range(count_x)]
        )

    ya_got = lax.ppermute(ya, "gy", pairs)
    yb_got = lax.ppermute(yb, ("gx", "gy"), others)
    blocks = [from_x(block, o) for o in offsets[1:]]
    wells_all = lax.all_to_all(wells_part, ("gx", "gy"), 0, 0)
    ya_all = [ya_got] + [lax.ppermute(v[columns_at:], "gy", pairs) for v in blocks]
    yb_all = [yb_got] + [from_x(yb_got, o) for o in offsets[1:]]

    residual, direction, sums = pl.pallas_call(
        functools.partial(main_kernel, count_x, count_y, tuple(offsets)),
        in_specs=[whole] * (4 + 3 * width),
        out_specs=[anywhere, whole, whole],
        out_shape=[
            pltpu.HBM((3, cx, nz, cy), f32),
            shape((3, cx, nz, cy), f32),
            shape((devices, 2, cy), f32),
        ],
        scratch_shapes=[pltpu.VMEM((3, cx, nz, cy), f32), pltpu.SemaphoreType.DMA],
        compiler_params=params,
        name="main",
    )(wells_all, diag, off, dinv, own, *blocks, *ya_all, *yb_all)

    sums_all = lax.all_to_all(sums, ("gx", "gy"), 0, 0)
    update = pl.pallas_call(
        after_kernel,
        in_specs=[whole] * 2,
        out_specs=whole,
        out_shape=shape((3, cx, nz, cy), f32),
        compiler_params=params,
        name="after",
    )(sums_all, direction)
    return (residual, update)


def solution(mesh):
    placed = (
        P("gx", None, "gy"),
        P(None, "gx", None, "gy"),
        P(None, "gx", None, "gy"),
        P("gx", None, "gy"),
        P("gx", None, "gy"),
        P(None, None, "gx", None, "gy"),
        P(None, None, None, "gx", None, "gy"),
        P("gx", "gy"),
        P("gx", "gy"),
        P("gx", "gy"),
        P("gx", "gy"),
    )
    return jax.shard_map(
        body,
        mesh=mesh,
        in_specs=placed,
        out_specs=(P(None, "gx", None, "gy"), P(None, "gx", None, "gy")),
        check_vma=False,
    )
```

```python
import functools

import jax
import jax.numpy as jnp
from jax import lax
from jax.experimental import pallas as pl
from jax.experimental.pallas import tpu as pltpu
from jax.sharding import PartitionSpec as P

SWEEPS = 4
WIDE = SWEEPS + 1

viscosity = (1.0, 2.0, 0.2)
vertical_ratio = 0.1
highest = lax.Precision.HIGHEST
f32 = jnp.float32

PRESS, MOB, PERM, PART, INV, COEF = 0, 1, 4, 5, 8, 9
BULK = 15
FACE = 5
DINV, DCOL, OFFC, EPART, EPRESS, EPERM, EWATER, EGAS = 0, 9, 12, 30, 33, 34, 35, 36
EDGE = 37
SEAM = 30
BORDER_AT = (BULK * WIDE + 1) // 2 * 2
SUM, INNER = 7, 8
TINY = 1e-30
NT = (((1,), (1,)), ((), ()))
NN = (((1,), (0,)), ((), ()))


def iota(shape, axis):
    return lax.broadcasted_iota(jnp.int32, shape, axis)


def split_dot(values, hot, dims):
    rows = values.shape[0]
    high = values.astype(jnp.bfloat16)
    rest = values - high.astype(f32)
    mid = rest.astype(jnp.bfloat16)
    low = (rest - mid.astype(f32)).astype(jnp.bfloat16)
    parts = jnp.concatenate([high, mid, low], axis=0)
    out = lax.dot_general(parts, hot, dims, preferred_element_type=f32)
    return out[:rows] + (out[rows : 2 * rows] + out[2 * rows :])


def hot_of(condition):
    return jnp.where(condition, 1.0, 0.0).astype(jnp.bfloat16)


def sent_tiles(cx, layers):
    edges = INNER * (cx - layers)
    borders = edges + EDGE * layers
    return edges, borders, borders + 1, borders + 2, borders + 3 + cx


def mobilities(water, gas):
    oil = 1.0 - water - gas
    return [
        water * water / viscosity[0],
        oil * oil / viscosity[1],
        gas * gas / viscosity[2],
    ]


def face_flows(here, there, weight):
    conduct = weight * here[PERM] * there[PERM] / (here[PERM] + there[PERM] + TINY)
    drop = here[PRESS] - there[PRESS]
    flow = conduct * drop
    return [
        flow * jnp.where(drop >= 0.0, here[MOB + c], there[MOB + c]) for c in range(3)
    ]


def window(count, cx):
    reach = -(-WIDE // cx)
    if count <= 2 * reach + 1:
        return list(range(count))
    return list(range(reach + 1)) + list(range(-reach, 0))


def before_kernel(
    count_x,
    count_y,
    *refs,
):
    sources, (wells_hbm, block_out, own_out, ya_out, yb_out, dinv_out) = refs[:11], refs[11:17]
    diag_ref, off_ref = refs[17:19]
    press_ref, sat_ref, old_ref, pore_ref, perm_ref = refs[19:24]
    cell_ref, well_ref, index_ref, rate_ref, wells_out, sems = refs[24:]
    targets = (*refs[19:24], diag_ref, off_ref, *refs[24:28])
    copies = []
    for i in (7, 8, 9, 10, 0, 1, 4, 2, 3, 5, 6):
        copies.append(pltpu.make_async_copy(sources[i], targets[i], sems.at[i]))
        copies[-1].start()
    for copy in copies[:6]:
        copy.wait()
    cx, nz, cy = press_ref.shape
    at_x = lax.axis_index("gx")
    at_y = lax.axis_index("gy")
    layers = 1 if count_x == 2 else 2
    edge_at, border_at, last, columns_at, _ = sent_tiles(cx, layers)

    press = press_ref[...]
    water, gas = sat_ref[0], sat_ref[1]
    mobile = mobilities(water, gas)

    cells = cell_ref[...]
    perfs = cells.shape[1]
    spot_xz = lax.div(cells, cy)
    spot_y = lax.rem(cells, cy)
    stacked = jnp.concatenate([m.reshape(cx * nz, cy) for m in mobile + [press]], axis=0)
    hot_y = hot_of(iota((cy, perfs), 0) == spot_y)
    picked = split_dot(stacked, hot_y, NN).reshape(4, cx * nz, perfs)
    on_xz = iota((cx * nz, perfs), 0) == spot_xz
    at_perf = [
        jnp.sum(jnp.where(on_xz, picked[i], 0.0), axis=0, keepdims=True) for i in range(4)
    ]
    index_vals = index_ref[...]
    parts = [index_vals * at_perf[i] for i in range(3)]
    strength = index_vals * (at_perf[0] + at_perf[1] + at_perf[2])
    weighted = strength * at_perf[3]
    row = iota((8, perfs), 0)
    both = jnp.where(row == 0, strength, jnp.where(row == 1, weighted, 0.0))
    wells = wells_out.shape[2]
    member = jnp.where(iota((wells, perfs), 0) == well_ref[...], 1.0, 0.0)
    sums = lax.dot_general(both, member, NT, precision=highest, preferred_element_type=f32)
    owned = rate_ref.shape[1]
    square = jnp.broadcast_to(rate_ref[...], (owned, owned))
    column = jnp.sum(
        jnp.where(iota((owned, owned), 0) == iota((owned, owned), 1), square, 0.0),
        axis=1,
        keepdims=True,
    )
    mine = iota((owned, wells), 1) == at_y * owned + iota((owned, wells), 0)
    rates = jnp.sum(jnp.where(mine, column, 0.0), axis=0, keepdims=True)
    pair = sums[:2] - jnp.where(iota((2, wells), 0) == 1, rates, 0.0)
    wells_out[...] = jnp.broadcast_to(pair[None], wells_out.shape)
    wells_copy = pltpu.make_async_copy(wells_out, wells_hbm, sems.at[11])
    wells_copy.start()

    perf_rows = [
        spot_xz.astype(f32),
        spot_y.astype(f32),
        well_ref[...].astype(f32),
        *parts,
        at_perf[3],
        jnp.zeros_like(at_perf[3]),
    ]
    for r, values in enumerate(perf_rows):
        block_out[last, r : r + 1, :] = values
        block_out[columns_at + cx, r : r + 1, :] = values
        own_out[BULK * cx, r : r + 1, :] = values
        ya_out[cx, r : r + 1, :] = values
        yb_out[cx, r : r + 1, :] = values

    for copy in copies[6:9]:
        copy.wait()
    perm = perm_ref[...]
    old_water, old_gas = old_ref[0], old_ref[1]
    oil, old_oil = 1.0 - water - gas, 1.0 - old_water - old_gas
    pore = pore_ref[...]
    part = [pore * (water - old_water), pore * (oil - old_oil), pore * (gas - old_gas)]
    layer_at = iota((cx, nz, cy), 1)
    lane_at = iota((cx, nz, cy), 2)
    cells_here = [press, *mobile, perm]
    flows = face_flows([v[:-1] for v in cells_here], [v[1:] for v in cells_here], 2.0)
    none = jnp.zeros((1, nz, cy), f32)
    for c in range(3):
        part[c] = part[c] + jnp.concatenate([flows[c], none], axis=0)
        part[c] = part[c] - jnp.concatenate([none, flows[c]], axis=0)
    for axis, weight, inside in (
        (2, 2.0, lane_at < cy - 1),
        (1, 2.0 * vertical_ratio, layer_at < nz - 1),
    ):
        size = cells_here[0].shape[axis]
        flows = face_flows(
            cells_here, [pltpu.roll(v, size - 1, axis) for v in cells_here], weight
        )
        for c in range(3):
            flow = jnp.where(inside, flows[c], 0.0)
            part[c] = part[c] + flow - pltpu.roll(flow, 1, axis)

    for copy in copies[9:]:
        copy.wait()
    columns = [[off_ref[q, c, 0] for c in range(3)] for q in range(6)]
    columns[4] = [jnp.where(layer_at > 0, v, 0.0) for v in columns[4]]
    columns[5] = [jnp.where(layer_at < nz - 1, v, 0.0) for v in columns[5]]
    diag = [[diag_ref[a, b] for b in range(3)] for a in range(3)]
    inverse = 1.0 / (diag[0][0] + diag[1][0] + diag[2][0])
    coefs = [(columns[q][0] + columns[q][1] + columns[q][2]) * inverse for q in range(6)]
    bulk = [press, *mobile, perm, *part, inverse, *coefs]

    def cofactor(a, b):
        return (
            diag[(a + 1) % 3][(b + 1) % 3] * diag[(a + 2) % 3][(b + 2) % 3]
            - diag[(a + 1) % 3][(b + 2) % 3] * diag[(a + 2) % 3][(b + 1) % 3]
        )

    cofactors = [[cofactor(a, b) for b in range(3)] for a in range(3)]
    over = 1.0 / (
        diag[0][0] * cofactors[0][0] + diag[0][1] * cofactors[0][1] + diag[0][2] * cofactors[0][2]
    )
    solve = [cofactors[b][a] * over for a in range(3) for b in range(3)]
    for i in range(9):
        dinv_out[i] = solve[i]
    edge = solve + [diag[c][0] for c in range(3)] + [columns[q][c] for q in range(6) for c in range(3)]

    for f in range(BULK):
        own_out[f * cx : (f + 1) * cx] = bulk[f]
    inner = [*coefs, inverse, part[0] + part[1] + part[2]]
    for i in range(INNER):
        for x in range(cx - layers):
            at = i * (cx - layers) + x
            if layers == 1:
                block_out[at] = jnp.where(at_x == 0, inner[i][x], inner[i][x + 1])
            else:
                block_out[at] = inner[i][x + 1]
    for e, values in enumerate([*edge, *part, press, perm, water, gas]):
        if layers == 1:
            block_out[edge_at + e] = jnp.where(at_x == 0, values[cx - 1], values[0])
        else:
            block_out[edge_at + e] = values[0]
            block_out[edge_at + EDGE + e] = values[cx - 1]

    lane = iota((nz, cy), 1)
    border = jnp.zeros((nz, cy), f32)
    for f in range(FACE):
        for x in range(cx):
            at = BORDER_AT + 2 * (f * cx + x) + 1
            first = pltpu.roll(bulk[f][x], at - 1, 1)
            second = pltpu.roll(bulk[f][x], at + 1, 1)
            border = jnp.where(lane == at - 1, first, jnp.where(lane == at, second, border))
    block_out[border_at] = border
    own_out[BULK * cx + 1] = border

    to_left = [jnp.zeros((nz, cy), f32) for _ in range(cx)]
    to_right = [jnp.zeros((nz, cy), f32) for _ in range(cx)]
    to_left[0] = to_right[0] = border
    for f in range(BULK):
        shift = f * WIDE
        on_left = (lane >= shift) & (lane < shift + WIDE)
        start = (shift - WIDE) % cy
        on_right = (lane >= start) & (lane < start + WIDE)
        for x in range(cx):
            turned = pltpu.roll(bulk[f][x], shift, 1) if shift else bulk[f][x]
            to_left[x] = jnp.where(on_left, turned, to_left[x])
            to_right[x] = jnp.where(on_right, turned, to_right[x])
    for group in range(0, SEAM, cy // (2 * cx)):
        left, right = jnp.zeros((nz, cy), f32), jnp.zeros((nz, cy), f32)
        for e in range(group, min(group + cy // (2 * cx), SEAM)):
            for x in range(cx):
                at = 2 * ((e - group) * cx + x) + 1
                turned = pltpu.roll(edge[e][x], at, 1)
                left = jnp.where(lane == at, turned, left)
                right = jnp.where(lane == at - 1, turned, right)
        to_left.append(left)
        to_right.append(right)
    even = lax.rem(at_y, 2) == 0
    for x in range(cx):
        block_out[columns_at + x] = jnp.where(even, to_right[x], to_left[x])
    for t, (left, right) in enumerate(zip(to_left, to_right)):
        at = t if t < cx else t + 1
        ya_out[at] = jnp.where(even, right, left)
        yb_out[at] = jnp.where(even, left, right)
    for spare in range(len(to_left) + 1, yb_out.shape[0]):
        yb_out[spare] = jnp.zeros((nz, cy), f32)
    wells_copy.wait()


def main_kernel(count_x, count_y, offsets, *refs):
    width = len(offsets)
    (wells_ref, diag_ref, off_ref, dinv_ref, own_ref), refs = refs[:5], refs[5:]
    blocks, refs = (None, *refs[: width - 1]), refs[width - 1 :]
    ya_refs, refs = refs[:width], refs[width:]
    yb_refs, refs = refs[:width], refs[width:]
    residual_out, z_out, sums_out = refs

    cx, nz, cy = residual_out.shape[1:]
    total = width * cx
    at_x = lax.axis_index("gx")
    at_y = lax.axis_index("gy")
    even = lax.rem(at_y, 2) == 0
    has_left = jnp.where(at_y > 0, 1.0, 0.0).astype(f32)
    has_right = jnp.where(at_y < count_y - 1, 1.0, 0.0).astype(f32)
    layers = 1 if count_x == 2 else 2
    edge_at, border_at, last, columns_at, _ = sent_tiles(cx, layers)
    index_x = [lax.rem(at_x + (o % count_x), count_x) for o in offsets]
    joined = [
        jnp.where(index_x[(j + 1) % width] == index_x[j] + 1, 1.0, 0.0).astype(f32)
        for j in range(width)
    ]

    from_left, from_right = [], []
    for j in range(width):
        first, second = ya_refs[j][: cx + 1], yb_refs[j][: cx + 1]
        from_right.append(jnp.where(even, first, second) * has_right)
        from_left.append(jnp.where(even, second, first) * has_left)
    lane = iota((nz, cy), 1)

    def halo(tiles_l, tiles_r, x, shift, wide):
        back = (cy - shift) % cy
        left, right = tiles_l[x], tiles_r[x]
        if back:
            left, right = pltpu.roll(left, back, 1), pltpu.roll(right, back, 1)
        return jnp.where(lane < wide, right, jnp.where(lane >= cy - wide, left, 0.0))

    def arranged(edges, inner):
        if layers == 2:
            return jnp.stack([edges[0], *inner, edges[1]])
        first = [edges[0], *inner]
        second = [*inner, edges[0]]
        return jnp.stack([jnp.where(at_x == 0, a, b) for a, b in zip(first, second)])

    def received(j):
        block = blocks[j]
        edges = [
            [block[edge_at + side * EDGE + e] for e in range(EDGE)] for side in range(layers)
        ]
        inner = [
            [block[i * (cx - layers) + x] for x in range(cx - layers)] for i in range(INNER)
        ]
        zero = jnp.zeros((nz, cy), f32)
        part = [
            arranged(
                [edge[EPART + c] for edge in edges], inner[SUM] if c == 0 else [zero] * (cx - layers)
            )
            for c in range(3)
        ]
        scale = [1.0 / (edge[DCOL] + edge[DCOL + 1] + edge[DCOL + 2]) for edge in edges]
        coefs = [
            arranged(
                [
                    (edge[OFFC + 3 * q] + edge[OFFC + 3 * q + 1] + edge[OFFC + 3 * q + 2]) * by
                    for edge, by in zip(edges, scale)
                ],
                inner[q],
            )
            for q in range(6)
        ]
        return dict(enumerate([*part, arranged(scale, inner[6]), *coefs], start=PART))

    others = [received(j) for j in range(1, width)]

    def extended(f):
        own = jnp.concatenate(
            [own_ref[f * cx : (f + 1) * cx], *[other[f] for other in others]], axis=0
        )
        side = jnp.stack(
            [
                halo(from_left[j], from_right[j], x, f * WIDE, WIDE)
                for j in range(width)
                for x in range(cx)
            ]
        )
        return jnp.concatenate([own, side], axis=2)

    lanes = 2 * cy
    level = iota((total, nz, lanes), 1)

    def next_x(v):
        return jnp.concatenate([v[1:], v[:1]], axis=0)

    def last_x(v):
        return jnp.concatenate([v[-1:], v[:-1]], axis=0)

    def next_y(v):
        return pltpu.roll(v, v.shape[2] - 1, 2)

    def last_y(v):
        return pltpu.roll(v, 1, 2)

    def next_z(v):
        return pltpu.roll(v, nz - 1, 1)

    def last_z(v):
        return pltpu.roll(v, 1, 1)

    def seam_after(v):
        rows = [v[i] for i in range(total)]
        for j in range(width):
            rows[j * cx + cx - 1] = rows[j * cx + cx - 1] * joined[j]
        return jnp.stack(rows)

    def seam_before(v):
        rows = [v[i] for i in range(total)]
        for j in range(width):
            at = ((j + 1) % width) * cx
            rows[at] = rows[at] * joined[j]
        return jnp.stack(rows)

    resid = [extended(PART + c) for c in range(3)]
    rows = [[resid[c][x] for x in range(total)] for c in range(3)]
    sides = {}

    def side_of(f, x):
        if (f, x) not in sides:
            j = x // cx
            sides[f, x] = halo(from_left[j], from_right[j], x % cx, f * WIDE, WIDE)
        return sides[f, x]

    even_lane = lane % 2 == 0
    ends = (lane == 0) | (lane == cy - 1)
    for j in range(width):
        border = blocks[j][border_at] if j else own_ref[BULK * cx + 1]
        beyond = jnp.where(
            even_lane, pltpu.roll(from_left[j][0], cy - 1, 1), pltpu.roll(from_right[j][0], 1, 1)
        )
        backs = [cy - BORDER_AT - 2 * f * cx for f in range(FACE)]
        flows = face_flows(
            [pltpu.roll(beyond, back, 1) for back in backs],
            [pltpu.roll(border, back, 1) for back in backs],
            2.0,
        )
        for c in range(3):
            flow = jnp.where(lane < 2 * cx, flows[c], 0.0)
            swapped = jnp.where(even_lane, pltpu.roll(flow, cy - 1, 1), pltpu.roll(flow, 1, 1))
            for x in range(cx):
                back = cy - 2 * x - 1
                inward = jnp.where(ends, pltpu.roll(swapped, back, 1), 0.0)
                outward = jnp.where(ends, pltpu.roll(flow, back, 1), 0.0)
                at = j * cx + x
                rows[c][at] = rows[c][at] + jnp.concatenate([-inward, outward], axis=1)

    def edge_cells(j, last_layer):
        x = cx - 1 if last_layer else 0
        if j == 0:
            inside = [own_ref[f * cx + x] for f in range(FACE)]
        else:
            at = edge_at + (EDGE if last_layer and layers == 2 else 0)
            water, gas = blocks[j][at + EWATER], blocks[j][at + EGAS]
            inside = [
                blocks[j][at + EPRESS],
                *mobilities(water, gas),
                blocks[j][at + EPERM],
            ]
        return [
            jnp.concatenate([inside[f], side_of(f, j * cx + x)], axis=1) for f in range(FACE)
        ]

    for j in range(width):
        after = (j + 1) % width
        flows = face_flows(edge_cells(j, True), edge_cells(after, False), 2.0 * joined[j])
        for c in range(3):
            near_x, far_x = j * cx + cx - 1, after * cx
            rows[c][near_x] = rows[c][near_x] + flows[c]
            rows[c][far_x] = rows[c][far_x] - flows[c]
    resid = [jnp.stack(rows[c]) for c in range(3)]

    wells = wells_ref.shape[2]
    perfs = own_ref.shape[2]
    added = [[] for _ in range(3)]
    for j in range(width):
        pair = jnp.sum(wells_ref[pl.ds(index_x[j] * count_y, count_y)], axis=0)
        hole = pair[1:2] / pair[0:1]
        tiles = jnp.concatenate(
            [
                blocks[j][last] if j else own_ref[BULK * cx],
                from_left[j][cx],
                from_right[j][cx],
            ],
            axis=1,
        )
        spot_xz, spot_y, well = tiles[0:1], tiles[1:2], tiles[2:3]
        member = hot_of(iota((wells, 3 * perfs), 0).astype(f32) == well)
        hole_at = split_dot(jnp.broadcast_to(hole, (16, wells)), member, NN)[0:1]
        fall = tiles[6:7] - hole_at
        on_xz = iota((cx * nz, 3 * perfs), 0).astype(f32) == spot_xz
        spread = jnp.concatenate(
            [jnp.where(on_xz, tiles[3 + c : 4 + c] * fall, 0.0) for c in range(3)], axis=0
        )
        hot_y = iota((cy, 3 * perfs), 0).astype(f32) == spot_y
        nearby = iota((cy, 3 * perfs), 0)
        source = iota((cy, 3 * perfs), 1)
        kept = jnp.where(
            source < 2 * perfs, jnp.where(nearby >= cy - WIDE, 1, 0), jnp.where(nearby < WIDE, 1, 0)
        )
        hot_side = hot_of(hot_y & (kept == 1))
        inner = split_dot(spread[:, :perfs], hot_of(hot_y[:, :perfs]), NT)
        outer = split_dot(spread[:, perfs:], hot_side[:, perfs:], NT)
        both = jnp.concatenate([inner, outer], axis=1).reshape(3, cx, nz, lanes)
        for c in range(3):
            added[c].append(both[c])
    start = [-(resid[c] + jnp.concatenate(added[c], axis=0)) for c in range(3)]
    for c in range(3):
        residual_out[c] = -start[c][:cx, :, :cy]

    coefs = [extended(COEF + q) for q in range(6)]
    coefs[0] = seam_before(coefs[0])
    coefs[1] = seam_after(coefs[1])
    scaled = (start[0] + start[1] + start[2]) * extended(INV)
    steps = (last_x, next_x, last_y, next_y, last_z, next_z)
    part = scaled
    for _ in range(1, SWEEPS):
        gathered = coefs[0] * steps[0](part)
        for q in range(1, 6):
            gathered = gathered + coefs[q] * steps[q](part)
        part = scaled - gathered

    near = [step(part) for step in steps]
    near[0] = seam_before(near[0])
    near[1] = seam_after(near[1])
    near[4] = jnp.where(level > 0, near[4], 0.0)
    near[5] = jnp.where(level < nz - 1, near[5], 0.0)

    def direction(edge_of, where):
        here = where(part)
        rest = []
        for c in range(3):
            coupled = edge_of(DCOL + c) * here
            for q in range(6):
                coupled = coupled + edge_of(OFFC + 3 * q + c) * where(near[q])
            rest.append(where(start[c]) - coupled)
        solved = []
        for a in range(3):
            value = edge_of(DINV + 3 * a) * rest[0]
            value = value + edge_of(DINV + 3 * a + 1) * rest[1]
            solved.append(value + edge_of(DINV + 3 * a + 2) * rest[2])
        solved[0] = solved[0] + here
        return solved

    def edge_own(e):
        if e < DCOL:
            return dinv_ref[e]
        if e < OFFC:
            return diag_ref[e - DCOL, 0]
        return off_ref[(e - OFFC) // 3, (e - OFFC) % 3, 0]

    beside = []
    for t in range(cx + 1, cx + 1 - (-SEAM * 2 * cx // cy)):
        one, two = ya_refs[0][t], yb_refs[0][t]
        left, right = jnp.where(even, two, one), jnp.where(even, one, two)
        beside.append(jnp.where(even_lane, left, right))

    def edge_side(e):
        tile, place = divmod(2 * cx * e, cy)
        return pltpu.roll(beside[tile], cy - place, 1) if place else beside[tile]

    def gathered_side(v):
        packed = jnp.zeros((nz, cy), f32)
        for x in range(cx):
            turned = pltpu.roll(v[x, :, cy:], 2 * x + 1, 1)
            packed = jnp.where((lane >= 2 * x) & (lane < 2 * x + 2), turned, packed)
        return packed

    after, before = 1 % width, width - 1
    z_own = direction(edge_own, lambda v: v[:cx, :, :cy])
    z_side = [
        jnp.stack([pltpu.roll(v, cy - 2 * x - 1, 1) for x in range(cx)])
        for v in direction(edge_side, gathered_side)
    ]
    if layers == 1:
        z_next = z_last = direction(
            lambda e: blocks[after][edge_at + e],
            lambda v: jnp.where(at_x == 0, v[cx, :, :cy], v[total - 1, :, :cy]),
        )
    else:
        z_next = direction(
            lambda e: blocks[after][edge_at + e], lambda v: v[after * cx, :, :cy]
        )
        z_last = direction(
            lambda e: blocks[before][edge_at + EDGE + e],
            lambda v: v[before * cx + cx - 1, :, :cy],
        )
    level_own = iota((cx, nz, cy), 1)
    around = []
    for k in range(3):
        z_out[k] = z_own[k]
        ext = jnp.concatenate([z_own[k], z_side[k]], axis=2)
        around.append(
            [
                jnp.concatenate([(z_last[k] * joined[width - 1])[None], z_own[k][:-1]], axis=0),
                jnp.concatenate([z_own[k][1:], (z_next[k] * joined[0])[None]], axis=0),
                last_y(ext)[:, :, :cy],
                next_y(ext)[:, :, :cy],
                jnp.where(level_own > 0, last_z(z_own[k]), 0.0),
                jnp.where(level_own < nz - 1, next_z(z_own[k]), 0.0),
            ]
        )
    along = jnp.zeros((nz, cy), f32)
    square = jnp.zeros((nz, cy), f32)
    for c in range(3):
        mapped = diag_ref[c, 0] * z_own[0]
        for k in range(1, 3):
            mapped = mapped + diag_ref[c, k] * z_own[k]
        for q in range(6):
            for k in range(3):
                mapped = mapped + off_ref[q, c, k] * around[k][q]
        along = along + jnp.sum(mapped * start[c][:cx, :, :cy], axis=0)
        square = square + jnp.sum(mapped * mapped, axis=0)
    along = jnp.sum(along, axis=0, keepdims=True)
    square = jnp.sum(square, axis=0, keepdims=True)
    pair = jnp.where(iota((2, cy), 0) == 0, along, square)
    sums_out[...] = jnp.broadcast_to(pair[None], sums_out.shape)


def after_kernel(sums_ref, z_ref, residual_ref, update_hbm, residual_hbm, update_out, sem, sems):
    copy = pltpu.make_async_copy(residual_ref, residual_hbm, sem)
    copy.start()
    pair = jnp.sum(sums_ref[...], axis=0)
    both = jnp.sum(pair, axis=1, keepdims=True)
    step = both[0:1] / both[1:2]
    copies = []
    for c in range(3):
        update_out[c] = z_ref[c] * step[None]
        copies.append(pltpu.make_async_copy(update_out.at[c], update_hbm.at[c], sems.at[c]))
        copies[-1].start()
    for each in [copy, *copies]:
        each.wait()


def other_pair(device, count_x, count_y):
    x, y = divmod(device, count_y)
    near = y + 1 if y % 2 else y - 1
    if 0 <= near < count_y:
        return x * count_y + near
    return (x ^ 1) * count_y + y if count_x % 2 == 0 else device


def body(
    pressure,
    saturation,
    saturation_old,
    pore_volume,
    permeability,
    jac_diag,
    jac_off,
    perf_cell,
    perf_well,
    perf_index,
    well_rate,
):
    count_x, count_y = lax.axis_size("gx"), lax.axis_size("gy")
    devices = count_x * count_y
    cx, nz, cy = pressure.shape
    wells = well_rate.shape[1] * count_y
    layers = 1 if count_x == 2 else 2
    columns_at, tiles = sent_tiles(cx, layers)[-2:]
    groups = -(-SEAM * 2 * cx // cy)
    offsets = window(count_x, cx)
    width = len(offsets)
    shape = jax.ShapeDtypeStruct
    whole = pl.BlockSpec(memory_space=pltpu.VMEM)
    anywhere = pl.BlockSpec(memory_space=pltpu.HBM)
    params = pltpu.CompilerParams(vmem_limit_bytes=32 * 1024 * 1024)

    fields = (pressure, saturation, saturation_old, pore_volume, permeability, jac_diag)
    perforations = (perf_cell, perf_well, perf_index, well_rate)
    wells_part, block, own, ya, yb, dinv, diag, off = pl.pallas_call(
        functools.partial(before_kernel, count_x, count_y),
        in_specs=[anywhere] * 11,
        out_specs=[anywhere, *[whole] * 7],
        out_shape=[
            pltpu.HBM((devices, 2, wells), f32),
            shape((tiles, nz, cy), f32),
            shape((BULK * cx + 2, nz, cy), f32),
            shape((cx + 1 + groups, nz, cy), f32),
            shape((max(cx + 1 + groups, 2 * cx), nz, cy), f32),
            shape((9, cx, nz, cy), f32),
            shape(jac_diag.shape, f32),
            shape(jac_off.shape, f32),
        ],
        scratch_shapes=[
            *[pltpu.VMEM(v.shape, v.dtype) for v in fields[:5]],
            *[pltpu.VMEM(v.shape, v.dtype) for v in perforations],
            pltpu.VMEM((devices, 2, wells), f32),
            pltpu.SemaphoreType.DMA((12,)),
        ],
        compiler_params=params,
        name="before",
    )(*[pltpu.with_memory_space_constraint(v, pltpu.HBM) for v in (*fields, jac_off, *perforations)])

    pairs = [(i, i ^ 1) for i in range(count_y)]
    others = [(i, other_pair(i, count_x, count_y)) for i in range(devices)]

    def from_x(values, offset):
        return lax.ppermute(
            values, "gx", [((i + offset) % count_x, i) for i in range(count_x)]
        )

    ya_got = lax.ppermute(ya, "gy", pairs)
    yb_got = lax.ppermute(yb, ("gx", "gy"), others)
    blocks = [from_x(block, o) for o in offsets[1:]]
    wells_all = lax.all_to_all(wells_part, ("gx", "gy"), 0, 0)
    ya_all = [ya_got] + [lax.ppermute(v[columns_at:], "gy", pairs) for v in blocks]
    yb_all = [yb_got] + [from_x(yb_got, o) for o in offsets[1:]]

    residual, direction, sums = pl.pallas_call(
        functools.partial(main_kernel, count_x, count_y, tuple(offsets)),
        in_specs=[whole] * (4 + 3 * width),
        out_specs=[whole] * 3,
        out_shape=[
            shape((3, cx, nz, cy), f32),
            shape((3, cx, nz, cy), f32),
            shape((devices, 2, cy), f32),
        ],
        compiler_params=params,
        name="main",
    )(wells_all, diag, off, dinv, own, *blocks, *ya_all, *yb_all)

    sums_all = lax.all_to_all(sums, ("gx", "gy"), 0, 0)
    update, residual = pl.pallas_call(
        after_kernel,
        in_specs=[whole] * 3,
        out_specs=[anywhere] * 2,
        out_shape=[pltpu.HBM((3, cx, nz, cy), f32)] * 2,
        scratch_shapes=[
            pltpu.VMEM((3, cx, nz, cy), f32),
            pltpu.SemaphoreType.DMA,
            pltpu.SemaphoreType.DMA((3,)),
        ],
        compiler_params=params,
        name="after",
    )(sums_all, direction, residual)
    return (residual, update)


def solution(mesh):
    placed = (
        P("gx", None, "gy"),
        P(None, "gx", None, "gy"),
        P(None, "gx", None, "gy"),
        P("gx", None, "gy"),
        P("gx", None, "gy"),
        P(None, None, "gx", None, "gy"),
        P(None, None, None, "gx", None, "gy"),
        P("gx", "gy"),
        P("gx", "gy"),
        P("gx", "gy"),
        P("gx", "gy"),
    )
    return jax.shard_map(
        body,
        mesh=mesh,
        in_specs=placed,
        out_specs=(P(None, "gx", None, "gy"), P(None, "gx", None, "gy")),
        check_vma=False,
    )
```

```python
import functools

import jax
import jax.numpy as jnp
from jax import lax
from jax.experimental import pallas as pl
from jax.experimental.pallas import tpu as pltpu
from jax.sharding import PartitionSpec as P

SWEEPS = 4
WIDE = SWEEPS + 1

viscosity = (1.0, 2.0, 0.2)
vertical_ratio = 0.1
f32 = jnp.float32

PRESS, MOB, PERM, PART, INV, COEF = 0, 1, 4, 5, 8, 9
BULK = 15
FACE = 5
DINV, DCOL, OFFC, EPART, EPRESS, EPERM, EWATER, EGAS = 0, 9, 12, 30, 33, 34, 35, 36
EDGE = 37
SEAM = 30
BORDER_AT = (BULK * WIDE + 1) // 2 * 2
SUM, INNER = 7, 8
TINY = 1e-30
NT = (((1,), (1,)), ((), ()))
NN = (((1,), (0,)), ((), ()))


def iota(shape, axis):
    return lax.broadcasted_iota(jnp.int32, shape, axis)


def split_dot(values, hot, dims):
    rows = values.shape[0]
    high = values.astype(jnp.bfloat16)
    rest = values - high.astype(f32)
    mid = rest.astype(jnp.bfloat16)
    low = (rest - mid.astype(f32)).astype(jnp.bfloat16)
    parts = jnp.concatenate([high, mid, low], axis=0)
    out = lax.dot_general(parts, hot, dims, preferred_element_type=f32)
    return out[:rows] + (out[rows : 2 * rows] + out[2 * rows :])


def hot_of(condition):
    return jnp.where(condition, 1.0, 0.0).astype(jnp.bfloat16)


def sent_tiles(cx, layers):
    edges = INNER * (cx - layers)
    borders = edges + EDGE * layers
    return edges, borders, borders + 1, borders + 2, borders + 3 + cx


def mobilities(water, gas):
    oil = 1.0 - water - gas
    return [
        water * water / viscosity[0],
        oil * oil / viscosity[1],
        gas * gas / viscosity[2],
    ]


def face_flows(here, there, weight):
    conduct = weight * here[PERM] * there[PERM] / (here[PERM] + there[PERM] + TINY)
    drop = here[PRESS] - there[PRESS]
    flow = conduct * drop
    return [
        flow * jnp.where(drop >= 0.0, here[MOB + c], there[MOB + c]) for c in range(3)
    ]


def window(count, cx):
    reach = -(-WIDE // cx)
    if count <= 2 * reach + 1:
        return list(range(count))
    return list(range(reach + 1)) + list(range(-reach, 0))


def before_kernel(
    count_x,
    count_y,
    *refs,
):
    sources, (wells_hbm, block_out, own_out, ya_out, yb_out, dinv_out) = refs[:11], refs[11:17]
    diag_ref, off_ref = refs[17:19]
    press_ref, sat_ref, old_ref, pore_ref, perm_ref = refs[19:24]
    cell_ref, well_ref, index_ref, rate_ref, wells_out, sems = refs[24:]
    targets = (*refs[19:24], diag_ref, off_ref, *refs[24:28])
    copies = []
    for i in (1, 0, 7, 9, 8, 10, 4, 2, 3, 5, 6):
        copies.append(pltpu.make_async_copy(sources[i], targets[i], sems.at[i]))
        copies[-1].start()
    for copy in copies[:6]:
        copy.wait()
    cx, nz, cy = press_ref.shape
    at_x = lax.axis_index("gx")
    at_y = lax.axis_index("gy")
    layers = 1 if count_x == 2 else 2
    edge_at, border_at, last, columns_at, _ = sent_tiles(cx, layers)

    press = press_ref[...]
    water, gas = sat_ref[0], sat_ref[1]
    mobile = mobilities(water, gas)

    cells = cell_ref[...]
    perfs = cells.shape[1]
    spot_xz = lax.div(cells, cy)
    spot_y = lax.rem(cells, cy)
    stacked = jnp.concatenate([m.reshape(cx * nz, cy) for m in mobile + [press]], axis=0)
    hot_y = hot_of(iota((cy, perfs), 0) == spot_y)
    picked = split_dot(stacked, hot_y, NN).reshape(4, cx * nz, perfs)
    on_xz = iota((cx * nz, perfs), 0) == spot_xz
    at_perf = [
        jnp.sum(jnp.where(on_xz, picked[i], 0.0), axis=0, keepdims=True) for i in range(4)
    ]
    index_vals = index_ref[...]
    parts = [index_vals * at_perf[i] for i in range(3)]
    strength = index_vals * (at_perf[0] + at_perf[1] + at_perf[2])
    weighted = strength * at_perf[3]
    row = iota((16, perfs), 0)
    both = jnp.where(row == 0, strength, jnp.where(row == 1, weighted, 0.0))
    wells = wells_out.shape[2]
    sums = split_dot(both, hot_of(iota((wells, perfs), 0) == well_ref[...]), NT)
    owned = rate_ref.shape[1]
    square = jnp.broadcast_to(rate_ref[...], (owned, owned))
    column = jnp.sum(
        jnp.where(iota((owned, owned), 0) == iota((owned, owned), 1), square, 0.0),
        axis=1,
        keepdims=True,
    )
    mine = iota((owned, wells), 1) == at_y * owned + iota((owned, wells), 0)
    rates = jnp.sum(jnp.where(mine, column, 0.0), axis=0, keepdims=True)
    pair = sums[:2] - jnp.where(iota((2, wells), 0) == 1, rates, 0.0)
    wells_out[...] = jnp.broadcast_to(pair[None], wells_out.shape)
    wells_copy = pltpu.make_async_copy(wells_out, wells_hbm, sems.at[11])
    wells_copy.start()

    perf_rows = [
        spot_xz.astype(f32),
        spot_y.astype(f32),
        well_ref[...].astype(f32),
        *parts,
        at_perf[3],
        jnp.zeros_like(at_perf[3]),
    ]
    for r, values in enumerate(perf_rows):
        block_out[last, r : r + 1, :] = values
        block_out[columns_at + cx, r : r + 1, :] = values
        own_out[BULK * cx, r : r + 1, :] = values
        ya_out[cx, r : r + 1, :] = values
        yb_out[cx, r : r + 1, :] = values

    for copy in copies[6:9]:
        copy.wait()
    perm = perm_ref[...]
    old_water, old_gas = old_ref[0], old_ref[1]
    oil, old_oil = 1.0 - water - gas, 1.0 - old_water - old_gas
    pore = pore_ref[...]
    part = [pore * (water - old_water), pore * (oil - old_oil), pore * (gas - old_gas)]
    layer_at = iota((cx, nz, cy), 1)
    lane_at = iota((cx, nz, cy), 2)
    cells_here = [press, *mobile, perm]
    flows = face_flows([v[:-1] for v in cells_here], [v[1:] for v in cells_here], 2.0)
    none = jnp.zeros((1, nz, cy), f32)
    for c in range(3):
        part[c] = part[c] + jnp.concatenate([flows[c], none], axis=0)
        part[c] = part[c] - jnp.concatenate([none, flows[c]], axis=0)
    for axis, weight, inside in (
        (2, 2.0, lane_at < cy - 1),
        (1, 2.0 * vertical_ratio, layer_at < nz - 1),
    ):
        size = cells_here[0].shape[axis]
        flows = face_flows(
            cells_here, [pltpu.roll(v, size - 1, axis) for v in cells_here], weight
        )
        for c in range(3):
            flow = jnp.where(inside, flows[c], 0.0)
            part[c] = part[c] + flow - pltpu.roll(flow, 1, axis)

    lane = iota((nz, cy), 1)
    to_left = [jnp.zeros((nz, cy), f32) for _ in range(cx)]
    to_right = [jnp.zeros((nz, cy), f32) for _ in range(cx)]
    beside = [jnp.zeros((nz, cy), f32) for _ in range(0, SEAM, cy // (2 * cx))]

    def put_bulk(f, values):
        own_out[f * cx : (f + 1) * cx] = values
        shift = f * WIDE
        on_left = (lane >= shift) & (lane < shift + WIDE)
        start = (shift - WIDE) % cy
        on_right = (lane >= start) & (lane < start + WIDE)
        for x in range(cx):
            turned = pltpu.roll(values[x], shift, 1) if shift else values[x]
            to_left[x] = jnp.where(on_left, turned, to_left[x])
            to_right[x] = jnp.where(on_right, turned, to_right[x])

    def put_edge(e, values):
        if layers == 1:
            block_out[edge_at + e] = jnp.where(at_x == 0, values[cx - 1], values[0])
        else:
            block_out[edge_at + e] = values[0]
            block_out[edge_at + EDGE + e] = values[cx - 1]
        if e < SEAM:
            group, place = divmod(e, cy // (2 * cx))
            for x in range(cx):
                at = 2 * (place * cx + x) + 1
                here = (lane == at - 1) | (lane == at)
                beside[group] = jnp.where(here, pltpu.roll(values[x], at, 1), beside[group])

    def put_inner(i, values):
        for x in range(cx - layers):
            at = i * (cx - layers) + x
            if layers == 1:
                block_out[at] = jnp.where(at_x == 0, values[x], values[x + 1])
            else:
                block_out[at] = values[x + 1]

    border = jnp.zeros((nz, cy), f32)
    for f in range(FACE):
        for x in range(cx):
            at = BORDER_AT + 2 * (f * cx + x) + 1
            first = pltpu.roll(cells_here[f][x], at - 1, 1)
            second = pltpu.roll(cells_here[f][x], at + 1, 1)
            border = jnp.where(lane == at - 1, first, jnp.where(lane == at, second, border))
    block_out[border_at] = border
    own_out[BULK * cx + 1] = border
    to_left[0] = to_right[0] = border
    for f, values in enumerate([*cells_here, *part]):
        put_bulk(f, values)
    for e, values in enumerate([*part, press, perm, water, gas]):
        put_edge(EPART + e, values)
    put_inner(SUM, part[0] + part[1] + part[2])

    copies[9].wait()
    diag = [[diag_ref[a, b] for b in range(3)] for a in range(3)]
    inverse = 1.0 / (diag[0][0] + diag[1][0] + diag[2][0])
    put_bulk(INV, inverse)
    put_inner(6, inverse)

    def cofactor(a, b):
        return (
            diag[(a + 1) % 3][(b + 1) % 3] * diag[(a + 2) % 3][(b + 2) % 3]
            - diag[(a + 1) % 3][(b + 2) % 3] * diag[(a + 2) % 3][(b + 1) % 3]
        )

    cofactors = [[cofactor(a, b) for b in range(3)] for a in range(3)]
    over = 1.0 / (
        diag[0][0] * cofactors[0][0] + diag[0][1] * cofactors[0][1] + diag[0][2] * cofactors[0][2]
    )
    for a in range(3):
        put_edge(DCOL + a, diag[a][0])
        for b in range(3):
            solve = cofactors[b][a] * over
            dinv_out[3 * a + b] = solve
            put_edge(DINV + 3 * a + b, solve)

    copies[10].wait()
    for q in range(6):
        columns = [off_ref[q, c, 0] for c in range(3)]
        if q == 4:
            columns = [jnp.where(layer_at > 0, v, 0.0) for v in columns]
        if q == 5:
            columns = [jnp.where(layer_at < nz - 1, v, 0.0) for v in columns]
        coef = (columns[0] + columns[1] + columns[2]) * inverse
        put_bulk(COEF + q, coef)
        put_inner(q, coef)
        for c in range(3):
            put_edge(OFFC + 3 * q + c, columns[c])

    even = lax.rem(at_y, 2) == 0
    for x in range(cx):
        ya_out[x] = jnp.where(even, to_right[x], to_left[x])
        yb_out[x] = jnp.where(even, to_left[x], to_right[x])
        block_out[columns_at + x] = ya_out[x]
    for t, values in enumerate(beside):
        ya_out[cx + 1 + t] = values
        yb_out[cx + 1 + t] = values
    for spare in range(cx + 1 + len(beside), yb_out.shape[0]):
        yb_out[spare] = jnp.zeros((nz, cy), f32)
    wells_copy.wait()


def main_kernel(count_x, count_y, offsets, *refs):
    width = len(offsets)
    (wells_ref, diag_ref, off_ref, dinv_ref, own_ref), refs = refs[:5], refs[5:]
    blocks, refs = (None, *refs[: width - 1]), refs[width - 1 :]
    ya_refs, refs = refs[:width], refs[width:]
    yb_refs, refs = refs[:width], refs[width:]
    residual_out, z_out, sums_out = refs

    cx, nz, cy = residual_out.shape[1:]
    total = width * cx
    at_x = lax.axis_index("gx")
    at_y = lax.axis_index("gy")
    even = lax.rem(at_y, 2) == 0
    has_left = jnp.where(at_y > 0, 1.0, 0.0).astype(f32)
    has_right = jnp.where(at_y < count_y - 1, 1.0, 0.0).astype(f32)
    layers = 1 if count_x == 2 else 2
    edge_at, border_at, last, columns_at, _ = sent_tiles(cx, layers)
    index_x = [lax.rem(at_x + (o % count_x), count_x) for o in offsets]
    joined = [
        jnp.where(index_x[(j + 1) % width] == index_x[j] + 1, 1.0, 0.0).astype(f32)
        for j in range(width)
    ]

    from_left, from_right = [], []
    for j in range(width):
        first, second = ya_refs[j][: cx + 1], yb_refs[j][: cx + 1]
        from_right.append(jnp.where(even, first, second) * has_right)
        from_left.append(jnp.where(even, second, first) * has_left)
    lane = iota((nz, cy), 1)

    merged = []
    for parity in range(2):
        of_right = lane < 0
        for f in range(parity, BULK, 2):
            of_right = of_right | ((lane >= f * WIDE) & (lane < (f + 1) * WIDE))
        merged.append(
            [
                jnp.where(of_right, from_right[j][x], from_left[j][x])
                for j in range(width)
                for x in range(cx)
            ]
        )

    def halo(f, x):
        tile = merged[f % 2][x]
        return pltpu.roll(tile, cy - f * WIDE, 1) if f else tile

    def arranged(edges, inner):
        if layers == 2:
            return jnp.stack([edges[0], *inner, edges[1]])
        first = [edges[0], *inner]
        second = [*inner, edges[0]]
        return jnp.stack([jnp.where(at_x == 0, a, b) for a, b in zip(first, second)])

    def received(j):
        block = blocks[j]
        edges = [
            [block[edge_at + side * EDGE + e] for e in range(EDGE)] for side in range(layers)
        ]
        inner = [
            [block[i * (cx - layers) + x] for x in range(cx - layers)] for i in range(INNER)
        ]
        zero = jnp.zeros((nz, cy), f32)
        part = [
            arranged(
                [edge[EPART + c] for edge in edges], inner[SUM] if c == 0 else [zero] * (cx - layers)
            )
            for c in range(3)
        ]
        scale = [1.0 / (edge[DCOL] + edge[DCOL + 1] + edge[DCOL + 2]) for edge in edges]
        coefs = [
            arranged(
                [
                    (edge[OFFC + 3 * q] + edge[OFFC + 3 * q + 1] + edge[OFFC + 3 * q + 2]) * by
                    for edge, by in zip(edges, scale)
                ],
                inner[q],
            )
            for q in range(6)
        ]
        return dict(enumerate([*part, arranged(scale, inner[6]), *coefs], start=PART))

    others = [received(j) for j in range(1, width)]

    def extended(f):
        own = jnp.concatenate(
            [own_ref[f * cx : (f + 1) * cx], *[other[f] for other in others]], axis=0
        )
        side = jnp.stack([halo(f, x) for x in range(total)])
        return jnp.concatenate([own, side], axis=2)

    lanes = 2 * cy
    level = iota((total, nz, lanes), 1)

    def next_x(v):
        return jnp.concatenate([v[1:], v[:1]], axis=0)

    def last_x(v):
        return jnp.concatenate([v[-1:], v[:-1]], axis=0)

    def next_y(v):
        return pltpu.roll(v, v.shape[2] - 1, 2)

    def last_y(v):
        return pltpu.roll(v, 1, 2)

    def next_z(v):
        return pltpu.roll(v, nz - 1, 1)

    def last_z(v):
        return pltpu.roll(v, 1, 1)

    def seam_after(v):
        rows = [v[i] for i in range(total)]
        for j in range(width):
            rows[j * cx + cx - 1] = rows[j * cx + cx - 1] * joined[j]
        return jnp.stack(rows)

    def seam_before(v):
        rows = [v[i] for i in range(total)]
        for j in range(width):
            at = ((j + 1) % width) * cx
            rows[at] = rows[at] * joined[j]
        return jnp.stack(rows)

    resid = [extended(PART + c) for c in range(3)]
    rows = [[resid[c][x] for x in range(total)] for c in range(3)]
    sides = {}

    def side_of(f, x):
        if (f, x) not in sides:
            sides[f, x] = halo(f, x)
        return sides[f, x]

    even_lane = lane % 2 == 0
    ends = (lane == 0) | (lane == cy - 1)
    for j in range(width):
        border = blocks[j][border_at] if j else own_ref[BULK * cx + 1]
        beyond = jnp.where(
            even_lane, pltpu.roll(from_left[j][0], cy - 1, 1), pltpu.roll(from_right[j][0], 1, 1)
        )
        backs = [cy - BORDER_AT - 2 * f * cx for f in range(FACE)]
        flows = face_flows(
            [pltpu.roll(beyond, back, 1) for back in backs],
            [pltpu.roll(border, back, 1) for back in backs],
            2.0,
        )
        for c in range(3):
            flow = jnp.where(lane < 2 * cx, flows[c], 0.0)
            swapped = jnp.where(even_lane, pltpu.roll(flow, cy - 1, 1), pltpu.roll(flow, 1, 1))
            for x in range(cx):
                back = cy - 2 * x - 1
                inward = jnp.where(ends, pltpu.roll(swapped, back, 1), 0.0)
                outward = jnp.where(ends, pltpu.roll(flow, back, 1), 0.0)
                at = j * cx + x
                rows[c][at] = rows[c][at] + jnp.concatenate([-inward, outward], axis=1)

    def edge_cells(j, last_layer):
        x = cx - 1 if last_layer else 0
        if j == 0:
            inside = [own_ref[f * cx + x] for f in range(FACE)]
        else:
            at = edge_at + (EDGE if last_layer and layers == 2 else 0)
            water, gas = blocks[j][at + EWATER], blocks[j][at + EGAS]
            inside = [
                blocks[j][at + EPRESS],
                *mobilities(water, gas),
                blocks[j][at + EPERM],
            ]
        return [
            jnp.concatenate([inside[f], side_of(f, j * cx + x)], axis=1) for f in range(FACE)
        ]

    for j in range(width):
        after = (j + 1) % width
        flows = face_flows(edge_cells(j, True), edge_cells(after, False), 2.0 * joined[j])
        for c in range(3):
            near_x, far_x = j * cx + cx - 1, after * cx
            rows[c][near_x] = rows[c][near_x] + flows[c]
            rows[c][far_x] = rows[c][far_x] - flows[c]
    resid = [jnp.stack(rows[c]) for c in range(3)]

    wells = wells_ref.shape[2]
    perfs = own_ref.shape[2]
    added = [[] for _ in range(3)]
    for j in range(width):
        pair = jnp.sum(wells_ref[pl.ds(index_x[j] * count_y, count_y)], axis=0)
        hole = pair[1:2] / pair[0:1]
        tiles = jnp.concatenate(
            [
                blocks[j][last] if j else own_ref[BULK * cx],
                from_left[j][cx],
                from_right[j][cx],
            ],
            axis=1,
        )
        spot_xz, spot_y, well = tiles[0:1], tiles[1:2], tiles[2:3]
        member = hot_of(iota((wells, 3 * perfs), 0).astype(f32) == well)
        hole_at = split_dot(jnp.broadcast_to(hole, (16, wells)), member, NN)[0:1]
        fall = tiles[6:7] - hole_at
        on_xz = iota((cx * nz, 3 * perfs), 0).astype(f32) == spot_xz
        spread = jnp.concatenate(
            [jnp.where(on_xz, tiles[3 + c : 4 + c] * fall, 0.0) for c in range(3)], axis=0
        )
        hot_y = iota((cy, 3 * perfs), 0).astype(f32) == spot_y
        nearby = iota((cy, 3 * perfs), 0)
        source = iota((cy, 3 * perfs), 1)
        kept = jnp.where(
            source < 2 * perfs, jnp.where(nearby >= cy - WIDE, 1, 0), jnp.where(nearby < WIDE, 1, 0)
        )
        hot_side = hot_of(hot_y & (kept == 1))
        inner = split_dot(spread[:, :perfs], hot_of(hot_y[:, :perfs]), NT)
        outer = split_dot(spread[:, perfs:], hot_side[:, perfs:], NT)
        both = jnp.concatenate([inner, outer], axis=1).reshape(3, cx, nz, lanes)
        for c in range(3):
            added[c].append(both[c])
    start = [-(resid[c] + jnp.concatenate(added[c], axis=0)) for c in range(3)]
    for c in range(3):
        residual_out[c] = -start[c][:cx, :, :cy]

    coefs = [extended(COEF + q) for q in range(6)]
    coefs[0] = seam_before(coefs[0])
    coefs[1] = seam_after(coefs[1])
    scaled = (start[0] + start[1] + start[2]) * extended(INV)
    steps = (last_x, next_x, last_y, next_y, last_z, next_z)
    part = scaled
    for _ in range(1, SWEEPS):
        gathered = coefs[0] * steps[0](part)
        for q in range(1, 6):
            gathered = gathered + coefs[q] * steps[q](part)
        part = scaled - gathered

    near = [step(part) for step in steps]
    near[0] = seam_before(near[0])
    near[1] = seam_after(near[1])
    near[4] = jnp.where(level > 0, near[4], 0.0)
    near[5] = jnp.where(level < nz - 1, near[5], 0.0)

    def direction(edge_of, where):
        here = where(part)
        rest = []
        for c in range(3):
            coupled = edge_of(DCOL + c) * here
            for q in range(6):
                coupled = coupled + edge_of(OFFC + 3 * q + c) * where(near[q])
            rest.append(where(start[c]) - coupled)
        solved = []
        for a in range(3):
            value = edge_of(DINV + 3 * a) * rest[0]
            value = value + edge_of(DINV + 3 * a + 1) * rest[1]
            solved.append(value + edge_of(DINV + 3 * a + 2) * rest[2])
        solved[0] = solved[0] + here
        return solved

    def edge_own(e):
        if e < DCOL:
            return dinv_ref[e]
        if e < OFFC:
            return diag_ref[e - DCOL, 0]
        return off_ref[(e - OFFC) // 3, (e - OFFC) % 3, 0]

    beside = []
    for t in range(cx + 1, cx + 1 - (-SEAM * 2 * cx // cy)):
        one, two = ya_refs[0][t], yb_refs[0][t]
        left, right = jnp.where(even, two, one), jnp.where(even, one, two)
        beside.append(jnp.where(even_lane, left, right))

    def edge_side(e):
        tile, place = divmod(2 * cx * e, cy)
        return pltpu.roll(beside[tile], cy - place, 1) if place else beside[tile]

    def gathered_side(v):
        packed = jnp.zeros((nz, cy), f32)
        for x in range(cx):
            turned = pltpu.roll(v[x, :, cy:], 2 * x + 1, 1)
            packed = jnp.where((lane >= 2 * x) & (lane < 2 * x + 2), turned, packed)
        return packed

    after, before = 1 % width, width - 1
    z_own = direction(edge_own, lambda v: v[:cx, :, :cy])
    z_side = [
        jnp.stack([pltpu.roll(v, cy - 2 * x - 1, 1) for x in range(cx)])
        for v in direction(edge_side, gathered_side)
    ]
    if layers == 1:
        z_next = z_last = direction(
            lambda e: blocks[after][edge_at + e],
            lambda v: jnp.where(at_x == 0, v[cx, :, :cy], v[total - 1, :, :cy]),
        )
    else:
        z_next = direction(
            lambda e: blocks[after][edge_at + e], lambda v: v[after * cx, :, :cy]
        )
        z_last = direction(
            lambda e: blocks[before][edge_at + EDGE + e],
            lambda v: v[before * cx + cx - 1, :, :cy],
        )
    level_own = iota((cx, nz, cy), 1)
    around = []
    for k in range(3):
        z_out[k] = z_own[k]
        ext = jnp.concatenate([z_own[k], z_side[k]], axis=2)
        around.append(
            [
                jnp.concatenate([(z_last[k] * joined[width - 1])[None], z_own[k][:-1]], axis=0),
                jnp.concatenate([z_own[k][1:], (z_next[k] * joined[0])[None]], axis=0),
                last_y(ext)[:, :, :cy],
                next_y(ext)[:, :, :cy],
                jnp.where(level_own > 0, last_z(z_own[k]), 0.0),
                jnp.where(level_own < nz - 1, next_z(z_own[k]), 0.0),
            ]
        )
    along = jnp.zeros((nz, cy), f32)
    square = jnp.zeros((nz, cy), f32)
    for c in range(3):
        mapped = diag_ref[c, 0] * z_own[0]
        for k in range(1, 3):
            mapped = mapped + diag_ref[c, k] * z_own[k]
        for q in range(6):
            for k in range(3):
                mapped = mapped + off_ref[q, c, k] * around[k][q]
        along = along + jnp.sum(mapped * start[c][:cx, :, :cy], axis=0)
        square = square + jnp.sum(mapped * mapped, axis=0)
    along = jnp.sum(along, axis=0, keepdims=True)
    square = jnp.sum(square, axis=0, keepdims=True)
    pair = jnp.where(iota((2, cy), 0) == 0, along, square)
    sums_out[...] = jnp.broadcast_to(pair[None], sums_out.shape)


def after_kernel(sums_ref, z_ref, residual_ref, update_hbm, residual_hbm, update_out, sem, sems):
    copy = pltpu.make_async_copy(residual_ref, residual_hbm, sem)
    copy.start()
    pair = jnp.sum(sums_ref[...], axis=0)
    both = jnp.sum(pair, axis=1, keepdims=True)
    step = both[0:1] / both[1:2]
    copies = []
    for c in range(3):
        update_out[c] = z_ref[c] * step[None]
        copies.append(pltpu.make_async_copy(update_out.at[c], update_hbm.at[c], sems.at[c]))
        copies[-1].start()
    for each in [copy, *copies]:
        each.wait()


def other_pair(device, count_x, count_y):
    x, y = divmod(device, count_y)
    near = y + 1 if y % 2 else y - 1
    if 0 <= near < count_y:
        return x * count_y + near
    return (x ^ 1) * count_y + y if count_x % 2 == 0 else device


def body(
    pressure,
    saturation,
    saturation_old,
    pore_volume,
    permeability,
    jac_diag,
    jac_off,
    perf_cell,
    perf_well,
    perf_index,
    well_rate,
):
    count_x, count_y = lax.axis_size("gx"), lax.axis_size("gy")
    devices = count_x * count_y
    cx, nz, cy = pressure.shape
    wells = well_rate.shape[1] * count_y
    layers = 1 if count_x == 2 else 2
    columns_at, tiles = sent_tiles(cx, layers)[-2:]
    groups = -(-SEAM * 2 * cx // cy)
    offsets = window(count_x, cx)
    width = len(offsets)
    shape = jax.ShapeDtypeStruct
    whole = pl.BlockSpec(memory_space=pltpu.VMEM)
    anywhere = pl.BlockSpec(memory_space=pltpu.HBM)
    params = pltpu.CompilerParams(vmem_limit_bytes=32 * 1024 * 1024)

    fields = (pressure, saturation, saturation_old, pore_volume, permeability, jac_diag)
    perforations = (perf_cell, perf_well, perf_index, well_rate)
    wells_part, block, own, ya, yb, dinv, diag, off = pl.pallas_call(
        functools.partial(before_kernel, count_x, count_y),
        in_specs=[anywhere] * 11,
        out_specs=[anywhere, *[whole] * 7],
        out_shape=[
            pltpu.HBM((devices, 2, wells), f32),
            shape((tiles, nz, cy), f32),
            shape((BULK * cx + 2, nz, cy), f32),
            shape((cx + 1 + groups, nz, cy), f32),
            shape((max(cx + 1 + groups, 2 * cx), nz, cy), f32),
            shape((9, cx, nz, cy), f32),
            shape(jac_diag.shape, f32),
            shape(jac_off.shape, f32),
        ],
        scratch_shapes=[
            *[pltpu.VMEM(v.shape, v.dtype) for v in fields[:5]],
            *[pltpu.VMEM(v.shape, v.dtype) for v in perforations],
            pltpu.VMEM((devices, 2, wells), f32),
            pltpu.SemaphoreType.DMA((12,)),
        ],
        compiler_params=params,
        name="before",
    )(*[pltpu.with_memory_space_constraint(v, pltpu.HBM) for v in (*fields, jac_off, *perforations)])

    pairs = [(i, i ^ 1) for i in range(count_y)]
    others = [(i, other_pair(i, count_x, count_y)) for i in range(devices)]

    def from_x(values, offset):
        return lax.ppermute(
            values, "gx", [((i + offset) % count_x, i) for i in range(count_x)]
        )

    ya_got = lax.ppermute(ya, "gy", pairs)
    yb_got = lax.ppermute(yb, ("gx", "gy"), others)
    blocks = [from_x(block, o) for o in offsets[1:]]
    wells_all = lax.all_to_all(wells_part, ("gx", "gy"), 0, 0)
    ya_all = [ya_got] + [lax.ppermute(v[columns_at:], "gy", pairs) for v in blocks]
    yb_all = [yb_got] + [from_x(yb_got, o) for o in offsets[1:]]

    residual, direction, sums = pl.pallas_call(
        functools.partial(main_kernel, count_x, count_y, tuple(offsets)),
        in_specs=[whole] * (4 + 3 * width),
        out_specs=[whole] * 3,
        out_shape=[
            shape((3, cx, nz, cy), f32),
            shape((3, cx, nz, cy), f32),
            shape((devices, 2, cy), f32),
        ],
        compiler_params=params,
        name="main",
    )(wells_all, diag, off, dinv, own, *blocks, *ya_all, *yb_all)

    sums_all = lax.all_to_all(sums, ("gx", "gy"), 0, 0)
    update, residual = pl.pallas_call(
        after_kernel,
        in_specs=[whole] * 3,
        out_specs=[anywhere] * 2,
        out_shape=[pltpu.HBM((3, cx, nz, cy), f32)] * 2,
        scratch_shapes=[
            pltpu.VMEM((3, cx, nz, cy), f32),
            pltpu.SemaphoreType.DMA,
            pltpu.SemaphoreType.DMA((3,)),
        ],
        compiler_params=params,
        name="after",
    )(sums_all, direction, residual)
    return (residual, update)


def solution(mesh):
    placed = (
        P("gx", None, "gy"),
        P(None, "gx", None, "gy"),
        P(None, "gx", None, "gy"),
        P("gx", None, "gy"),
        P("gx", None, "gy"),
        P(None, None, "gx", None, "gy"),
        P(None, None, None, "gx", None, "gy"),
        P("gx", "gy"),
        P("gx", "gy"),
        P("gx", "gy"),
        P("gx", "gy"),
    )
    return jax.shard_map(
        body,
        mesh=mesh,
        in_specs=placed,
        out_specs=(P(None, "gx", None, "gy"), P(None, "gx", None, "gy")),
        check_vma=False,
    )
```

```python
import functools

import jax
import jax.numpy as jnp
from jax import lax
from jax.experimental import pallas as pl
from jax.experimental.pallas import tpu as pltpu
from jax.sharding import PartitionSpec as P

SWEEPS = 4
WIDE = SWEEPS + 1

viscosity = (1.0, 2.0, 0.2)
vertical_ratio = 0.1
f32 = jnp.float32

PRESS, MOB, PERM, PART, INV, COEF = 0, 1, 4, 5, 8, 9
BULK = 15
FACE = 5
DINV, DCOL, OFFC, EPART, EPRESS, EPERM, EWATER, EGAS = 0, 9, 12, 30, 33, 34, 35, 36
EDGE = 37
SEAM = 30
BORDER_AT = (BULK * WIDE + 1) // 2 * 2
SUM, INNER = 7, 8
TINY = 1e-30
NT = (((1,), (1,)), ((), ()))
NN = (((1,), (0,)), ((), ()))


def iota(shape, axis):
    return lax.broadcasted_iota(jnp.int32, shape, axis)


def split_dot(values, hot, dims):
    rows = values.shape[0]
    high = values.astype(jnp.bfloat16)
    rest = values - high.astype(f32)
    mid = rest.astype(jnp.bfloat16)
    low = (rest - mid.astype(f32)).astype(jnp.bfloat16)
    parts = jnp.concatenate([high, mid, low], axis=0)
    out = lax.dot_general(parts, hot, dims, preferred_element_type=f32)
    return out[:rows] + (out[rows : 2 * rows] + out[2 * rows :])


def hot_of(condition):
    return jnp.where(condition, 1.0, 0.0).astype(jnp.bfloat16)


def sent_tiles(cx, layers):
    edges = INNER * (cx - layers)
    borders = edges + EDGE * layers
    return edges, borders, borders + 1, borders + 2, borders + 3 + cx


def mobilities(water, gas):
    oil = 1.0 - water - gas
    return [
        water * water / viscosity[0],
        oil * oil / viscosity[1],
        gas * gas / viscosity[2],
    ]


def face_flows(here, there, weight):
    conduct = weight * here[PERM] * there[PERM] / (here[PERM] + there[PERM] + TINY)
    drop = here[PRESS] - there[PRESS]
    flow = conduct * drop
    return [
        flow * jnp.where(drop >= 0.0, here[MOB + c], there[MOB + c]) for c in range(3)
    ]


def window(count, cx):
    reach = -(-WIDE // cx)
    if count <= 2 * reach + 1:
        return list(range(count))
    return list(range(reach + 1)) + list(range(-reach, 0))


def before_kernel(
    count_x,
    count_y,
    *refs,
):
    sources, (wells_hbm, block_out, own_out, ya_out, yb_out, dinv_out) = refs[:11], refs[11:17]
    diag_ref, off_ref = refs[17:19]
    press_ref, sat_ref, old_ref, pore_ref, perm_ref = refs[19:24]
    cell_ref, well_ref, index_ref, rate_ref, wells_out, sems = refs[24:]
    targets = (*refs[19:24], diag_ref, off_ref, *refs[24:28])
    copies = []
    for i in (1, 0, 7, 9, 8, 10, 4, 2, 3, 5, 6):
        copies.append(pltpu.make_async_copy(sources[i], targets[i], sems.at[i]))
        copies[-1].start()
    for copy in copies[:6]:
        copy.wait()
    cx, nz, cy = press_ref.shape
    at_x = lax.axis_index("gx")
    at_y = lax.axis_index("gy")
    layers = 1 if count_x == 2 else 2
    edge_at, border_at, last, columns_at, _ = sent_tiles(cx, layers)

    press = press_ref[...]
    water, gas = sat_ref[0], sat_ref[1]
    mobile = mobilities(water, gas)

    cells = cell_ref[...]
    perfs = cells.shape[1]
    spot_xz = lax.div(cells, cy)
    spot_y = lax.rem(cells, cy)
    stacked = jnp.concatenate([m.reshape(cx * nz, cy) for m in mobile + [press]], axis=0)
    hot_y = hot_of(iota((cy, perfs), 0) == spot_y)
    picked = split_dot(stacked, hot_y, NN).reshape(4, cx * nz, perfs)
    on_xz = iota((cx * nz, perfs), 0) == spot_xz
    at_perf = [
        jnp.sum(jnp.where(on_xz, picked[i], 0.0), axis=0, keepdims=True) for i in range(4)
    ]
    index_vals = index_ref[...]
    parts = [index_vals * at_perf[i] for i in range(3)]
    strength = index_vals * (at_perf[0] + at_perf[1] + at_perf[2])
    weighted = strength * at_perf[3]
    row = iota((16, perfs), 0)
    both = jnp.where(row == 0, strength, jnp.where(row == 1, weighted, 0.0))
    wells = wells_out.shape[2]
    sums = split_dot(both, hot_of(iota((wells, perfs), 0) == well_ref[...]), NT)
    owned = rate_ref.shape[1]
    square = jnp.broadcast_to(rate_ref[...], (owned, owned))
    column = jnp.sum(
        jnp.where(iota((owned, owned), 0) == iota((owned, owned), 1), square, 0.0),
        axis=1,
        keepdims=True,
    )
    mine = iota((owned, wells), 1) == at_y * owned + iota((owned, wells), 0)
    rates = jnp.sum(jnp.where(mine, column, 0.0), axis=0, keepdims=True)
    pair = sums[:2] - jnp.where(iota((2, wells), 0) == 1, rates, 0.0)
    wells_out[...] = jnp.broadcast_to(pair[None], wells_out.shape)
    wells_copy = pltpu.make_async_copy(wells_out, wells_hbm, sems.at[11])
    wells_copy.start()

    perf_rows = [
        spot_xz.astype(f32),
        spot_y.astype(f32),
        well_ref[...].astype(f32),
        *parts,
        at_perf[3],
        jnp.zeros_like(at_perf[3]),
    ]
    for r, values in enumerate(perf_rows):
        block_out[last, r : r + 1, :] = values
        block_out[columns_at + cx, r : r + 1, :] = values
        own_out[BULK * cx, r : r + 1, :] = values
        ya_out[cx, r : r + 1, :] = values
        yb_out[cx, r : r + 1, :] = values

    for copy in copies[6:9]:
        copy.wait()
    perm = perm_ref[...]
    old_water, old_gas = old_ref[0], old_ref[1]
    oil, old_oil = 1.0 - water - gas, 1.0 - old_water - old_gas
    pore = pore_ref[...]
    part = [pore * (water - old_water), pore * (oil - old_oil), pore * (gas - old_gas)]
    layer_at = iota((cx, nz, cy), 1)
    lane_at = iota((cx, nz, cy), 2)
    cells_here = [press, *mobile, perm]
    flows = face_flows([v[:-1] for v in cells_here], [v[1:] for v in cells_here], 2.0)
    none = jnp.zeros((1, nz, cy), f32)
    for c in range(3):
        part[c] = part[c] + jnp.concatenate([flows[c], none], axis=0)
        part[c] = part[c] - jnp.concatenate([none, flows[c]], axis=0)
    for axis, weight, inside in (
        (2, 2.0, lane_at < cy - 1),
        (1, 2.0 * vertical_ratio, layer_at < nz - 1),
    ):
        size = cells_here[0].shape[axis]
        flows = face_flows(
            cells_here, [pltpu.roll(v, size - 1, axis) for v in cells_here], weight
        )
        for c in range(3):
            flow = jnp.where(inside, flows[c], 0.0)
            part[c] = part[c] + flow - pltpu.roll(flow, 1, axis)

    lane = iota((nz, cy), 1)
    to_left = [jnp.zeros((nz, cy), f32) for _ in range(cx)]
    to_right = [jnp.zeros((nz, cy), f32) for _ in range(cx)]
    beside = [jnp.zeros((nz, cy), f32) for _ in range(0, SEAM, cy // (2 * cx))]

    def put_bulk(f, values):
        own_out[f * cx : (f + 1) * cx] = values
        shift = f * WIDE
        on_left = (lane >= shift) & (lane < shift + WIDE)
        start = (shift - WIDE) % cy
        on_right = (lane >= start) & (lane < start + WIDE)
        for x in range(cx):
            turned = pltpu.roll(values[x], shift, 1) if shift else values[x]
            to_left[x] = jnp.where(on_left, turned, to_left[x])
            to_right[x] = jnp.where(on_right, turned, to_right[x])

    def put_edge(e, values):
        if layers == 1:
            block_out[edge_at + e] = jnp.where(at_x == 0, values[cx - 1], values[0])
        else:
            block_out[edge_at + e] = values[0]
            block_out[edge_at + EDGE + e] = values[cx - 1]
        if e < SEAM:
            group, place = divmod(e, cy // (2 * cx))
            for x in range(cx):
                at = 2 * (place * cx + x) + 1
                here = (lane == at - 1) | (lane == at)
                beside[group] = jnp.where(here, pltpu.roll(values[x], at, 1), beside[group])

    def put_inner(i, values):
        for x in range(cx - layers):
            at = i * (cx - layers) + x
            if layers == 1:
                block_out[at] = jnp.where(at_x == 0, values[x], values[x + 1])
            else:
                block_out[at] = values[x + 1]

    border = jnp.zeros((nz, cy), f32)
    for f in range(FACE):
        for x in range(cx):
            at = BORDER_AT + 2 * (f * cx + x) + 1
            first = pltpu.roll(cells_here[f][x], at - 1, 1)
            second = pltpu.roll(cells_here[f][x], at + 1, 1)
            border = jnp.where(lane == at - 1, first, jnp.where(lane == at, second, border))
    block_out[border_at] = border
    own_out[BULK * cx + 1] = border
    to_left[0] = to_right[0] = border
    for f, values in enumerate([*cells_here, *part]):
        put_bulk(f, values)
    for e, values in enumerate([*part, press, perm, water, gas]):
        put_edge(EPART + e, values)
    put_inner(SUM, part[0] + part[1] + part[2])

    copies[9].wait()
    diag = [[diag_ref[a, b] for b in range(3)] for a in range(3)]
    inverse = 1.0 / (diag[0][0] + diag[1][0] + diag[2][0])
    put_bulk(INV, inverse)
    put_inner(6, inverse)

    def cofactor(a, b):
        return (
            diag[(a + 1) % 3][(b + 1) % 3] * diag[(a + 2) % 3][(b + 2) % 3]
            - diag[(a + 1) % 3][(b + 2) % 3] * diag[(a + 2) % 3][(b + 1) % 3]
        )

    cofactors = [[cofactor(a, b) for b in range(3)] for a in range(3)]
    over = 1.0 / (
        diag[0][0] * cofactors[0][0] + diag[0][1] * cofactors[0][1] + diag[0][2] * cofactors[0][2]
    )
    for a in range(3):
        put_edge(DCOL + a, diag[a][0])
        for b in range(3):
            solve = cofactors[b][a] * over
            dinv_out[3 * a + b] = solve
            put_edge(DINV + 3 * a + b, solve)

    copies[10].wait()
    for q in range(6):
        columns = [off_ref[q, c, 0] for c in range(3)]
        if q == 4:
            columns = [jnp.where(layer_at > 0, v, 0.0) for v in columns]
        if q == 5:
            columns = [jnp.where(layer_at < nz - 1, v, 0.0) for v in columns]
        coef = (columns[0] + columns[1] + columns[2]) * inverse
        put_bulk(COEF + q, coef)
        put_inner(q, coef)
        for c in range(3):
            put_edge(OFFC + 3 * q + c, columns[c])

    even = lax.rem(at_y, 2) == 0
    for x in range(cx):
        ya_out[x] = jnp.where(even, to_right[x], to_left[x])
        yb_out[x] = jnp.where(even, to_left[x], to_right[x])
        block_out[columns_at + x] = ya_out[x]
    for t, values in enumerate(beside):
        ya_out[cx + 1 + t] = values
        yb_out[cx + 1 + t] = values
    for spare in range(cx + 1 + len(beside), yb_out.shape[0]):
        yb_out[spare] = jnp.zeros((nz, cy), f32)
    wells_copy.wait()


def main_kernel(count_x, count_y, offsets, *refs):
    width = len(offsets)
    (wells_ref, diag_ref, off_ref, dinv_ref, own_ref), refs = refs[:5], refs[5:]
    blocks, refs = (None, *refs[: width - 1]), refs[width - 1 :]
    ya_refs, refs = refs[:width], refs[width:]
    yb_refs, refs = refs[:width], refs[width:]
    residual_out, z_out, sums_out = refs

    cx, nz, cy = residual_out.shape[1:]
    total = width * cx
    at_x = lax.axis_index("gx")
    at_y = lax.axis_index("gy")
    even = lax.rem(at_y, 2) == 0
    has_left = jnp.where(at_y > 0, 1.0, 0.0).astype(f32)
    has_right = jnp.where(at_y < count_y - 1, 1.0, 0.0).astype(f32)
    layers = 1 if count_x == 2 else 2
    edge_at, border_at, last, columns_at, _ = sent_tiles(cx, layers)
    index_x = [lax.rem(at_x + (o % count_x), count_x) for o in offsets]
    joined = [
        jnp.where(index_x[(j + 1) % width] == index_x[j] + 1, 1.0, 0.0).astype(f32)
        for j in range(width)
    ]

    from_left, from_right = [], []
    for j in range(width):
        first, second = ya_refs[j][: cx + 1], yb_refs[j][: cx + 1]
        from_right.append(jnp.where(even, first, second) * has_right)
        from_left.append(jnp.where(even, second, first) * has_left)
    lane = iota((nz, cy), 1)

    merged = []
    for parity in range(2):
        of_right = lane < 0
        for f in range(parity, BULK, 2):
            of_right = of_right | ((lane >= f * WIDE) & (lane < (f + 1) * WIDE))
        merged.append(
            [
                jnp.where(of_right, from_right[j][x], from_left[j][x])
                for j in range(width)
                for x in range(cx)
            ]
        )

    def halo(f, x):
        tile = merged[f % 2][x]
        return pltpu.roll(tile, cy - f * WIDE, 1) if f else tile

    def arranged(edges, inner):
        if layers == 2:
            return jnp.stack([edges[0], *inner, edges[1]])
        first = [edges[0], *inner]
        second = [*inner, edges[0]]
        return jnp.stack([jnp.where(at_x == 0, a, b) for a, b in zip(first, second)])

    def received(j):
        block = blocks[j]
        edges = [
            [block[edge_at + side * EDGE + e] for e in range(EDGE)] for side in range(layers)
        ]
        inner = [
            [block[i * (cx - layers) + x] for x in range(cx - layers)] for i in range(INNER)
        ]
        zero = jnp.zeros((nz, cy), f32)
        part = [
            arranged(
                [edge[EPART + c] for edge in edges], inner[SUM] if c == 0 else [zero] * (cx - layers)
            )
            for c in range(3)
        ]
        scale = [1.0 / (edge[DCOL] + edge[DCOL + 1] + edge[DCOL + 2]) for edge in edges]
        coefs = [
            arranged(
                [
                    (edge[OFFC + 3 * q] + edge[OFFC + 3 * q + 1] + edge[OFFC + 3 * q + 2]) * by
                    for edge, by in zip(edges, scale)
                ],
                inner[q],
            )
            for q in range(6)
        ]
        return dict(enumerate([*part, arranged(scale, inner[6]), *coefs], start=PART))

    others = [received(j) for j in range(1, width)]

    def extended(f):
        own = jnp.concatenate(
            [own_ref[f * cx : (f + 1) * cx], *[other[f] for other in others]], axis=0
        )
        side = jnp.stack([halo(f, x) for x in range(total)])
        return jnp.concatenate([own, side], axis=2)

    lanes = 2 * cy
    level = iota((total, nz, lanes), 1)

    def next_x(v):
        return jnp.concatenate([v[1:], v[:1]], axis=0)

    def last_x(v):
        return jnp.concatenate([v[-1:], v[:-1]], axis=0)

    def next_y(v):
        return pltpu.roll(v, v.shape[2] - 1, 2)

    def last_y(v):
        return pltpu.roll(v, 1, 2)

    def next_z(v):
        return pltpu.roll(v, nz - 1, 1)

    def last_z(v):
        return pltpu.roll(v, 1, 1)

    def seam_after(v):
        rows = [v[i] for i in range(total)]
        for j in range(width):
            rows[j * cx + cx - 1] = rows[j * cx + cx - 1] * joined[j]
        return jnp.stack(rows)

    def seam_before(v):
        rows = [v[i] for i in range(total)]
        for j in range(width):
            at = ((j + 1) % width) * cx
            rows[at] = rows[at] * joined[j]
        return jnp.stack(rows)

    resid = [extended(PART + c) for c in range(3)]
    rows = [[resid[c][x] for x in range(total)] for c in range(3)]
    sides = {}

    def side_of(f, x):
        if (f, x) not in sides:
            sides[f, x] = halo(f, x)
        return sides[f, x]

    even_lane = lane % 2 == 0
    ends = (lane == 0) | (lane == cy - 1)
    for j in range(width):
        border = blocks[j][border_at] if j else own_ref[BULK * cx + 1]
        beyond = jnp.where(
            even_lane, pltpu.roll(from_left[j][0], cy - 1, 1), pltpu.roll(from_right[j][0], 1, 1)
        )
        backs = [cy - BORDER_AT - 2 * f * cx for f in range(FACE)]
        flows = face_flows(
            [pltpu.roll(beyond, back, 1) for back in backs],
            [pltpu.roll(border, back, 1) for back in backs],
            2.0,
        )
        for c in range(3):
            flow = jnp.where(lane < 2 * cx, flows[c], 0.0)
            swapped = jnp.where(even_lane, pltpu.roll(flow, cy - 1, 1), pltpu.roll(flow, 1, 1))
            for x in range(cx):
                back = cy - 2 * x - 1
                inward = jnp.where(ends, pltpu.roll(swapped, back, 1), 0.0)
                outward = jnp.where(ends, pltpu.roll(flow, back, 1), 0.0)
                at = j * cx + x
                rows[c][at] = rows[c][at] + jnp.concatenate([-inward, outward], axis=1)

    def edge_cells(j, last_layer):
        x = cx - 1 if last_layer else 0
        if j == 0:
            inside = [own_ref[f * cx + x] for f in range(FACE)]
        else:
            at = edge_at + (EDGE if last_layer and layers == 2 else 0)
            water, gas = blocks[j][at + EWATER], blocks[j][at + EGAS]
            inside = [
                blocks[j][at + EPRESS],
                *mobilities(water, gas),
                blocks[j][at + EPERM],
            ]
        return [
            jnp.concatenate([inside[f], side_of(f, j * cx + x)], axis=1) for f in range(FACE)
        ]

    for j in range(width):
        after = (j + 1) % width
        flows = face_flows(edge_cells(j, True), edge_cells(after, False), 2.0 * joined[j])
        for c in range(3):
            near_x, far_x = j * cx + cx - 1, after * cx
            rows[c][near_x] = rows[c][near_x] + flows[c]
            rows[c][far_x] = rows[c][far_x] - flows[c]
    resid = [jnp.stack(rows[c]) for c in range(3)]

    wells = wells_ref.shape[2]
    perfs = own_ref.shape[2]
    added = [[] for _ in range(3)]
    for j in range(width):
        pair = jnp.sum(wells_ref[pl.ds(index_x[j] * count_y, count_y)], axis=0)
        hole = pair[1:2] / pair[0:1]
        tiles = jnp.concatenate(
            [
                blocks[j][last] if j else own_ref[BULK * cx],
                from_left[j][cx],
                from_right[j][cx],
            ],
            axis=1,
        )
        spot_xz, spot_y, well = tiles[0:1], tiles[1:2], tiles[2:3]
        member = hot_of(iota((wells, 3 * perfs), 0).astype(f32) == well)
        hole_at = split_dot(jnp.broadcast_to(hole, (16, wells)), member, NN)[0:1]
        fall = tiles[6:7] - hole_at
        on_xz = iota((cx * nz, 3 * perfs), 0).astype(f32) == spot_xz
        spread = jnp.concatenate(
            [jnp.where(on_xz, tiles[3 + c : 4 + c] * fall, 0.0) for c in range(3)], axis=0
        )
        hot_y = iota((cy, 3 * perfs), 0).astype(f32) == spot_y
        nearby = iota((cy, 3 * perfs), 0)
        source = iota((cy, 3 * perfs), 1)
        kept = jnp.where(
            source < 2 * perfs, jnp.where(nearby >= cy - WIDE, 1, 0), jnp.where(nearby < WIDE, 1, 0)
        )
        hot_side = hot_of(hot_y & (kept == 1))
        inner = split_dot(spread[:, :perfs], hot_of(hot_y[:, :perfs]), NT)
        outer = split_dot(spread[:, perfs:], hot_side[:, perfs:], NT)
        both = jnp.concatenate([inner, outer], axis=1).reshape(3, cx, nz, lanes)
        for c in range(3):
            added[c].append(both[c])
    start = [-(resid[c] + jnp.concatenate(added[c], axis=0)) for c in range(3)]
    for c in range(3):
        residual_out[c] = -start[c][:cx, :, :cy]

    coefs = [extended(COEF + q) for q in range(6)]
    coefs[0] = seam_before(coefs[0])
    coefs[1] = seam_after(coefs[1])
    scaled = (start[0] + start[1] + start[2]) * extended(INV)
    steps = (last_x, next_x, last_y, next_y, last_z, next_z)
    part = scaled
    for _ in range(1, SWEEPS):
        along_x, along_y, along_z = (
            coefs[q] * steps[q](part) + coefs[q + 1] * steps[q + 1](part) for q in (0, 2, 4)
        )
        part = (scaled - along_x) - (along_z + along_y)

    near = [step(part) for step in steps]
    near[0] = seam_before(near[0])
    near[1] = seam_after(near[1])
    near[4] = jnp.where(level > 0, near[4], 0.0)
    near[5] = jnp.where(level < nz - 1, near[5], 0.0)

    def direction(edge_of, where):
        here = where(part)
        rest = []
        for c in range(3):
            coupled = edge_of(DCOL + c) * here
            for q in range(6):
                coupled = coupled + edge_of(OFFC + 3 * q + c) * where(near[q])
            rest.append(where(start[c]) - coupled)
        solved = []
        for a in range(3):
            value = edge_of(DINV + 3 * a) * rest[0]
            value = value + edge_of(DINV + 3 * a + 1) * rest[1]
            solved.append(value + edge_of(DINV + 3 * a + 2) * rest[2])
        solved[0] = solved[0] + here
        return solved

    def edge_own(e):
        if e < DCOL:
            return dinv_ref[e]
        if e < OFFC:
            return diag_ref[e - DCOL, 0]
        return off_ref[(e - OFFC) // 3, (e - OFFC) % 3, 0]

    beside = []
    for t in range(cx + 1, cx + 1 - (-SEAM * 2 * cx // cy)):
        one, two = ya_refs[0][t], yb_refs[0][t]
        left, right = jnp.where(even, two, one) * has_left, jnp.where(even, one, two) * has_right
        beside.append(jnp.where(even_lane, left, right))

    def edge_side(e):
        tile, place = divmod(2 * cx * e, cy)
        return pltpu.roll(beside[tile], cy - place, 1) if place else beside[tile]

    def gathered_side(v):
        packed = jnp.zeros((nz, cy), f32)
        for x in range(cx):
            turned = pltpu.roll(v[x, :, cy:], 2 * x + 1, 1)
            packed = jnp.where((lane >= 2 * x) & (lane < 2 * x + 2), turned, packed)
        return packed

    after, before = 1 % width, width - 1
    z_own = direction(edge_own, lambda v: v[:cx, :, :cy])
    z_side = [
        jnp.stack([pltpu.roll(v, cy - 2 * x - 1, 1) for x in range(cx)])
        for v in direction(edge_side, gathered_side)
    ]
    if layers == 1:
        z_next = z_last = direction(
            lambda e: blocks[after][edge_at + e],
            lambda v: jnp.where(at_x == 0, v[cx, :, :cy], v[total - 1, :, :cy]),
        )
    else:
        z_next = direction(
            lambda e: blocks[after][edge_at + e], lambda v: v[after * cx, :, :cy]
        )
        z_last = direction(
            lambda e: blocks[before][edge_at + EDGE + e],
            lambda v: v[before * cx + cx - 1, :, :cy],
        )
    level_own = iota((cx, nz, cy), 1)
    around = []
    for k in range(3):
        z_out[k] = z_own[k]
        ext = jnp.concatenate([z_own[k], z_side[k]], axis=2)
        around.append(
            [
                jnp.concatenate([(z_last[k] * joined[width - 1])[None], z_own[k][:-1]], axis=0),
                jnp.concatenate([z_own[k][1:], (z_next[k] * joined[0])[None]], axis=0),
                last_y(ext)[:, :, :cy],
                next_y(ext)[:, :, :cy],
                jnp.where(level_own > 0, last_z(z_own[k]), 0.0),
                jnp.where(level_own < nz - 1, next_z(z_own[k]), 0.0),
            ]
        )
    along = jnp.zeros((nz, cy), f32)
    square = jnp.zeros((nz, cy), f32)
    for c in range(3):
        mapped = diag_ref[c, 0] * z_own[0]
        for k in range(1, 3):
            mapped = mapped + diag_ref[c, k] * z_own[k]
        for q in range(6):
            for k in range(3):
                mapped = mapped + off_ref[q, c, k] * around[k][q]
        along = along + jnp.sum(mapped * start[c][:cx, :, :cy], axis=0)
        square = square + jnp.sum(mapped * mapped, axis=0)
    along = jnp.sum(along, axis=0, keepdims=True)
    square = jnp.sum(square, axis=0, keepdims=True)
    pair = jnp.where(iota((2, cy), 0) == 0, along, square)
    sums_out[...] = jnp.broadcast_to(pair[None], sums_out.shape)


def after_kernel(sums_ref, z_ref, residual_ref, update_hbm, residual_hbm, update_out, sem, sems):
    copy = pltpu.make_async_copy(residual_ref, residual_hbm, sem)
    copy.start()
    pair = jnp.sum(sums_ref[...], axis=0)
    both = jnp.sum(pair, axis=1, keepdims=True)
    step = both[0:1] / both[1:2]
    copies = []
    for c in range(3):
        update_out[c] = z_ref[c] * step[None]
        copies.append(pltpu.make_async_copy(update_out.at[c], update_hbm.at[c], sems.at[c]))
        copies[-1].start()
    for each in [copy, *copies]:
        each.wait()


def other_pair(device, count_x, count_y):
    x, y = divmod(device, count_y)
    near = y + 1 if y % 2 else y - 1
    if 0 <= near < count_y:
        return x * count_y + near
    return (x ^ 1) * count_y + y if count_x % 2 == 0 else device


def body(
    pressure,
    saturation,
    saturation_old,
    pore_volume,
    permeability,
    jac_diag,
    jac_off,
    perf_cell,
    perf_well,
    perf_index,
    well_rate,
):
    count_x, count_y = lax.axis_size("gx"), lax.axis_size("gy")
    devices = count_x * count_y
    cx, nz, cy = pressure.shape
    wells = well_rate.shape[1] * count_y
    layers = 1 if count_x == 2 else 2
    columns_at, tiles = sent_tiles(cx, layers)[-2:]
    groups = -(-SEAM * 2 * cx // cy)
    offsets = window(count_x, cx)
    width = len(offsets)
    shape = jax.ShapeDtypeStruct
    whole = pl.BlockSpec(memory_space=pltpu.VMEM)
    anywhere = pl.BlockSpec(memory_space=pltpu.HBM)
    params = pltpu.CompilerParams(vmem_limit_bytes=32 * 1024 * 1024)

    fields = (pressure, saturation, saturation_old, pore_volume, permeability, jac_diag)
    perforations = (perf_cell, perf_well, perf_index, well_rate)
    wells_part, block, own, ya, yb, dinv, diag, off = pl.pallas_call(
        functools.partial(before_kernel, count_x, count_y),
        in_specs=[anywhere] * 11,
        out_specs=[anywhere, *[whole] * 7],
        out_shape=[
            pltpu.HBM((devices, 2, wells), f32),
            shape((tiles, nz, cy), f32),
            shape((BULK * cx + 2, nz, cy), f32),
            shape((cx + 1 + groups, nz, cy), f32),
            shape((max(cx + 1 + groups, 2 * cx), nz, cy), f32),
            shape((9, cx, nz, cy), f32),
            shape(jac_diag.shape, f32),
            shape(jac_off.shape, f32),
        ],
        scratch_shapes=[
            *[pltpu.VMEM(v.shape, v.dtype) for v in fields[:5]],
            *[pltpu.VMEM(v.shape, v.dtype) for v in perforations],
            pltpu.VMEM((devices, 2, wells), f32),
            pltpu.SemaphoreType.DMA((12,)),
        ],
        compiler_params=params,
        name="before",
    )(*[pltpu.with_memory_space_constraint(v, pltpu.HBM) for v in (*fields, jac_off, *perforations)])

    pairs = [(i, i ^ 1) for i in range(count_y)]
    others = [(i, other_pair(i, count_x, count_y)) for i in range(devices)]

    def from_x(values, offset):
        return lax.ppermute(
            values, "gx", [((i + offset) % count_x, i) for i in range(count_x)]
        )

    ya_got = lax.ppermute(ya, "gy", pairs)
    yb_got = lax.ppermute(yb, ("gx", "gy"), others)
    blocks = [from_x(block, o) for o in offsets[1:]]
    wells_all = lax.all_to_all(wells_part, ("gx", "gy"), 0, 0)
    ya_all = [ya_got] + [lax.ppermute(v[columns_at:], "gy", pairs) for v in blocks]
    yb_all = [yb_got] + [from_x(yb_got, o) for o in offsets[1:]]

    residual, direction, sums = pl.pallas_call(
        functools.partial(main_kernel, count_x, count_y, tuple(offsets)),
        in_specs=[whole] * (4 + 3 * width),
        out_specs=[whole] * 3,
        out_shape=[
            shape((3, cx, nz, cy), f32),
            shape((3, cx, nz, cy), f32),
            shape((devices, 2, cy), f32),
        ],
        compiler_params=params,
        name="main",
    )(wells_all, diag, off, dinv, own, *blocks, *ya_all, *yb_all)

    sums_all = lax.all_to_all(sums, ("gx", "gy"), 0, 0)
    update, residual = pl.pallas_call(
        after_kernel,
        in_specs=[whole] * 3,
        out_specs=[anywhere] * 2,
        out_shape=[pltpu.HBM((3, cx, nz, cy), f32)] * 2,
        scratch_shapes=[
            pltpu.VMEM((3, cx, nz, cy), f32),
            pltpu.SemaphoreType.DMA,
            pltpu.SemaphoreType.DMA((3,)),
        ],
        compiler_params=params,
        name="after",
    )(sums_all, direction, residual)
    return (residual, update)


def solution(mesh):
    placed = (
        P("gx", None, "gy"),
        P(None, "gx", None, "gy"),
        P(None, "gx", None, "gy"),
        P("gx", None, "gy"),
        P("gx", None, "gy"),
        P(None, None, "gx", None, "gy"),
        P(None, None, None, "gx", None, "gy"),
        P("gx", "gy"),
        P("gx", "gy"),
        P("gx", "gy"),
        P("gx", "gy"),
    )
    return jax.shard_map(
        body,
        mesh=mesh,
        in_specs=placed,
        out_specs=(P(None, "gx", None, "gy"), P(None, "gx", None, "gy")),
        check_vma=False,
    )
```

```python
import functools

import jax
import jax.numpy as jnp
from jax import lax
from jax.experimental import pallas as pl
from jax.experimental.pallas import tpu as pltpu
from jax.sharding import PartitionSpec as P

SWEEPS = 4
WIDE = SWEEPS + 1

viscosity = (1.0, 2.0, 0.2)
vertical_ratio = 0.1
f32 = jnp.float32

PRESS, MOB, PERM, PART, INV, COEF = 0, 1, 4, 5, 8, 9
BULK = 15
FACE = 5
DINV, DCOL, OFFC, EPART, EPRESS, EPERM, EWATER, EGAS = 0, 9, 12, 30, 33, 34, 35, 36
EDGE = 37
SEAM = 30
BORDER_AT = (BULK * WIDE + 1) // 2 * 2
SUM, INNER = 7, 8
TINY = 1e-30
NT = (((1,), (1,)), ((), ()))
NN = (((1,), (0,)), ((), ()))


def iota(shape, axis):
    return lax.broadcasted_iota(jnp.int32, shape, axis)


def split_dot(values, hot, dims):
    rows = values.shape[0]
    high = values.astype(jnp.bfloat16)
    rest = values - high.astype(f32)
    mid = rest.astype(jnp.bfloat16)
    low = (rest - mid.astype(f32)).astype(jnp.bfloat16)
    parts = jnp.concatenate([high, mid, low], axis=0)
    out = lax.dot_general(parts, hot, dims, preferred_element_type=f32)
    return out[:rows] + (out[rows : 2 * rows] + out[2 * rows :])


def total_of(terms):
    while len(terms) > 1:
        paired = [a + b for a, b in zip(terms[::2], terms[1::2])]
        terms = paired + terms[len(terms) - len(terms) % 2 :]
    return terms[0]


def hot_of(condition):
    return jnp.where(condition, 1.0, 0.0).astype(jnp.bfloat16)


def sent_tiles(cx, layers):
    edges = INNER * (cx - layers)
    borders = edges + EDGE * layers
    return edges, borders, borders + 1, borders + 2, borders + 3 + cx


def mobilities(water, gas):
    oil = 1.0 - water - gas
    return [
        water * water / viscosity[0],
        oil * oil / viscosity[1],
        gas * gas / viscosity[2],
    ]


def face_flows(here, there, weight):
    conduct = weight * here[PERM] * there[PERM] / (here[PERM] + there[PERM] + TINY)
    drop = here[PRESS] - there[PRESS]
    flow = conduct * drop
    return [
        flow * jnp.where(drop >= 0.0, here[MOB + c], there[MOB + c]) for c in range(3)
    ]


def window(count, cx):
    reach = -(-WIDE // cx)
    if count <= 2 * reach + 1:
        return list(range(count))
    return list(range(reach + 1)) + list(range(-reach, 0))


def before_kernel(
    count_x,
    count_y,
    *refs,
):
    sources, (wells_hbm, block_out, own_out, ya_out, yb_out, dinv_out) = refs[:11], refs[11:17]
    diag_ref, off_ref = refs[17:19]
    press_ref, sat_ref, old_ref, pore_ref, perm_ref = refs[19:24]
    cell_ref, well_ref, index_ref, rate_ref, wells_out, sems = refs[24:]
    targets = (*refs[19:24], diag_ref, off_ref, *refs[24:28])
    copies = []
    for i in (1, 0, 7, 9, 8, 10, 4, 2, 3, 5, 6):
        copies.append(pltpu.make_async_copy(sources[i], targets[i], sems.at[i]))
        copies[-1].start()
    for copy in copies[:6]:
        copy.wait()
    cx, nz, cy = press_ref.shape
    at_x = lax.axis_index("gx")
    at_y = lax.axis_index("gy")
    layers = 1 if count_x == 2 else 2
    edge_at, border_at, last, columns_at, _ = sent_tiles(cx, layers)

    press = press_ref[...]
    water, gas = sat_ref[0], sat_ref[1]
    mobile = mobilities(water, gas)

    cells = cell_ref[...]
    perfs = cells.shape[1]
    spot_xz = lax.div(cells, cy)
    spot_y = lax.rem(cells, cy)
    stacked = jnp.concatenate([m.reshape(cx * nz, cy) for m in mobile + [press]], axis=0)
    hot_y = hot_of(iota((cy, perfs), 0) == spot_y)
    picked = split_dot(stacked, hot_y, NN).reshape(4, cx * nz, perfs)
    on_xz = iota((cx * nz, perfs), 0) == spot_xz
    at_perf = [
        jnp.sum(jnp.where(on_xz, picked[i], 0.0), axis=0, keepdims=True) for i in range(4)
    ]
    index_vals = index_ref[...]
    parts = [index_vals * at_perf[i] for i in range(3)]
    strength = index_vals * (at_perf[0] + at_perf[1] + at_perf[2])
    weighted = strength * at_perf[3]
    row = iota((16, perfs), 0)
    both = jnp.where(row == 0, strength, jnp.where(row == 1, weighted, 0.0))
    wells = wells_out.shape[2]
    sums = split_dot(both, hot_of(iota((wells, perfs), 0) == well_ref[...]), NT)
    owned = rate_ref.shape[1]
    square = jnp.broadcast_to(rate_ref[...], (owned, owned))
    column = jnp.sum(
        jnp.where(iota((owned, owned), 0) == iota((owned, owned), 1), square, 0.0),
        axis=1,
        keepdims=True,
    )
    mine = iota((owned, wells), 1) == at_y * owned + iota((owned, wells), 0)
    rates = jnp.sum(jnp.where(mine, column, 0.0), axis=0, keepdims=True)
    pair = sums[:2] - jnp.where(iota((2, wells), 0) == 1, rates, 0.0)
    wells_out[...] = jnp.broadcast_to(pair[None], wells_out.shape)
    wells_copy = pltpu.make_async_copy(wells_out, wells_hbm, sems.at[11])
    wells_copy.start()

    perf_rows = [
        spot_xz.astype(f32),
        spot_y.astype(f32),
        well_ref[...].astype(f32),
        *parts,
        at_perf[3],
        jnp.zeros_like(at_perf[3]),
    ]
    for r, values in enumerate(perf_rows):
        block_out[last, r : r + 1, :] = values
        block_out[columns_at + cx, r : r + 1, :] = values
        own_out[BULK * cx, r : r + 1, :] = values
        ya_out[cx, r : r + 1, :] = values
        yb_out[cx, r : r + 1, :] = values

    for copy in copies[6:9]:
        copy.wait()
    perm = perm_ref[...]
    old_water, old_gas = old_ref[0], old_ref[1]
    oil, old_oil = 1.0 - water - gas, 1.0 - old_water - old_gas
    pore = pore_ref[...]
    part = [pore * (water - old_water), pore * (oil - old_oil), pore * (gas - old_gas)]
    layer_at = iota((cx, nz, cy), 1)
    lane_at = iota((cx, nz, cy), 2)
    cells_here = [press, *mobile, perm]
    flows = face_flows([v[:-1] for v in cells_here], [v[1:] for v in cells_here], 2.0)
    none = jnp.zeros((1, nz, cy), f32)
    for c in range(3):
        part[c] = part[c] + jnp.concatenate([flows[c], none], axis=0)
        part[c] = part[c] - jnp.concatenate([none, flows[c]], axis=0)
    for axis, weight, inside in (
        (2, 2.0, lane_at < cy - 1),
        (1, 2.0 * vertical_ratio, layer_at < nz - 1),
    ):
        size = cells_here[0].shape[axis]
        flows = face_flows(
            cells_here, [pltpu.roll(v, size - 1, axis) for v in cells_here], weight
        )
        for c in range(3):
            flow = jnp.where(inside, flows[c], 0.0)
            part[c] = part[c] + flow - pltpu.roll(flow, 1, axis)

    lane = iota((nz, cy), 1)
    to_left = [jnp.zeros((nz, cy), f32) for _ in range(cx)]
    to_right = [jnp.zeros((nz, cy), f32) for _ in range(cx)]
    beside = [jnp.zeros((nz, cy), f32) for _ in range(0, SEAM, cy // (2 * cx))]

    def put_bulk(f, values):
        own_out[f * cx : (f + 1) * cx] = values
        shift = f * WIDE
        on_left = (lane >= shift) & (lane < shift + WIDE)
        start = (shift - WIDE) % cy
        on_right = (lane >= start) & (lane < start + WIDE)
        for x in range(cx):
            turned = pltpu.roll(values[x], shift, 1) if shift else values[x]
            to_left[x] = jnp.where(on_left, turned, to_left[x])
            to_right[x] = jnp.where(on_right, turned, to_right[x])

    def put_edge(e, values):
        if layers == 1:
            block_out[edge_at + e] = jnp.where(at_x == 0, values[cx - 1], values[0])
        else:
            block_out[edge_at + e] = values[0]
            block_out[edge_at + EDGE + e] = values[cx - 1]
        if e < SEAM:
            group, place = divmod(e, cy // (2 * cx))
            for x in range(cx):
                at = 2 * (place * cx + x) + 1
                here = (lane == at - 1) | (lane == at)
                beside[group] = jnp.where(here, pltpu.roll(values[x], at, 1), beside[group])

    def put_inner(i, values):
        for x in range(cx - layers):
            at = i * (cx - layers) + x
            if layers == 1:
                block_out[at] = jnp.where(at_x == 0, values[x], values[x + 1])
            else:
                block_out[at] = values[x + 1]

    border = jnp.zeros((nz, cy), f32)
    for f in range(FACE):
        for x in range(cx):
            at = BORDER_AT + 2 * (f * cx + x) + 1
            first = pltpu.roll(cells_here[f][x], at - 1, 1)
            second = pltpu.roll(cells_here[f][x], at + 1, 1)
            border = jnp.where(lane == at - 1, first, jnp.where(lane == at, second, border))
    block_out[border_at] = border
    own_out[BULK * cx + 1] = border
    to_left[0] = to_right[0] = border
    for f, values in enumerate([*cells_here, *part]):
        put_bulk(f, values)
    for e, values in enumerate([*part, press, perm, water, gas]):
        put_edge(EPART + e, values)
    put_inner(SUM, part[0] + part[1] + part[2])

    copies[9].wait()
    diag = [[diag_ref[a, b] for b in range(3)] for a in range(3)]
    inverse = 1.0 / (diag[0][0] + diag[1][0] + diag[2][0])
    put_bulk(INV, inverse)
    put_inner(6, inverse)

    def cofactor(a, b):
        return (
            diag[(a + 1) % 3][(b + 1) % 3] * diag[(a + 2) % 3][(b + 2) % 3]
            - diag[(a + 1) % 3][(b + 2) % 3] * diag[(a + 2) % 3][(b + 1) % 3]
        )

    cofactors = [[cofactor(a, b) for b in range(3)] for a in range(3)]
    over = 1.0 / (
        diag[0][0] * cofactors[0][0] + diag[0][1] * cofactors[0][1] + diag[0][2] * cofactors[0][2]
    )
    for a in range(3):
        put_edge(DCOL + a, diag[a][0])
        for b in range(3):
            solve = cofactors[b][a] * over
            dinv_out[3 * a + b] = solve
            put_edge(DINV + 3 * a + b, solve)

    copies[10].wait()
    for q in range(6):
        columns = [off_ref[q, c, 0] for c in range(3)]
        if q == 4:
            columns = [jnp.where(layer_at > 0, v, 0.0) for v in columns]
        if q == 5:
            columns = [jnp.where(layer_at < nz - 1, v, 0.0) for v in columns]
        coef = (columns[0] + columns[1] + columns[2]) * inverse
        put_bulk(COEF + q, coef)
        put_inner(q, coef)
        for c in range(3):
            put_edge(OFFC + 3 * q + c, columns[c])

    even = lax.rem(at_y, 2) == 0
    for x in range(cx):
        ya_out[x] = jnp.where(even, to_right[x], to_left[x])
        yb_out[x] = jnp.where(even, to_left[x], to_right[x])
        block_out[columns_at + x] = ya_out[x]
    for t, values in enumerate(beside):
        ya_out[cx + 1 + t] = values
        yb_out[cx + 1 + t] = values
    for spare in range(cx + 1 + len(beside), yb_out.shape[0]):
        yb_out[spare] = jnp.zeros((nz, cy), f32)
    wells_copy.wait()


def main_kernel(count_x, count_y, offsets, *refs):
    width = len(offsets)
    (wells_ref, diag_ref, off_ref, dinv_ref, own_ref), refs = refs[:5], refs[5:]
    blocks, refs = (None, *refs[: width - 1]), refs[width - 1 :]
    ya_refs, refs = refs[:width], refs[width:]
    yb_refs, refs = refs[:width], refs[width:]
    residual_out, z_out, sums_out = refs

    cx, nz, cy = residual_out.shape[1:]
    total = width * cx
    at_x = lax.axis_index("gx")
    at_y = lax.axis_index("gy")
    even = lax.rem(at_y, 2) == 0
    has_left = jnp.where(at_y > 0, 1.0, 0.0).astype(f32)
    has_right = jnp.where(at_y < count_y - 1, 1.0, 0.0).astype(f32)
    layers = 1 if count_x == 2 else 2
    edge_at, border_at, last, columns_at, _ = sent_tiles(cx, layers)
    index_x = [lax.rem(at_x + (o % count_x), count_x) for o in offsets]
    joined = [
        jnp.where(index_x[(j + 1) % width] == index_x[j] + 1, 1.0, 0.0).astype(f32)
        for j in range(width)
    ]

    from_left, from_right = [], []
    for j in range(width):
        first, second = ya_refs[j][: cx + 1], yb_refs[j][: cx + 1]
        from_right.append(jnp.where(even, first, second) * has_right)
        from_left.append(jnp.where(even, second, first) * has_left)
    lane = iota((nz, cy), 1)

    merged = []
    for parity in range(2):
        of_right = lane < 0
        for f in range(parity, BULK, 2):
            of_right = of_right | ((lane >= f * WIDE) & (lane < (f + 1) * WIDE))
        merged.append(
            [
                jnp.where(of_right, from_right[j][x], from_left[j][x])
                for j in range(width)
                for x in range(cx)
            ]
        )

    def halo(f, x):
        tile = merged[f % 2][x]
        return pltpu.roll(tile, cy - f * WIDE, 1) if f else tile

    def arranged(edges, inner):
        if layers == 2:
            return jnp.stack([edges[0], *inner, edges[1]])
        first = [edges[0], *inner]
        second = [*inner, edges[0]]
        return jnp.stack([jnp.where(at_x == 0, a, b) for a, b in zip(first, second)])

    def received(j):
        block = blocks[j]
        edges = [
            [block[edge_at + side * EDGE + e] for e in range(EDGE)] for side in range(layers)
        ]
        inner = [
            [block[i * (cx - layers) + x] for x in range(cx - layers)] for i in range(INNER)
        ]
        zero = jnp.zeros((nz, cy), f32)
        part = [
            arranged(
                [edge[EPART + c] for edge in edges], inner[SUM] if c == 0 else [zero] * (cx - layers)
            )
            for c in range(3)
        ]
        scale = [1.0 / (edge[DCOL] + edge[DCOL + 1] + edge[DCOL + 2]) for edge in edges]
        coefs = [
            arranged(
                [
                    (edge[OFFC + 3 * q] + edge[OFFC + 3 * q + 1] + edge[OFFC + 3 * q + 2]) * by
                    for edge, by in zip(edges, scale)
                ],
                inner[q],
            )
            for q in range(6)
        ]
        return dict(enumerate([*part, arranged(scale, inner[6]), *coefs], start=PART))

    others = [received(j) for j in range(1, width)]

    def extended(f):
        own = jnp.concatenate(
            [own_ref[f * cx : (f + 1) * cx], *[other[f] for other in others]], axis=0
        )
        side = jnp.stack([halo(f, x) for x in range(total)])
        return jnp.concatenate([own, side], axis=2)

    lanes = 2 * cy
    level = iota((total, nz, lanes), 1)

    def next_x(v):
        return jnp.concatenate([v[1:], v[:1]], axis=0)

    def last_x(v):
        return jnp.concatenate([v[-1:], v[:-1]], axis=0)

    def next_y(v):
        return pltpu.roll(v, v.shape[2] - 1, 2)

    def last_y(v):
        return pltpu.roll(v, 1, 2)

    def next_z(v):
        return pltpu.roll(v, nz - 1, 1)

    def last_z(v):
        return pltpu.roll(v, 1, 1)

    def seam_after(v):
        rows = [v[i] for i in range(total)]
        for j in range(width):
            rows[j * cx + cx - 1] = rows[j * cx + cx - 1] * joined[j]
        return jnp.stack(rows)

    def seam_before(v):
        rows = [v[i] for i in range(total)]
        for j in range(width):
            at = ((j + 1) % width) * cx
            rows[at] = rows[at] * joined[j]
        return jnp.stack(rows)

    resid = [extended(PART + c) for c in range(3)]
    rows = [[resid[c][x] for x in range(total)] for c in range(3)]
    sides = {}

    def side_of(f, x):
        if (f, x) not in sides:
            sides[f, x] = halo(f, x)
        return sides[f, x]

    even_lane = lane % 2 == 0
    ends = (lane == 0) | (lane == cy - 1)
    for j in range(width):
        border = blocks[j][border_at] if j else own_ref[BULK * cx + 1]
        beyond = jnp.where(
            even_lane, pltpu.roll(from_left[j][0], cy - 1, 1), pltpu.roll(from_right[j][0], 1, 1)
        )
        backs = [cy - BORDER_AT - 2 * f * cx for f in range(FACE)]
        flows = face_flows(
            [pltpu.roll(beyond, back, 1) for back in backs],
            [pltpu.roll(border, back, 1) for back in backs],
            2.0,
        )
        for c in range(3):
            flow = jnp.where(lane < 2 * cx, flows[c], 0.0)
            swapped = jnp.where(even_lane, pltpu.roll(flow, cy - 1, 1), pltpu.roll(flow, 1, 1))
            for x in range(cx):
                back = cy - 2 * x - 1
                inward = jnp.where(ends, pltpu.roll(swapped, back, 1), 0.0)
                outward = jnp.where(ends, pltpu.roll(flow, back, 1), 0.0)
                at = j * cx + x
                rows[c][at] = rows[c][at] + jnp.concatenate([-inward, outward], axis=1)

    def edge_cells(j, last_layer):
        x = cx - 1 if last_layer else 0
        if j == 0:
            inside = [own_ref[f * cx + x] for f in range(FACE)]
        else:
            at = edge_at + (EDGE if last_layer and layers == 2 else 0)
            water, gas = blocks[j][at + EWATER], blocks[j][at + EGAS]
            inside = [
                blocks[j][at + EPRESS],
                *mobilities(water, gas),
                blocks[j][at + EPERM],
            ]
        return [
            jnp.concatenate([inside[f], side_of(f, j * cx + x)], axis=1) for f in range(FACE)
        ]

    for j in range(width):
        after = (j + 1) % width
        flows = face_flows(edge_cells(j, True), edge_cells(after, False), 2.0 * joined[j])
        for c in range(3):
            near_x, far_x = j * cx + cx - 1, after * cx
            rows[c][near_x] = rows[c][near_x] + flows[c]
            rows[c][far_x] = rows[c][far_x] - flows[c]
    resid = [jnp.stack(rows[c]) for c in range(3)]

    wells = wells_ref.shape[2]
    perfs = own_ref.shape[2]
    added = [[] for _ in range(3)]
    holes = jnp.zeros((16, wells), f32)
    lists = []
    for j in range(width):
        pair = jnp.sum(wells_ref[pl.ds(index_x[j] * count_y, count_y)], axis=0)
        holes = jnp.where(iota((16, wells), 0) == j, pair[1:2] / pair[0:1], holes)
        lists += [
            blocks[j][last] if j else own_ref[BULK * cx],
            from_left[j][cx],
            from_right[j][cx],
        ]
    listed = jnp.concatenate(lists, axis=1)
    number = iota((wells, perfs), 0).astype(f32)
    holes_at = jnp.concatenate(
        [split_dot(holes, hot_of(number == v[2:3]), NN) for v in lists], axis=1
    )
    for j in range(width):
        tiles = listed[:, 3 * perfs * j : 3 * perfs * (j + 1)]
        spot_xz, spot_y = tiles[0:1], tiles[1:2]
        fall = tiles[6:7] - holes_at[j : j + 1, 3 * perfs * j : 3 * perfs * (j + 1)]
        on_xz = iota((cx * nz, 3 * perfs), 0).astype(f32) == spot_xz
        spread = jnp.concatenate(
            [jnp.where(on_xz, tiles[3 + c : 4 + c] * fall, 0.0) for c in range(3)], axis=0
        )
        hot_y = iota((cy, 3 * perfs), 0).astype(f32) == spot_y
        nearby = iota((cy, 3 * perfs), 0)
        source = iota((cy, 3 * perfs), 1)
        kept = jnp.where(
            source < 2 * perfs, jnp.where(nearby >= cy - WIDE, 1, 0), jnp.where(nearby < WIDE, 1, 0)
        )
        hot_side = hot_of(hot_y & (kept == 1))
        inner = split_dot(spread[:, :perfs], hot_of(hot_y[:, :perfs]), NT)
        inner = inner.reshape(3, cx, nz, cy)
        aside = spread[:, perfs:]
        if j:
            aside = aside.reshape(3, cx * nz, 2 * perfs)
            aside = aside[0] + aside[1] + aside[2]
        outer = split_dot(aside, hot_side[:, perfs:], NT).reshape(-1, cx, nz, cy)
        for c in range(3):
            side = outer[c] if c < outer.shape[0] else jnp.zeros_like(outer[0])
            added[c].append(jnp.concatenate([inner[c], side], axis=2))
    start = [-(resid[c] + jnp.concatenate(added[c], axis=0)) for c in range(3)]
    for c in range(3):
        residual_out[c] = -start[c][:cx, :, :cy]

    coefs = [extended(COEF + q) for q in range(6)]
    coefs[0] = seam_before(coefs[0])
    coefs[1] = seam_after(coefs[1])
    scaled = (start[0] + start[1] + start[2]) * extended(INV)
    steps = (last_x, next_x, last_y, next_y, last_z, next_z)
    part = scaled
    for _ in range(1, SWEEPS):
        along_x, along_y, along_z = (
            coefs[q] * steps[q](part) + coefs[q + 1] * steps[q + 1](part) for q in (0, 2, 4)
        )
        part = (scaled - along_x) - (along_z + along_y)

    near = [step(part) for step in steps]
    near[0] = seam_before(near[0])
    near[1] = seam_after(near[1])
    near[4] = jnp.where(level > 0, near[4], 0.0)
    near[5] = jnp.where(level < nz - 1, near[5], 0.0)

    def direction(edge_of, here, around, initial):
        rest = []
        for c in range(3):
            coupled = [edge_of(OFFC + 3 * q + c) * beyond for q, beyond in enumerate(around)]
            rest.append(initial[c] - total_of([edge_of(DCOL + c) * here, *coupled]))
        solved = []
        for a in range(3):
            value = edge_of(DINV + 3 * a) * rest[0]
            value = value + edge_of(DINV + 3 * a + 1) * rest[1]
            solved.append(value + edge_of(DINV + 3 * a + 2) * rest[2])
        solved[0] = solved[0] + here
        return solved

    def edge_own(e):
        if e < DCOL:
            return dinv_ref[e]
        if e < OFFC:
            return diag_ref[e - DCOL, 0]
        return off_ref[(e - OFFC) // 3, (e - OFFC) % 3, 0]

    beside = []
    for t in range(cx + 1, cx + 1 - (-SEAM * 2 * cx // cy)):
        one, two = ya_refs[0][t], yb_refs[0][t]
        left, right = jnp.where(even, two, one) * has_left, jnp.where(even, one, two) * has_right
        beside.append(jnp.where(even_lane, left, right))

    def edge_side(e):
        tile, place = divmod(2 * cx * e, cy)
        return pltpu.roll(beside[tile], cy - place, 1) if place else beside[tile]

    def packed(tiles, shift):
        result = jnp.zeros((nz, cy), f32)
        for x in range(cx):
            turned = pltpu.roll(tiles[x], (2 * x + shift) % cy, 1)
            result = jnp.where((lane >= 2 * x) & (lane < 2 * x + 2), turned, result)
        return result

    inside = [part[x, :, :cy] for x in range(cx)]
    outside = [part[x, :, cy:] for x in range(cx)]
    here = packed(outside, 1)
    depth = iota((nz, cy), 0)
    z_side = direction(
        edge_side,
        here,
        [
            packed([part[total - 1, :, cy:] * joined[width - 1], *outside[:-1]], 1),
            packed([*outside[1:], part[cx % total, :, cy:] * joined[0]], 1),
            packed([jnp.where(lane == cy - 1, a, b) for a, b in zip(inside, outside)], 2),
            packed([jnp.where(lane == 0, a, b) for a, b in zip(inside, outside)], 0),
            jnp.where(depth > 0, pltpu.roll(here, 1, 0), 0.0),
            jnp.where(depth < nz - 1, pltpu.roll(here, nz - 1, 0), 0.0),
        ],
        [packed([start[c][x, :, cy:] for x in range(cx)], 1) for c in range(3)],
    )

    def direction_at(edge_of, where):
        return direction(
            edge_of, where(part), [where(v) for v in near], [where(v) for v in start]
        )

    after, before = 1 % width, width - 1
    z_own = direction_at(edge_own, lambda v: v[:cx, :, :cy])
    if layers == 1:
        z_next = z_last = direction_at(
            lambda e: blocks[after][edge_at + e],
            lambda v: jnp.where(at_x == 0, v[cx, :, :cy], v[total - 1, :, :cy]),
        )
    else:
        z_next = direction_at(
            lambda e: blocks[after][edge_at + e], lambda v: v[after * cx, :, :cy]
        )
        z_last = direction_at(
            lambda e: blocks[before][edge_at + EDGE + e],
            lambda v: v[before * cx + cx - 1, :, :cy],
        )
    level_own = iota((cx, nz, cy), 1)
    around = []
    for k in range(3):
        z_out[k] = z_own[k]
        before_y, after_y = [], []
        for x in range(cx):
            left = pltpu.roll(z_side[k], (cy - 2 * x) % cy, 1) if x else z_side[k]
            right = pltpu.roll(z_side[k], (cy - 2 - 2 * x) % cy, 1)
            before_y.append(jnp.where(lane == 0, left, pltpu.roll(z_own[k][x], 1, 1)))
            after_y.append(
                jnp.where(lane == cy - 1, right, pltpu.roll(z_own[k][x], cy - 1, 1))
            )
        around.append(
            [
                jnp.concatenate([(z_last[k] * joined[width - 1])[None], z_own[k][:-1]], axis=0),
                jnp.concatenate([z_own[k][1:], (z_next[k] * joined[0])[None]], axis=0),
                jnp.stack(before_y),
                jnp.stack(after_y),
                jnp.where(level_own > 0, last_z(z_own[k]), 0.0),
                jnp.where(level_own < nz - 1, next_z(z_own[k]), 0.0),
            ]
        )
    along = jnp.zeros((nz, cy), f32)
    square = jnp.zeros((nz, cy), f32)
    for c in range(3):
        terms = [diag_ref[c, k] * z_own[k] for k in range(3)]
        terms += [off_ref[q, c, k] * around[k][q] for q in range(6) for k in range(3)]
        mapped = total_of(terms)
        along = along + jnp.sum(mapped * start[c][:cx, :, :cy], axis=0)
        square = square + jnp.sum(mapped * mapped, axis=0)
    along = jnp.sum(along, axis=0, keepdims=True)
    square = jnp.sum(square, axis=0, keepdims=True)
    pair = jnp.where(iota((2, cy), 0) == 0, along, square)
    sums_out[...] = jnp.broadcast_to(pair[None], sums_out.shape)


def after_kernel(sums_ref, z_ref, residual_ref, update_hbm, residual_hbm, update_out, sem, sems):
    copy = pltpu.make_async_copy(residual_ref, residual_hbm, sem)
    copy.start()
    pair = jnp.sum(sums_ref[...], axis=0)
    both = jnp.sum(pair, axis=1, keepdims=True)
    step = both[0:1] / both[1:2]
    copies = []
    for c in range(3):
        update_out[c] = z_ref[c] * step[None]
        copies.append(pltpu.make_async_copy(update_out.at[c], update_hbm.at[c], sems.at[c]))
        copies[-1].start()
    for each in [copy, *copies]:
        each.wait()


def other_pair(device, count_x, count_y):
    x, y = divmod(device, count_y)
    near = y + 1 if y % 2 else y - 1
    if 0 <= near < count_y:
        return x * count_y + near
    return (x ^ 1) * count_y + y if count_x % 2 == 0 else device


def body(
    pressure,
    saturation,
    saturation_old,
    pore_volume,
    permeability,
    jac_diag,
    jac_off,
    perf_cell,
    perf_well,
    perf_index,
    well_rate,
):
    count_x, count_y = lax.axis_size("gx"), lax.axis_size("gy")
    devices = count_x * count_y
    cx, nz, cy = pressure.shape
    wells = well_rate.shape[1] * count_y
    layers = 1 if count_x == 2 else 2
    columns_at, tiles = sent_tiles(cx, layers)[-2:]
    groups = -(-SEAM * 2 * cx // cy)
    offsets = window(count_x, cx)
    width = len(offsets)
    shape = jax.ShapeDtypeStruct
    whole = pl.BlockSpec(memory_space=pltpu.VMEM)
    anywhere = pl.BlockSpec(memory_space=pltpu.HBM)
    params = pltpu.CompilerParams(vmem_limit_bytes=32 * 1024 * 1024)

    fields = (pressure, saturation, saturation_old, pore_volume, permeability, jac_diag)
    perforations = (perf_cell, perf_well, perf_index, well_rate)
    wells_part, block, own, ya, yb, dinv, diag, off = pl.pallas_call(
        functools.partial(before_kernel, count_x, count_y),
        in_specs=[anywhere] * 11,
        out_specs=[anywhere, *[whole] * 7],
        out_shape=[
            pltpu.HBM((devices, 2, wells), f32),
            shape((tiles, nz, cy), f32),
            shape((BULK * cx + 2, nz, cy), f32),
            shape((cx + 1 + groups, nz, cy), f32),
            shape((max(cx + 1 + groups, 2 * cx), nz, cy), f32),
            shape((9, cx, nz, cy), f32),
            shape(jac_diag.shape, f32),
            shape(jac_off.shape, f32),
        ],
        scratch_shapes=[
            *[pltpu.VMEM(v.shape, v.dtype) for v in fields[:5]],
            *[pltpu.VMEM(v.shape, v.dtype) for v in perforations],
            pltpu.VMEM((devices, 2, wells), f32),
            pltpu.SemaphoreType.DMA((12,)),
        ],
        compiler_params=params,
        name="before",
    )(*[pltpu.with_memory_space_constraint(v, pltpu.HBM) for v in (*fields, jac_off, *perforations)])

    pairs = [(i, i ^ 1) for i in range(count_y)]
    others = [(i, other_pair(i, count_x, count_y)) for i in range(devices)]

    def from_x(values, offset):
        return lax.ppermute(
            values, "gx", [((i + offset) % count_x, i) for i in range(count_x)]
        )

    ya_got = lax.ppermute(ya, "gy", pairs)
    yb_got = lax.ppermute(yb, ("gx", "gy"), others)
    blocks = [from_x(block, o) for o in offsets[1:]]
    wells_all = lax.all_to_all(wells_part, ("gx", "gy"), 0, 0)
    ya_all = [ya_got] + [lax.ppermute(v[columns_at:], "gy", pairs) for v in blocks]
    yb_all = [yb_got] + [from_x(yb_got, o) for o in offsets[1:]]

    residual, direction, sums = pl.pallas_call(
        functools.partial(main_kernel, count_x, count_y, tuple(offsets)),
        in_specs=[whole] * (4 + 3 * width),
        out_specs=[whole] * 3,
        out_shape=[
            shape((3, cx, nz, cy), f32),
            shape((3, cx, nz, cy), f32),
            shape((devices, 2, cy), f32),
        ],
        compiler_params=params,
        name="main",
    )(wells_all, diag, off, dinv, own, *blocks, *ya_all, *yb_all)

    sums_all = lax.all_to_all(sums, ("gx", "gy"), 0, 0)
    update, residual = pl.pallas_call(
        after_kernel,
        in_specs=[whole] * 3,
        out_specs=[anywhere] * 2,
        out_shape=[pltpu.HBM((3, cx, nz, cy), f32)] * 2,
        scratch_shapes=[
            pltpu.VMEM((3, cx, nz, cy), f32),
            pltpu.SemaphoreType.DMA,
            pltpu.SemaphoreType.DMA((3,)),
        ],
        compiler_params=params,
        name="after",
    )(sums_all, direction, residual)
    return (residual, update)


def solution(mesh):
    placed = (
        P("gx", None, "gy"),
        P(None, "gx", None, "gy"),
        P(None, "gx", None, "gy"),
        P("gx", None, "gy"),
        P("gx", None, "gy"),
        P(None, None, "gx", None, "gy"),
        P(None, None, None, "gx", None, "gy"),
        P("gx", "gy"),
        P("gx", "gy"),
        P("gx", "gy"),
        P("gx", "gy"),
    )
    return jax.shard_map(
        body,
        mesh=mesh,
        in_specs=placed,
        out_specs=(P(None, "gx", None, "gy"), P(None, "gx", None, "gy")),
        check_vma=False,
    )
```

```python
import functools

import jax
import jax.numpy as jnp
from jax import lax
from jax.experimental import pallas as pl
from jax.experimental.pallas import tpu as pltpu
from jax.sharding import PartitionSpec as P

SWEEPS = 4
WIDE = SWEEPS + 1

viscosity = (1.0, 2.0, 0.2)
vertical_ratio = 0.1
f32 = jnp.float32

PRESS, MOB, PERM, PART, INV, COEF = 0, 1, 4, 5, 8, 9
BULK = 15
FACE = 5
DINV, DCOL, OFFC, EPART, EPRESS, EPERM, EWATER, EGAS = 0, 9, 12, 30, 33, 34, 35, 36
EDGE = 37
SEAM = 30
BORDER_AT = (BULK * WIDE + 1) // 2 * 2
SUM, INNER = 7, 8
TINY = 1e-30
NT = (((1,), (1,)), ((), ()))
NN = (((1,), (0,)), ((), ()))


def iota(shape, axis):
    return lax.broadcasted_iota(jnp.int32, shape, axis)


def split_dot(values, hot, dims):
    rows = values.shape[0]
    high = values.astype(jnp.bfloat16)
    rest = values - high.astype(f32)
    mid = rest.astype(jnp.bfloat16)
    low = (rest - mid.astype(f32)).astype(jnp.bfloat16)
    parts = jnp.concatenate([high, mid, low], axis=0)
    out = lax.dot_general(parts, hot, dims, preferred_element_type=f32)
    return out[:rows] + (out[rows : 2 * rows] + out[2 * rows :])


def total_of(terms):
    while len(terms) > 1:
        paired = [a + b for a, b in zip(terms[::2], terms[1::2])]
        terms = paired + terms[len(terms) - len(terms) % 2 :]
    return terms[0]


def hot_of(condition):
    return jnp.where(condition, 1.0, 0.0).astype(jnp.bfloat16)


def sent_tiles(cx, layers):
    edges = INNER * (cx - layers)
    borders = edges + EDGE * layers
    return edges, borders, borders + 1, borders + 2, borders + 3 + cx


def mobilities(water, gas):
    oil = 1.0 - water - gas
    return [
        water * water / viscosity[0],
        oil * oil / viscosity[1],
        gas * gas / viscosity[2],
    ]


def face_flows(here, there, weight):
    conduct = weight * here[PERM] * there[PERM] / (here[PERM] + there[PERM] + TINY)
    drop = here[PRESS] - there[PRESS]
    flow = conduct * drop
    return [
        flow * jnp.where(drop >= 0.0, here[MOB + c], there[MOB + c]) for c in range(3)
    ]


def window(count, cx):
    reach = -(-WIDE // cx)
    if count <= 2 * reach + 1:
        return list(range(count))
    return list(range(reach + 1)) + list(range(-reach, 0))


def before_kernel(
    count_x,
    count_y,
    *refs,
):
    sources, (wells_hbm, block_out, own_out, ya_out, yb_out, dinv_out) = refs[:11], refs[11:17]
    diag_ref, off_ref = refs[17:19]
    press_ref, sat_ref, old_ref, pore_ref, perm_ref = refs[19:24]
    cell_ref, well_ref, index_ref, rate_ref, wells_out, sems = refs[24:]
    targets = (*refs[19:24], diag_ref, off_ref, *refs[24:28])
    copies = []
    for i in (1, 0, 7, 9, 8, 10, 4, 2, 3, 5, 6):
        copies.append(pltpu.make_async_copy(sources[i], targets[i], sems.at[i]))
        copies[-1].start()
    for copy in copies[:6]:
        copy.wait()
    cx, nz, cy = press_ref.shape
    at_x = lax.axis_index("gx")
    at_y = lax.axis_index("gy")
    layers = 1 if count_x == 2 else 2
    edge_at, border_at, last, columns_at, _ = sent_tiles(cx, layers)

    press = press_ref[...]
    water, gas = sat_ref[0], sat_ref[1]
    mobile = mobilities(water, gas)

    cells = cell_ref[...]
    perfs = cells.shape[1]
    spot_xz = lax.div(cells, cy)
    spot_y = lax.rem(cells, cy)
    stacked = jnp.concatenate([v.reshape(cx * nz, cy) for v in (water, gas, press)], axis=0)
    hot_y = hot_of(iota((cy, perfs), 0) == spot_y)
    picked = split_dot(stacked, hot_y, NN).reshape(3, cx * nz, perfs)
    on_xz = iota((cx * nz, perfs), 0) == spot_xz
    water_at, gas_at, press_at = (
        jnp.sum(jnp.where(on_xz, picked[i], 0.0), axis=0, keepdims=True) for i in range(3)
    )
    at_perf = [*mobilities(water_at, gas_at), press_at]
    index_vals = index_ref[...]
    parts = [index_vals * at_perf[i] for i in range(3)]
    strength = index_vals * (at_perf[0] + at_perf[1] + at_perf[2])
    weighted = strength * at_perf[3]
    row = iota((16, perfs), 0)
    both = jnp.where(row == 0, strength, jnp.where(row == 1, weighted, 0.0))
    wells = wells_out.shape[2]
    sums = split_dot(both, hot_of(iota((wells, perfs), 0) == well_ref[...]), NT)
    owned = rate_ref.shape[1]
    square = jnp.broadcast_to(rate_ref[...], (owned, owned))
    column = jnp.sum(
        jnp.where(iota((owned, owned), 0) == iota((owned, owned), 1), square, 0.0),
        axis=1,
        keepdims=True,
    )
    mine = iota((owned, wells), 1) == at_y * owned + iota((owned, wells), 0)
    rates = jnp.sum(jnp.where(mine, column, 0.0), axis=0, keepdims=True)
    pair = sums[:2] - jnp.where(iota((2, wells), 0) == 1, rates, 0.0)
    wells_out[...] = jnp.broadcast_to(pair[None], wells_out.shape)
    wells_copy = pltpu.make_async_copy(wells_out, wells_hbm, sems.at[11])
    wells_copy.start()

    perf_rows = [
        spot_xz.astype(f32),
        spot_y.astype(f32),
        well_ref[...].astype(f32),
        *parts,
        at_perf[3],
        jnp.zeros_like(at_perf[3]),
    ]
    for r, values in enumerate(perf_rows):
        block_out[last, r : r + 1, :] = values
        block_out[columns_at + cx, r : r + 1, :] = values
        own_out[BULK * cx, r : r + 1, :] = values
        ya_out[cx, r : r + 1, :] = values
        yb_out[cx, r : r + 1, :] = values

    for copy in copies[6:9]:
        copy.wait()
    perm = perm_ref[...]
    old_water, old_gas = old_ref[0], old_ref[1]
    oil, old_oil = 1.0 - water - gas, 1.0 - old_water - old_gas
    pore = pore_ref[...]
    part = [pore * (water - old_water), pore * (oil - old_oil), pore * (gas - old_gas)]
    layer_at = iota((cx, nz, cy), 1)
    lane_at = iota((cx, nz, cy), 2)
    cells_here = [press, *mobile, perm]
    flows = face_flows([v[:-1] for v in cells_here], [v[1:] for v in cells_here], 2.0)
    none = jnp.zeros((1, nz, cy), f32)
    for c in range(3):
        part[c] = part[c] + jnp.concatenate([flows[c], none], axis=0)
        part[c] = part[c] - jnp.concatenate([none, flows[c]], axis=0)
    for axis, weight, inside in (
        (2, 2.0, lane_at < cy - 1),
        (1, 2.0 * vertical_ratio, layer_at < nz - 1),
    ):
        size = cells_here[0].shape[axis]
        flows = face_flows(
            cells_here, [pltpu.roll(v, size - 1, axis) for v in cells_here], weight
        )
        for c in range(3):
            flow = jnp.where(inside, flows[c], 0.0)
            part[c] = part[c] + flow - pltpu.roll(flow, 1, axis)

    lane = iota((nz, cy), 1)
    to_left = [jnp.zeros((nz, cy), f32) for _ in range(cx)]
    to_right = [jnp.zeros((nz, cy), f32) for _ in range(cx)]
    beside = [jnp.zeros((nz, cy), f32) for _ in range(0, SEAM, cy // (2 * cx))]

    def put_bulk(f, values):
        own_out[f * cx : (f + 1) * cx] = values
        shift = f * WIDE
        on_left = (lane >= shift) & (lane < shift + WIDE)
        start = (shift - WIDE) % cy
        on_right = (lane >= start) & (lane < start + WIDE)
        for x in range(cx):
            turned = pltpu.roll(values[x], shift, 1) if shift else values[x]
            to_left[x] = jnp.where(on_left, turned, to_left[x])
            to_right[x] = jnp.where(on_right, turned, to_right[x])

    def put_edge(e, values):
        if layers == 1:
            block_out[edge_at + e] = jnp.where(at_x == 0, values[cx - 1], values[0])
        else:
            block_out[edge_at + e] = values[0]
            block_out[edge_at + EDGE + e] = values[cx - 1]
        if e < SEAM:
            group, place = divmod(e, cy // (2 * cx))
            for x in range(cx):
                at = 2 * (place * cx + x) + 1
                here = (lane == at - 1) | (lane == at)
                beside[group] = jnp.where(here, pltpu.roll(values[x], at, 1), beside[group])

    def put_inner(i, values):
        for x in range(cx - layers):
            at = i * (cx - layers) + x
            if layers == 1:
                block_out[at] = jnp.where(at_x == 0, values[x], values[x + 1])
            else:
                block_out[at] = values[x + 1]

    border = jnp.zeros((nz, cy), f32)
    for f in range(FACE):
        for x in range(cx):
            at = BORDER_AT + 2 * (f * cx + x) + 1
            first = pltpu.roll(cells_here[f][x], at - 1, 1)
            second = pltpu.roll(cells_here[f][x], at + 1, 1)
            border = jnp.where(lane == at - 1, first, jnp.where(lane == at, second, border))
    block_out[border_at] = border
    own_out[BULK * cx + 1] = border
    to_left[0] = to_right[0] = border
    for f, values in enumerate([*cells_here, *part]):
        put_bulk(f, values)
    for e, values in enumerate([*part, press, perm, water, gas]):
        put_edge(EPART + e, values)
    put_inner(SUM, part[0] + part[1] + part[2])

    copies[9].wait()
    diag = [[diag_ref[a, b] for b in range(3)] for a in range(3)]
    inverse = 1.0 / (diag[0][0] + diag[1][0] + diag[2][0])
    put_bulk(INV, inverse)
    put_inner(6, inverse)

    def cofactor(a, b):
        return (
            diag[(a + 1) % 3][(b + 1) % 3] * diag[(a + 2) % 3][(b + 2) % 3]
            - diag[(a + 1) % 3][(b + 2) % 3] * diag[(a + 2) % 3][(b + 1) % 3]
        )

    cofactors = [[cofactor(a, b) for b in range(3)] for a in range(3)]
    over = 1.0 / (
        diag[0][0] * cofactors[0][0] + diag[0][1] * cofactors[0][1] + diag[0][2] * cofactors[0][2]
    )
    for a in range(3):
        put_edge(DCOL + a, diag[a][0])
        for b in range(3):
            solve = cofactors[b][a] * over
            dinv_out[3 * a + b] = solve
            put_edge(DINV + 3 * a + b, solve)

    copies[10].wait()
    for q in range(6):
        columns = [off_ref[q, c, 0] for c in range(3)]
        if q == 4:
            columns = [jnp.where(layer_at > 0, v, 0.0) for v in columns]
        if q == 5:
            columns = [jnp.where(layer_at < nz - 1, v, 0.0) for v in columns]
        coef = (columns[0] + columns[1] + columns[2]) * inverse
        put_bulk(COEF + q, coef)
        put_inner(q, coef)
        for c in range(3):
            put_edge(OFFC + 3 * q + c, columns[c])

    even = lax.rem(at_y, 2) == 0
    for x in range(cx):
        ya_out[x] = jnp.where(even, to_right[x], to_left[x])
        yb_out[x] = jnp.where(even, to_left[x], to_right[x])
        block_out[columns_at + x] = ya_out[x]
    for t, values in enumerate(beside):
        ya_out[cx + 1 + t] = values
        yb_out[cx + 1 + t] = values
    for spare in range(cx + 1 + len(beside), yb_out.shape[0]):
        yb_out[spare] = jnp.zeros((nz, cy), f32)
    wells_copy.wait()


def main_kernel(count_x, count_y, offsets, *refs):
    width = len(offsets)
    (wells_ref, diag_ref, off_ref, dinv_ref, own_ref), refs = refs[:5], refs[5:]
    blocks, refs = (None, *refs[: width - 1]), refs[width - 1 :]
    ya_refs, refs = refs[:width], refs[width:]
    yb_refs, refs = refs[:width], refs[width:]
    residual_out, z_out, sums_out = refs

    cx, nz, cy = residual_out.shape[1:]
    total = width * cx
    at_x = lax.axis_index("gx")
    at_y = lax.axis_index("gy")
    even = lax.rem(at_y, 2) == 0
    has_left = jnp.where(at_y > 0, 1.0, 0.0).astype(f32)
    has_right = jnp.where(at_y < count_y - 1, 1.0, 0.0).astype(f32)
    layers = 1 if count_x == 2 else 2
    edge_at, border_at, last, columns_at, _ = sent_tiles(cx, layers)
    index_x = [lax.rem(at_x + (o % count_x), count_x) for o in offsets]
    joined = [
        jnp.where(index_x[(j + 1) % width] == index_x[j] + 1, 1.0, 0.0).astype(f32)
        for j in range(width)
    ]

    from_left, from_right = [], []
    for j in range(width):
        first, second = ya_refs[j][: cx + 1], yb_refs[j][: cx + 1]
        from_right.append(jnp.where(even, first, second) * has_right)
        from_left.append(jnp.where(even, second, first) * has_left)
    lane = iota((nz, cy), 1)

    merged = []
    for parity in range(2):
        of_right = lane < 0
        for f in range(parity, BULK, 2):
            of_right = of_right | ((lane >= f * WIDE) & (lane < (f + 1) * WIDE))
        merged.append(
            [
                jnp.where(of_right, from_right[j][x], from_left[j][x])
                for j in range(width)
                for x in range(cx)
            ]
        )

    def halo(f, x):
        tile = merged[f % 2][x]
        return pltpu.roll(tile, cy - f * WIDE, 1) if f else tile

    def arranged(edges, inner):
        if layers == 2:
            return jnp.stack([edges[0], *inner, edges[1]])
        first = [edges[0], *inner]
        second = [*inner, edges[0]]
        return jnp.stack([jnp.where(at_x == 0, a, b) for a, b in zip(first, second)])

    def received(j):
        block = blocks[j]
        edges = [
            [block[edge_at + side * EDGE + e] for e in range(EDGE)] for side in range(layers)
        ]
        inner = [
            [block[i * (cx - layers) + x] for x in range(cx - layers)] for i in range(INNER)
        ]
        zero = jnp.zeros((nz, cy), f32)
        part = [
            arranged(
                [edge[EPART + c] for edge in edges], inner[SUM] if c == 0 else [zero] * (cx - layers)
            )
            for c in range(3)
        ]
        scale = [1.0 / (edge[DCOL] + edge[DCOL + 1] + edge[DCOL + 2]) for edge in edges]
        coefs = [
            arranged(
                [
                    (edge[OFFC + 3 * q] + edge[OFFC + 3 * q + 1] + edge[OFFC + 3 * q + 2]) * by
                    for edge, by in zip(edges, scale)
                ],
                inner[q],
            )
            for q in range(6)
        ]
        return dict(enumerate([*part, arranged(scale, inner[6]), *coefs], start=PART))

    others = [received(j) for j in range(1, width)]

    def extended(f):
        own = jnp.concatenate(
            [own_ref[f * cx : (f + 1) * cx], *[other[f] for other in others]], axis=0
        )
        side = jnp.stack([halo(f, x) for x in range(total)])
        return jnp.concatenate([own, side], axis=2)

    lanes = 2 * cy
    level = iota((total, nz, lanes), 1)

    def next_x(v):
        return jnp.concatenate([v[1:], v[:1]], axis=0)

    def last_x(v):
        return jnp.concatenate([v[-1:], v[:-1]], axis=0)

    def next_y(v):
        return pltpu.roll(v, v.shape[2] - 1, 2)

    def last_y(v):
        return pltpu.roll(v, 1, 2)

    def next_z(v):
        return pltpu.roll(v, nz - 1, 1)

    def last_z(v):
        return pltpu.roll(v, 1, 1)

    def seam_after(v):
        rows = [v[i] for i in range(total)]
        for j in range(width):
            rows[j * cx + cx - 1] = rows[j * cx + cx - 1] * joined[j]
        return jnp.stack(rows)

    def seam_before(v):
        rows = [v[i] for i in range(total)]
        for j in range(width):
            at = ((j + 1) % width) * cx
            rows[at] = rows[at] * joined[j]
        return jnp.stack(rows)

    resid = [extended(PART + c) for c in range(3)]
    rows = [[resid[c][x] for x in range(total)] for c in range(3)]
    sides = {}

    def side_of(f, x):
        if (f, x) not in sides:
            sides[f, x] = halo(f, x)
        return sides[f, x]

    even_lane = lane % 2 == 0
    ends = (lane == 0) | (lane == cy - 1)
    for j in range(width):
        border = blocks[j][border_at] if j else own_ref[BULK * cx + 1]
        beyond = jnp.where(
            even_lane, pltpu.roll(from_left[j][0], cy - 1, 1), pltpu.roll(from_right[j][0], 1, 1)
        )
        backs = [cy - BORDER_AT - 2 * f * cx for f in range(FACE)]
        flows = face_flows(
            [pltpu.roll(beyond, back, 1) for back in backs],
            [pltpu.roll(border, back, 1) for back in backs],
            2.0,
        )
        for c in range(3):
            flow = jnp.where(lane < 2 * cx, flows[c], 0.0)
            swapped = jnp.where(even_lane, pltpu.roll(flow, cy - 1, 1), pltpu.roll(flow, 1, 1))
            for x in range(cx):
                back = cy - 2 * x - 1
                inward = jnp.where(ends, pltpu.roll(swapped, back, 1), 0.0)
                outward = jnp.where(ends, pltpu.roll(flow, back, 1), 0.0)
                at = j * cx + x
                rows[c][at] = rows[c][at] + jnp.concatenate([-inward, outward], axis=1)

    def edge_cells(j, last_layer):
        x = cx - 1 if last_layer else 0
        if j == 0:
            inside = [own_ref[f * cx + x] for f in range(FACE)]
        else:
            at = edge_at + (EDGE if last_layer and layers == 2 else 0)
            water, gas = blocks[j][at + EWATER], blocks[j][at + EGAS]
            inside = [
                blocks[j][at + EPRESS],
                *mobilities(water, gas),
                blocks[j][at + EPERM],
            ]
        return [
            jnp.concatenate([inside[f], side_of(f, j * cx + x)], axis=1) for f in range(FACE)
        ]

    for j in range(width):
        after = (j + 1) % width
        flows = face_flows(edge_cells(j, True), edge_cells(after, False), 2.0 * joined[j])
        for c in range(3):
            near_x, far_x = j * cx + cx - 1, after * cx
            rows[c][near_x] = rows[c][near_x] + flows[c]
            rows[c][far_x] = rows[c][far_x] - flows[c]
    resid = [jnp.stack(rows[c]) for c in range(3)]

    wells = wells_ref.shape[2]
    perfs = own_ref.shape[2]
    added = [[] for _ in range(3)]
    holes = jnp.zeros((16, wells), f32)
    lists = []
    for j in range(width):
        pair = jnp.sum(wells_ref[pl.ds(index_x[j] * count_y, count_y)], axis=0)
        holes = jnp.where(iota((16, wells), 0) == j, pair[1:2] / pair[0:1], holes)
        lists += [
            blocks[j][last] if j else own_ref[BULK * cx],
            from_left[j][cx],
            from_right[j][cx],
        ]
    listed = jnp.concatenate(lists, axis=1)
    number = iota((wells, perfs), 0).astype(f32)
    holes_at = jnp.concatenate(
        [split_dot(holes, hot_of(number == v[2:3]), NN) for v in lists], axis=1
    )
    for j in range(width):
        tiles = listed[:, 3 * perfs * j : 3 * perfs * (j + 1)]
        spot_xz, spot_y = tiles[0:1], tiles[1:2]
        fall = tiles[6:7] - holes_at[j : j + 1, 3 * perfs * j : 3 * perfs * (j + 1)]
        on_xz = iota((cx * nz, 3 * perfs), 0).astype(f32) == spot_xz
        spread = jnp.concatenate(
            [jnp.where(on_xz, tiles[3 + c : 4 + c] * fall, 0.0) for c in range(3)], axis=0
        )
        hot_y = iota((cy, 3 * perfs), 0).astype(f32) == spot_y
        nearby = iota((cy, 3 * perfs), 0)
        source = iota((cy, 3 * perfs), 1)
        kept = jnp.where(
            source < 2 * perfs, jnp.where(nearby >= cy - WIDE, 1, 0), jnp.where(nearby < WIDE, 1, 0)
        )
        hot_side = hot_of(hot_y & (kept == 1))
        inner = split_dot(spread[:, :perfs], hot_of(hot_y[:, :perfs]), NT)
        inner = inner.reshape(3, cx, nz, cy)
        aside = spread[:, perfs:]
        if j:
            aside = aside.reshape(3, cx * nz, 2 * perfs)
            aside = aside[0] + aside[1] + aside[2]
        outer = split_dot(aside, hot_side[:, perfs:], NT).reshape(-1, cx, nz, cy)
        for c in range(3):
            side = outer[c] if c < outer.shape[0] else jnp.zeros_like(outer[0])
            added[c].append(jnp.concatenate([inner[c], side], axis=2))
    start = [-(resid[c] + jnp.concatenate(added[c], axis=0)) for c in range(3)]
    for c in range(3):
        residual_out[c] = -start[c][:cx, :, :cy]

    coefs = [extended(COEF + q) for q in range(6)]
    coefs[0] = seam_before(coefs[0])
    coefs[1] = seam_after(coefs[1])
    scaled = (start[0] + start[1] + start[2]) * extended(INV)
    steps = (last_x, next_x, last_y, next_y, last_z, next_z)
    part = scaled
    for _ in range(1, SWEEPS):
        along_x, along_y, along_z = (
            coefs[q] * steps[q](part) + coefs[q + 1] * steps[q + 1](part) for q in (0, 2, 4)
        )
        part = (scaled - along_x) - (along_z + along_y)

    near = [step(part) for step in steps]
    near[0] = seam_before(near[0])
    near[1] = seam_after(near[1])
    near[4] = jnp.where(level > 0, near[4], 0.0)
    near[5] = jnp.where(level < nz - 1, near[5], 0.0)

    def direction(edge_of, here, around, initial):
        rest = []
        for c in range(3):
            coupled = [edge_of(OFFC + 3 * q + c) * beyond for q, beyond in enumerate(around)]
            rest.append(initial[c] - total_of([edge_of(DCOL + c) * here, *coupled]))
        solved = []
        for a in range(3):
            value = edge_of(DINV + 3 * a) * rest[0]
            value = value + edge_of(DINV + 3 * a + 1) * rest[1]
            solved.append(value + edge_of(DINV + 3 * a + 2) * rest[2])
        solved[0] = solved[0] + here
        return solved

    def edge_own(e):
        if e < DCOL:
            return dinv_ref[e]
        if e < OFFC:
            return diag_ref[e - DCOL, 0]
        return off_ref[(e - OFFC) // 3, (e - OFFC) % 3, 0]

    beside = []
    for t in range(cx + 1, cx + 1 - (-SEAM * 2 * cx // cy)):
        one, two = ya_refs[0][t], yb_refs[0][t]
        left, right = jnp.where(even, two, one) * has_left, jnp.where(even, one, two) * has_right
        beside.append(jnp.where(even_lane, left, right))

    def edge_side(e):
        tile, place = divmod(2 * cx * e, cy)
        return pltpu.roll(beside[tile], cy - place, 1) if place else beside[tile]

    def packed(tiles, shift):
        result = jnp.zeros((nz, cy), f32)
        for x in range(cx):
            turned = pltpu.roll(tiles[x], (2 * x + shift) % cy, 1)
            result = jnp.where((lane >= 2 * x) & (lane < 2 * x + 2), turned, result)
        return result

    inside = [part[x, :, :cy] for x in range(cx)]
    outside = [part[x, :, cy:] for x in range(cx)]
    here = packed(outside, 1)
    depth = iota((nz, cy), 0)
    z_side = direction(
        edge_side,
        here,
        [
            packed([part[total - 1, :, cy:] * joined[width - 1], *outside[:-1]], 1),
            packed([*outside[1:], part[cx % total, :, cy:] * joined[0]], 1),
            packed([jnp.where(lane == cy - 1, a, b) for a, b in zip(inside, outside)], 2),
            packed([jnp.where(lane == 0, a, b) for a, b in zip(inside, outside)], 0),
            jnp.where(depth > 0, pltpu.roll(here, 1, 0), 0.0),
            jnp.where(depth < nz - 1, pltpu.roll(here, nz - 1, 0), 0.0),
        ],
        [packed([start[c][x, :, cy:] for x in range(cx)], 1) for c in range(3)],
    )

    def direction_at(edge_of, where):
        return direction(
            edge_of, where(part), [where(v) for v in near], [where(v) for v in start]
        )

    after, before = 1 % width, width - 1
    z_own = direction_at(edge_own, lambda v: v[:cx, :, :cy])
    if layers == 1:
        z_next = z_last = direction_at(
            lambda e: blocks[after][edge_at + e],
            lambda v: jnp.where(at_x == 0, v[cx, :, :cy], v[total - 1, :, :cy]),
        )
    else:
        z_next = direction_at(
            lambda e: blocks[after][edge_at + e], lambda v: v[after * cx, :, :cy]
        )
        z_last = direction_at(
            lambda e: blocks[before][edge_at + EDGE + e],
            lambda v: v[before * cx + cx - 1, :, :cy],
        )
    level_own = iota((cx, nz, cy), 1)
    around = []
    for k in range(3):
        z_out[k] = z_own[k]
        before_y, after_y = [], []
        for x in range(cx):
            left = pltpu.roll(z_side[k], (cy - 2 * x) % cy, 1) if x else z_side[k]
            right = pltpu.roll(z_side[k], (cy - 2 - 2 * x) % cy, 1)
            before_y.append(jnp.where(lane == 0, left, pltpu.roll(z_own[k][x], 1, 1)))
            after_y.append(
                jnp.where(lane == cy - 1, right, pltpu.roll(z_own[k][x], cy - 1, 1))
            )
        around.append(
            [
                jnp.concatenate([(z_last[k] * joined[width - 1])[None], z_own[k][:-1]], axis=0),
                jnp.concatenate([z_own[k][1:], (z_next[k] * joined[0])[None]], axis=0),
                jnp.stack(before_y),
                jnp.stack(after_y),
                jnp.where(level_own > 0, last_z(z_own[k]), 0.0),
                jnp.where(level_own < nz - 1, next_z(z_own[k]), 0.0),
            ]
        )
    along = jnp.zeros((nz, cy), f32)
    square = jnp.zeros((nz, cy), f32)
    for c in range(3):
        terms = [diag_ref[c, k] * z_own[k] for k in range(3)]
        terms += [off_ref[q, c, k] * around[k][q] for q in range(6) for k in range(3)]
        mapped = total_of(terms)
        along = along + jnp.sum(mapped * start[c][:cx, :, :cy], axis=0)
        square = square + jnp.sum(mapped * mapped, axis=0)
    along = jnp.sum(along, axis=0, keepdims=True)
    square = jnp.sum(square, axis=0, keepdims=True)
    pair = jnp.where(iota((2, cy), 0) == 0, along, square)
    sums_out[...] = jnp.broadcast_to(pair[None], sums_out.shape)


def after_kernel(sums_ref, z_ref, residual_ref, update_hbm, residual_hbm, update_out, sem, sems):
    copy = pltpu.make_async_copy(residual_ref, residual_hbm, sem)
    copy.start()
    pair = jnp.sum(sums_ref[...], axis=0)
    both = jnp.sum(pair, axis=1, keepdims=True)
    step = both[0:1] / both[1:2]
    copies = []
    for c in range(3):
        update_out[c] = z_ref[c] * step[None]
        copies.append(pltpu.make_async_copy(update_out.at[c], update_hbm.at[c], sems.at[c]))
        copies[-1].start()
    for each in [copy, *copies]:
        each.wait()


def other_pair(device, count_x, count_y):
    x, y = divmod(device, count_y)
    near = y + 1 if y % 2 else y - 1
    if 0 <= near < count_y:
        return x * count_y + near
    return (x ^ 1) * count_y + y if count_x % 2 == 0 else device


def body(
    pressure,
    saturation,
    saturation_old,
    pore_volume,
    permeability,
    jac_diag,
    jac_off,
    perf_cell,
    perf_well,
    perf_index,
    well_rate,
):
    count_x, count_y = lax.axis_size("gx"), lax.axis_size("gy")
    devices = count_x * count_y
    cx, nz, cy = pressure.shape
    wells = well_rate.shape[1] * count_y
    layers = 1 if count_x == 2 else 2
    columns_at, tiles = sent_tiles(cx, layers)[-2:]
    groups = -(-SEAM * 2 * cx // cy)
    offsets = window(count_x, cx)
    width = len(offsets)
    shape = jax.ShapeDtypeStruct
    whole = pl.BlockSpec(memory_space=pltpu.VMEM)
    anywhere = pl.BlockSpec(memory_space=pltpu.HBM)
    params = pltpu.CompilerParams(vmem_limit_bytes=32 * 1024 * 1024)

    fields = (pressure, saturation, saturation_old, pore_volume, permeability, jac_diag)
    perforations = (perf_cell, perf_well, perf_index, well_rate)
    wells_part, block, own, ya, yb, dinv, diag, off = pl.pallas_call(
        functools.partial(before_kernel, count_x, count_y),
        in_specs=[anywhere] * 11,
        out_specs=[anywhere, *[whole] * 7],
        out_shape=[
            pltpu.HBM((devices, 2, wells), f32),
            shape((tiles, nz, cy), f32),
            shape((BULK * cx + 2, nz, cy), f32),
            shape((cx + 1 + groups, nz, cy), f32),
            shape((max(cx + 1 + groups, 3 * cx), nz, cy), f32),
            shape((9, cx, nz, cy), f32),
            shape(jac_diag.shape, f32),
            shape(jac_off.shape, f32),
        ],
        scratch_shapes=[
            *[pltpu.VMEM(v.shape, v.dtype) for v in fields[:5]],
            *[pltpu.VMEM(v.shape, v.dtype) for v in perforations],
            pltpu.VMEM((devices, 2, wells), f32),
            pltpu.SemaphoreType.DMA((12,)),
        ],
        compiler_params=params,
        name="before",
    )(*[pltpu.with_memory_space_constraint(v, pltpu.HBM) for v in (*fields, jac_off, *perforations)])

    pairs = [(i, i ^ 1) for i in range(count_y)]
    others = [(i, other_pair(i, count_x, count_y)) for i in range(devices)]

    def from_x(values, offset):
        return lax.ppermute(
            values, "gx", [((i + offset) % count_x, i) for i in range(count_x)]
        )

    ya_got = lax.ppermute(ya, "gy", pairs)
    yb_got = lax.ppermute(yb, ("gx", "gy"), others)
    blocks = [from_x(block, o) for o in offsets[1:]]
    wells_all = lax.all_to_all(wells_part, ("gx", "gy"), 0, 0)
    ya_all = [ya_got] + [lax.ppermute(v[columns_at:], "gy", pairs) for v in blocks]
    yb_all = [yb_got] + [from_x(yb_got[: cx + 1], o) for o in offsets[1:]]

    residual, direction, sums = pl.pallas_call(
        functools.partial(main_kernel, count_x, count_y, tuple(offsets)),
        in_specs=[whole] * (4 + 3 * width),
        out_specs=[whole] * 3,
        out_shape=[
            shape((3, cx, nz, cy), f32),
            shape((3, cx, nz, cy), f32),
            shape((devices, 2, cy), f32),
        ],
        compiler_params=params,
        name="main",
    )(wells_all, diag, off, dinv, own, *blocks, *ya_all, *yb_all)

    sums_all = lax.all_to_all(sums, ("gx", "gy"), 0, 0)
    update, residual = pl.pallas_call(
        after_kernel,
        in_specs=[whole] * 3,
        out_specs=[anywhere] * 2,
        out_shape=[pltpu.HBM((3, cx, nz, cy), f32)] * 2,
        scratch_shapes=[
            pltpu.VMEM((3, cx, nz, cy), f32),
            pltpu.SemaphoreType.DMA,
            pltpu.SemaphoreType.DMA((3,)),
        ],
        compiler_params=params,
        name="after",
    )(sums_all, direction, residual)
    return (residual, update)


def solution(mesh):
    placed = (
        P("gx", None, "gy"),
        P(None, "gx", None, "gy"),
        P(None, "gx", None, "gy"),
        P("gx", None, "gy"),
        P("gx", None, "gy"),
        P(None, None, "gx", None, "gy"),
        P(None, None, None, "gx", None, "gy"),
        P("gx", "gy"),
        P("gx", "gy"),
        P("gx", "gy"),
        P("gx", "gy"),
    )
    return jax.shard_map(
        body,
        mesh=mesh,
        in_specs=placed,
        out_specs=(P(None, "gx", None, "gy"), P(None, "gx", None, "gy")),
        check_vma=False,
    )
```

```python
import functools

import jax
import jax.numpy as jnp
from jax import lax
from jax.experimental import pallas as pl
from jax.experimental.pallas import tpu as pltpu
from jax.sharding import PartitionSpec as P

SWEEPS = 4
WIDE = SWEEPS + 1

viscosity = (1.0, 2.0, 0.2)
vertical_ratio = 0.1
f32 = jnp.float32

PRESS, MOB, PERM, PART, INV, COEF = 0, 1, 4, 5, 8, 9
BULK = 15
FACE = 5
DINV, DCOL, OFFC, EPART, EPRESS, EPERM, EWATER, EGAS = 0, 9, 12, 30, 33, 34, 35, 36
EDGE = 37
SEAM = 30
BORDER_AT = (BULK * WIDE + 1) // 2 * 2
SUM, INNER = 7, 8
TINY = 1e-30
NT = (((1,), (1,)), ((), ()))
NN = (((1,), (0,)), ((), ()))


def iota(shape, axis):
    return lax.broadcasted_iota(jnp.int32, shape, axis)


def split_dot(values, hot, dims):
    rows = values.shape[0]
    high = values.astype(jnp.bfloat16)
    rest = values - high.astype(f32)
    mid = rest.astype(jnp.bfloat16)
    low = (rest - mid.astype(f32)).astype(jnp.bfloat16)
    parts = jnp.concatenate([high, mid, low], axis=0)
    out = lax.dot_general(parts, hot, dims, preferred_element_type=f32)
    return out[:rows] + (out[rows : 2 * rows] + out[2 * rows :])


def total_of(terms):
    while len(terms) > 1:
        paired = [a + b for a, b in zip(terms[::2], terms[1::2])]
        terms = paired + terms[len(terms) - len(terms) % 2 :]
    return terms[0]


def hot_of(condition):
    return jnp.where(condition, 1.0, 0.0).astype(jnp.bfloat16)


def sent_tiles(cx, layers):
    edges = INNER * (cx - layers)
    borders = edges + EDGE * layers
    return edges, borders, borders + 1, borders + 2, borders + 3 + cx


def mobilities(water, gas):
    oil = 1.0 - water - gas
    return [
        water * water / viscosity[0],
        oil * oil / viscosity[1],
        gas * gas / viscosity[2],
    ]


def face_flows(here, there, weight):
    conduct = weight * here[PERM] * there[PERM] / (here[PERM] + there[PERM] + TINY)
    drop = here[PRESS] - there[PRESS]
    flow = conduct * drop
    return [
        flow * jnp.where(drop >= 0.0, here[MOB + c], there[MOB + c]) for c in range(3)
    ]


def window(count, cx):
    reach = -(-WIDE // cx)
    if count <= 2 * reach + 1:
        return list(range(count))
    return list(range(reach + 1)) + list(range(-reach, 0))


def before_kernel(
    count_x,
    count_y,
    *refs,
):
    sources, (wells_hbm, block_out, own_out, ya_out, yb_out, dinv_out) = refs[:11], refs[11:17]
    diag_ref, off_ref = refs[17:19]
    press_ref, sat_ref, old_ref, pore_ref, perm_ref = refs[19:24]
    cell_ref, well_ref, index_ref, rate_ref, wells_out, sems = refs[24:]
    targets = (*refs[19:24], diag_ref, off_ref, *refs[24:28])
    copies = []
    for i in (1, 0, 7, 9, 8, 10, 4, 2, 3, 5, 6):
        copies.append(pltpu.make_async_copy(sources[i], targets[i], sems.at[i]))
        copies[-1].start()
    for copy in copies[:6]:
        copy.wait()
    cx, nz, cy = press_ref.shape
    at_x = lax.axis_index("gx")
    at_y = lax.axis_index("gy")
    layers = 1 if count_x == 2 else 2
    edge_at, border_at, last, columns_at, _ = sent_tiles(cx, layers)

    press = press_ref[...]
    water, gas = sat_ref[0], sat_ref[1]
    mobile = mobilities(water, gas)

    cells = cell_ref[...]
    perfs = cells.shape[1]
    spot_xz = lax.div(cells, cy)
    spot_y = lax.rem(cells, cy)
    stacked = jnp.concatenate([v.reshape(cx * nz, cy) for v in (water, gas, press)], axis=0)
    hot_y = hot_of(iota((cy, perfs), 0) == spot_y)
    picked = split_dot(stacked, hot_y, NN).reshape(3, cx * nz, perfs)
    on_xz = iota((cx * nz, perfs), 0) == spot_xz
    water_at, gas_at, press_at = (
        jnp.sum(jnp.where(on_xz, picked[i], 0.0), axis=0, keepdims=True) for i in range(3)
    )
    at_perf = [*mobilities(water_at, gas_at), press_at]
    index_vals = index_ref[...]
    parts = [index_vals * at_perf[i] for i in range(3)]
    strength = index_vals * (at_perf[0] + at_perf[1] + at_perf[2])
    weighted = strength * at_perf[3]
    row = iota((16, perfs), 0)
    both = jnp.where(row == 0, strength, jnp.where(row == 1, weighted, 0.0))
    wells = wells_out.shape[2]
    sums = split_dot(both, hot_of(iota((wells, perfs), 0) == well_ref[...]), NT)
    owned = rate_ref.shape[1]
    square = jnp.broadcast_to(rate_ref[...], (owned, owned))
    column = jnp.sum(
        jnp.where(iota((owned, owned), 0) == iota((owned, owned), 1), square, 0.0),
        axis=1,
        keepdims=True,
    )
    mine = iota((owned, wells), 1) == at_y * owned + iota((owned, wells), 0)
    rates = jnp.sum(jnp.where(mine, column, 0.0), axis=0, keepdims=True)
    pair = sums[:2] - jnp.where(iota((2, wells), 0) == 1, rates, 0.0)
    wells_out[...] = jnp.broadcast_to(pair[None], wells_out.shape)
    part_size = wells_out.shape[0] // 2
    wells_copies = [
        pltpu.make_async_copy(
            wells_out.at[pl.ds(i * part_size, part_size)],
            wells_hbm.at[pl.ds(i * part_size, part_size)],
            sems.at[11 + i],
        )
        for i in range(2)
    ]
    for each in wells_copies:
        each.start()

    perf_rows = [
        spot_xz.astype(f32),
        spot_y.astype(f32),
        well_ref[...].astype(f32),
        *parts,
        at_perf[3],
        jnp.zeros_like(at_perf[3]),
    ]
    for r, values in enumerate(perf_rows):
        block_out[last, r : r + 1, :] = values
        block_out[columns_at + cx, r : r + 1, :] = values
        own_out[BULK * cx, r : r + 1, :] = values
        ya_out[cx, r : r + 1, :] = values
        yb_out[cx, r : r + 1, :] = values

    for copy in copies[6:9]:
        copy.wait()
    perm = perm_ref[...]
    old_water, old_gas = old_ref[0], old_ref[1]
    oil, old_oil = 1.0 - water - gas, 1.0 - old_water - old_gas
    pore = pore_ref[...]
    part = [pore * (water - old_water), pore * (oil - old_oil), pore * (gas - old_gas)]
    layer_at = iota((cx, nz, cy), 1)
    lane_at = iota((cx, nz, cy), 2)
    cells_here = [press, *mobile, perm]
    flows = face_flows([v[:-1] for v in cells_here], [v[1:] for v in cells_here], 2.0)
    none = jnp.zeros((1, nz, cy), f32)
    for c in range(3):
        part[c] = part[c] + jnp.concatenate([flows[c], none], axis=0)
        part[c] = part[c] - jnp.concatenate([none, flows[c]], axis=0)
    for axis, weight, inside in (
        (2, 2.0, lane_at < cy - 1),
        (1, 2.0 * vertical_ratio, layer_at < nz - 1),
    ):
        size = cells_here[0].shape[axis]
        flows = face_flows(
            cells_here, [pltpu.roll(v, size - 1, axis) for v in cells_here], weight
        )
        for c in range(3):
            flow = jnp.where(inside, flows[c], 0.0)
            part[c] = part[c] + flow - pltpu.roll(flow, 1, axis)

    lane = iota((nz, cy), 1)
    to_left = [jnp.zeros((nz, cy), f32) for _ in range(cx)]
    to_right = [jnp.zeros((nz, cy), f32) for _ in range(cx)]
    beside = [jnp.zeros((nz, cy), f32) for _ in range(0, SEAM, cy // (2 * cx))]

    def put_bulk(f, values):
        own_out[f * cx : (f + 1) * cx] = values
        shift = f * WIDE
        on_left = (lane >= shift) & (lane < shift + WIDE)
        start = (shift - WIDE) % cy
        on_right = (lane >= start) & (lane < start + WIDE)
        for x in range(cx):
            turned = pltpu.roll(values[x], shift, 1) if shift else values[x]
            to_left[x] = jnp.where(on_left, turned, to_left[x])
            to_right[x] = jnp.where(on_right, turned, to_right[x])

    def put_edge(e, values):
        if layers == 1:
            block_out[edge_at + e] = jnp.where(at_x == 0, values[cx - 1], values[0])
        else:
            block_out[edge_at + e] = values[0]
            block_out[edge_at + EDGE + e] = values[cx - 1]
        if e < SEAM:
            group, place = divmod(e, cy // (2 * cx))
            for x in range(cx):
                at = 2 * (place * cx + x) + 1
                here = (lane == at - 1) | (lane == at)
                beside[group] = jnp.where(here, pltpu.roll(values[x], at, 1), beside[group])

    def put_inner(i, values):
        for x in range(cx - layers):
            at = i * (cx - layers) + x
            if layers == 1:
                block_out[at] = jnp.where(at_x == 0, values[x], values[x + 1])
            else:
                block_out[at] = values[x + 1]

    border = jnp.zeros((nz, cy), f32)
    for f in range(FACE):
        for x in range(cx):
            at = BORDER_AT + 2 * (f * cx + x) + 1
            first = pltpu.roll(cells_here[f][x], at - 1, 1)
            second = pltpu.roll(cells_here[f][x], at + 1, 1)
            border = jnp.where(lane == at - 1, first, jnp.where(lane == at, second, border))
    block_out[border_at] = border
    own_out[BULK * cx + 1] = border
    to_left[0] = to_right[0] = border
    for f, values in enumerate([*cells_here, *part]):
        put_bulk(f, values)
    for e, values in enumerate([*part, press, perm, water, gas]):
        put_edge(EPART + e, values)
    put_inner(SUM, part[0] + part[1] + part[2])

    copies[9].wait()
    copies[10].wait()
    diag = [[diag_ref[a, b] for b in range(3)] for a in range(3)]
    inverse = 1.0 / (diag[0][0] + diag[1][0] + diag[2][0])
    put_bulk(INV, inverse)
    put_inner(6, inverse)

    def cofactor(a, b):
        return (
            diag[(a + 1) % 3][(b + 1) % 3] * diag[(a + 2) % 3][(b + 2) % 3]
            - diag[(a + 1) % 3][(b + 2) % 3] * diag[(a + 2) % 3][(b + 1) % 3]
        )

    cofactors = [[cofactor(a, b) for b in range(3)] for a in range(3)]
    over = 1.0 / (
        diag[0][0] * cofactors[0][0] + diag[0][1] * cofactors[0][1] + diag[0][2] * cofactors[0][2]
    )
    for a in range(3):
        put_edge(DCOL + a, diag[a][0])
        for b in range(3):
            solve = cofactors[b][a] * over
            dinv_out[3 * a + b] = solve
            put_edge(DINV + 3 * a + b, solve)

    for q in range(6):
        columns = [off_ref[q, c, 0] for c in range(3)]
        if q == 4:
            columns = [jnp.where(layer_at > 0, v, 0.0) for v in columns]
        if q == 5:
            columns = [jnp.where(layer_at < nz - 1, v, 0.0) for v in columns]
        coef = (columns[0] + columns[1] + columns[2]) * inverse
        put_bulk(COEF + q, coef)
        put_inner(q, coef)
        for c in range(3):
            put_edge(OFFC + 3 * q + c, columns[c])

    even = lax.rem(at_y, 2) == 0
    for x in range(cx):
        ya_out[x] = jnp.where(even, to_right[x], to_left[x])
        yb_out[x] = jnp.where(even, to_left[x], to_right[x])
        block_out[columns_at + x] = ya_out[x]
    for t, values in enumerate(beside):
        ya_out[cx + 1 + t] = values
        yb_out[cx + 1 + t] = values
    for spare in range(cx + 1 + len(beside), yb_out.shape[0]):
        yb_out[spare] = jnp.zeros((nz, cy), f32)
    for each in wells_copies:
        each.wait()


def main_kernel(count_x, count_y, offsets, *refs):
    width = len(offsets)
    (wells_ref, diag_ref, off_ref, dinv_ref, own_ref), refs = refs[:5], refs[5:]
    blocks, refs = (None, *refs[: width - 1]), refs[width - 1 :]
    ya_refs, refs = refs[:width], refs[width:]
    yb_refs, refs = refs[:width], refs[width:]
    residual_out, z_out, sums_out = refs

    cx, nz, cy = residual_out.shape[1:]
    total = width * cx
    at_x = lax.axis_index("gx")
    at_y = lax.axis_index("gy")
    even = lax.rem(at_y, 2) == 0
    has_left = jnp.where(at_y > 0, 1.0, 0.0).astype(f32)
    has_right = jnp.where(at_y < count_y - 1, 1.0, 0.0).astype(f32)
    layers = 1 if count_x == 2 else 2
    edge_at, border_at, last, columns_at, _ = sent_tiles(cx, layers)
    index_x = [lax.rem(at_x + (o % count_x), count_x) for o in offsets]
    joined = [
        jnp.where(index_x[(j + 1) % width] == index_x[j] + 1, 1.0, 0.0).astype(f32)
        for j in range(width)
    ]

    from_left, from_right = [], []
    for j in range(width):
        first, second = ya_refs[j][: cx + 1], yb_refs[j][: cx + 1]
        from_right.append(jnp.where(even, first, second) * has_right)
        from_left.append(jnp.where(even, second, first) * has_left)
    lane = iota((nz, cy), 1)

    merged = []
    for parity in range(2):
        of_right = lane < 0
        for f in range(parity, BULK, 2):
            of_right = of_right | ((lane >= f * WIDE) & (lane < (f + 1) * WIDE))
        merged.append(
            [
                jnp.where(of_right, from_right[j][x], from_left[j][x])
                for j in range(width)
                for x in range(cx)
            ]
        )

    def halo(f, x):
        tile = merged[f % 2][x]
        return pltpu.roll(tile, cy - f * WIDE, 1) if f else tile

    def arranged(edges, inner):
        if layers == 2:
            return jnp.stack([edges[0], *inner, edges[1]])
        first = [edges[0], *inner]
        second = [*inner, edges[0]]
        return jnp.stack([jnp.where(at_x == 0, a, b) for a, b in zip(first, second)])

    def received(j):
        block = blocks[j]
        edges = [
            [block[edge_at + side * EDGE + e] for e in range(EDGE)] for side in range(layers)
        ]
        inner = [
            [block[i * (cx - layers) + x] for x in range(cx - layers)] for i in range(INNER)
        ]
        zero = jnp.zeros((nz, cy), f32)
        part = [
            arranged(
                [edge[EPART + c] for edge in edges], inner[SUM] if c == 0 else [zero] * (cx - layers)
            )
            for c in range(3)
        ]
        scale = [1.0 / (edge[DCOL] + edge[DCOL + 1] + edge[DCOL + 2]) for edge in edges]
        coefs = [
            arranged(
                [
                    (edge[OFFC + 3 * q] + edge[OFFC + 3 * q + 1] + edge[OFFC + 3 * q + 2]) * by
                    for edge, by in zip(edges, scale)
                ],
                inner[q],
            )
            for q in range(6)
        ]
        return dict(enumerate([*part, arranged(scale, inner[6]), *coefs], start=PART))

    others = [received(j) for j in range(1, width)]

    def extended(f):
        own = jnp.concatenate(
            [own_ref[f * cx : (f + 1) * cx], *[other[f] for other in others]], axis=0
        )
        side = jnp.stack([halo(f, x) for x in range(total)])
        return jnp.concatenate([own, side], axis=2)

    lanes = 2 * cy
    level = iota((total, nz, lanes), 1)

    def next_x(v):
        return jnp.concatenate([v[1:], v[:1]], axis=0)

    def last_x(v):
        return jnp.concatenate([v[-1:], v[:-1]], axis=0)

    def next_y(v):
        return pltpu.roll(v, v.shape[2] - 1, 2)

    def last_y(v):
        return pltpu.roll(v, 1, 2)

    def next_z(v):
        return pltpu.roll(v, nz - 1, 1)

    def last_z(v):
        return pltpu.roll(v, 1, 1)

    def seam_after(v):
        rows = [v[i] for i in range(total)]
        for j in range(width):
            rows[j * cx + cx - 1] = rows[j * cx + cx - 1] * joined[j]
        return jnp.stack(rows)

    def seam_before(v):
        rows = [v[i] for i in range(total)]
        for j in range(width):
            at = ((j + 1) % width) * cx
            rows[at] = rows[at] * joined[j]
        return jnp.stack(rows)

    resid = [extended(PART + c) for c in range(3)]
    rows = [[resid[c][x] for x in range(total)] for c in range(3)]
    sides = {}

    def side_of(f, x):
        if (f, x) not in sides:
            sides[f, x] = halo(f, x)
        return sides[f, x]

    even_lane = lane % 2 == 0
    ends = (lane == 0) | (lane == cy - 1)
    for j in range(width):
        border = blocks[j][border_at] if j else own_ref[BULK * cx + 1]
        beyond = jnp.where(
            even_lane, pltpu.roll(from_left[j][0], cy - 1, 1), pltpu.roll(from_right[j][0], 1, 1)
        )
        backs = [cy - BORDER_AT - 2 * f * cx for f in range(FACE)]
        flows = face_flows(
            [pltpu.roll(beyond, back, 1) for back in backs],
            [pltpu.roll(border, back, 1) for back in backs],
            2.0,
        )
        for c in range(3):
            flow = jnp.where(lane < 2 * cx, flows[c], 0.0)
            swapped = jnp.where(even_lane, pltpu.roll(flow, cy - 1, 1), pltpu.roll(flow, 1, 1))
            for x in range(cx):
                back = cy - 2 * x - 1
                inward = jnp.where(ends, pltpu.roll(swapped, back, 1), 0.0)
                outward = jnp.where(ends, pltpu.roll(flow, back, 1), 0.0)
                at = j * cx + x
                rows[c][at] = rows[c][at] + jnp.concatenate([-inward, outward], axis=1)

    def edge_cells(j, last_layer):
        x = cx - 1 if last_layer else 0
        if j == 0:
            inside = [own_ref[f * cx + x] for f in range(FACE)]
        else:
            at = edge_at + (EDGE if last_layer and layers == 2 else 0)
            water, gas = blocks[j][at + EWATER], blocks[j][at + EGAS]
            inside = [
                blocks[j][at + EPRESS],
                *mobilities(water, gas),
                blocks[j][at + EPERM],
            ]
        return [
            jnp.concatenate([inside[f], side_of(f, j * cx + x)], axis=1) for f in range(FACE)
        ]

    for j in range(width):
        after = (j + 1) % width
        flows = face_flows(edge_cells(j, True), edge_cells(after, False), 2.0 * joined[j])
        for c in range(3):
            near_x, far_x = j * cx + cx - 1, after * cx
            rows[c][near_x] = rows[c][near_x] + flows[c]
            rows[c][far_x] = rows[c][far_x] - flows[c]
    resid = [jnp.stack(rows[c]) for c in range(3)]

    wells = wells_ref.shape[2]
    perfs = own_ref.shape[2]
    added = [[] for _ in range(3)]
    holes = jnp.zeros((16, wells), f32)
    lists = []
    for j in range(width):
        pair = jnp.sum(wells_ref[pl.ds(index_x[j] * count_y, count_y)], axis=0)
        holes = jnp.where(iota((16, wells), 0) == j, pair[1:2] / pair[0:1], holes)
        lists += [
            blocks[j][last] if j else own_ref[BULK * cx],
            from_left[j][cx],
            from_right[j][cx],
        ]
    listed = jnp.concatenate(lists, axis=1)
    number = iota((wells, perfs), 0).astype(f32)
    holes_at = jnp.concatenate(
        [split_dot(holes, hot_of(number == v[2:3]), NN) for v in lists], axis=1
    )
    for j in range(width):
        tiles = listed[:, 3 * perfs * j : 3 * perfs * (j + 1)]
        spot_xz, spot_y = tiles[0:1], tiles[1:2]
        fall = tiles[6:7] - holes_at[j : j + 1, 3 * perfs * j : 3 * perfs * (j + 1)]
        on_xz = iota((cx * nz, 3 * perfs), 0).astype(f32) == spot_xz
        spread = jnp.concatenate(
            [jnp.where(on_xz, tiles[3 + c : 4 + c] * fall, 0.0) for c in range(3)], axis=0
        )
        hot_y = iota((cy, 3 * perfs), 0).astype(f32) == spot_y
        nearby = iota((cy, 3 * perfs), 0)
        source = iota((cy, 3 * perfs), 1)
        kept = jnp.where(
            source < 2 * perfs, jnp.where(nearby >= cy - WIDE, 1, 0), jnp.where(nearby < WIDE, 1, 0)
        )
        hot_side = hot_of(hot_y & (kept == 1))
        inner = split_dot(spread[:, :perfs], hot_of(hot_y[:, :perfs]), NT)
        inner = inner.reshape(3, cx, nz, cy)
        aside = spread[:, perfs:]
        if j:
            aside = aside.reshape(3, cx * nz, 2 * perfs)
            aside = aside[0] + aside[1] + aside[2]
        outer = split_dot(aside, hot_side[:, perfs:], NT).reshape(-1, cx, nz, cy)
        for c in range(3):
            side = outer[c] if c < outer.shape[0] else jnp.zeros_like(outer[0])
            added[c].append(jnp.concatenate([inner[c], side], axis=2))
    start = [-(resid[c] + jnp.concatenate(added[c], axis=0)) for c in range(3)]
    for c in range(3):
        residual_out[c] = -start[c][:cx, :, :cy]

    coefs = [extended(COEF + q) for q in range(6)]
    coefs[0] = seam_before(coefs[0])
    coefs[1] = seam_after(coefs[1])
    scaled = (start[0] + start[1] + start[2]) * extended(INV)
    steps = (last_x, next_x, last_y, next_y, last_z, next_z)
    part = scaled
    for _ in range(1, SWEEPS):
        along_x, along_y, along_z = (
            coefs[q] * steps[q](part) + coefs[q + 1] * steps[q + 1](part) for q in (0, 2, 4)
        )
        part = (scaled - along_x) - (along_z + along_y)

    near = [step(part) for step in steps]
    near[0] = seam_before(near[0])
    near[1] = seam_after(near[1])
    near[4] = jnp.where(level > 0, near[4], 0.0)
    near[5] = jnp.where(level < nz - 1, near[5], 0.0)

    def direction(edge_of, here, around, initial):
        rest = []
        for c in range(3):
            coupled = [edge_of(OFFC + 3 * q + c) * beyond for q, beyond in enumerate(around)]
            rest.append(initial[c] - total_of([edge_of(DCOL + c) * here, *coupled]))
        solved = []
        for a in range(3):
            value = edge_of(DINV + 3 * a) * rest[0]
            value = value + edge_of(DINV + 3 * a + 1) * rest[1]
            solved.append(value + edge_of(DINV + 3 * a + 2) * rest[2])
        solved[0] = solved[0] + here
        return solved

    def edge_own(e):
        if e < DCOL:
            return dinv_ref[e]
        if e < OFFC:
            return diag_ref[e - DCOL, 0]
        return off_ref[(e - OFFC) // 3, (e - OFFC) % 3, 0]

    beside = []
    for t in range(cx + 1, cx + 1 - (-SEAM * 2 * cx // cy)):
        one, two = ya_refs[0][t], yb_refs[0][t]
        left, right = jnp.where(even, two, one) * has_left, jnp.where(even, one, two) * has_right
        beside.append(jnp.where(even_lane, left, right))

    def edge_side(e):
        tile, place = divmod(2 * cx * e, cy)
        return pltpu.roll(beside[tile], cy - place, 1) if place else beside[tile]

    def packed(tiles, shift):
        result = jnp.zeros((nz, cy), f32)
        for x in range(cx):
            turned = pltpu.roll(tiles[x], (2 * x + shift) % cy, 1)
            result = jnp.where((lane >= 2 * x) & (lane < 2 * x + 2), turned, result)
        return result

    inside = [part[x, :, :cy] for x in range(cx)]
    outside = [part[x, :, cy:] for x in range(cx)]
    here = packed(outside, 1)
    depth = iota((nz, cy), 0)
    z_side = direction(
        edge_side,
        here,
        [
            packed([part[total - 1, :, cy:] * joined[width - 1], *outside[:-1]], 1),
            packed([*outside[1:], part[cx % total, :, cy:] * joined[0]], 1),
            packed([jnp.where(lane == cy - 1, a, b) for a, b in zip(inside, outside)], 2),
            packed([jnp.where(lane == 0, a, b) for a, b in zip(inside, outside)], 0),
            jnp.where(depth > 0, pltpu.roll(here, 1, 0), 0.0),
            jnp.where(depth < nz - 1, pltpu.roll(here, nz - 1, 0), 0.0),
        ],
        [packed([start[c][x, :, cy:] for x in range(cx)], 1) for c in range(3)],
    )

    def direction_at(edge_of, where):
        return direction(
            edge_of, where(part), [where(v) for v in near], [where(v) for v in start]
        )

    after, before = 1 % width, width - 1
    z_own = direction_at(edge_own, lambda v: v[:cx, :, :cy])
    if layers == 1:
        z_next = z_last = direction_at(
            lambda e: blocks[after][edge_at + e],
            lambda v: jnp.where(at_x == 0, v[cx, :, :cy], v[total - 1, :, :cy]),
        )
    else:
        z_next = direction_at(
            lambda e: blocks[after][edge_at + e], lambda v: v[after * cx, :, :cy]
        )
        z_last = direction_at(
            lambda e: blocks[before][edge_at + EDGE + e],
            lambda v: v[before * cx + cx - 1, :, :cy],
        )
    level_own = iota((cx, nz, cy), 1)
    around = []
    for k in range(3):
        z_out[k] = z_own[k]
        before_y, after_y = [], []
        for x in range(cx):
            left = pltpu.roll(z_side[k], (cy - 2 * x) % cy, 1) if x else z_side[k]
            right = pltpu.roll(z_side[k], (cy - 2 - 2 * x) % cy, 1)
            before_y.append(jnp.where(lane == 0, left, pltpu.roll(z_own[k][x], 1, 1)))
            after_y.append(
                jnp.where(lane == cy - 1, right, pltpu.roll(z_own[k][x], cy - 1, 1))
            )
        around.append(
            [
                jnp.concatenate([(z_last[k] * joined[width - 1])[None], z_own[k][:-1]], axis=0),
                jnp.concatenate([z_own[k][1:], (z_next[k] * joined[0])[None]], axis=0),
                jnp.stack(before_y),
                jnp.stack(after_y),
                jnp.where(level_own > 0, last_z(z_own[k]), 0.0),
                jnp.where(level_own < nz - 1, next_z(z_own[k]), 0.0),
            ]
        )
    along = jnp.zeros((nz, cy), f32)
    square = jnp.zeros((nz, cy), f32)
    for c in range(3):
        terms = [diag_ref[c, k] * z_own[k] for k in range(3)]
        terms += [off_ref[q, c, k] * around[k][q] for q in range(6) for k in range(3)]
        mapped = total_of(terms)
        along = along + jnp.sum(mapped * start[c][:cx, :, :cy], axis=0)
        square = square + jnp.sum(mapped * mapped, axis=0)
    along = jnp.sum(along, axis=0, keepdims=True)
    square = jnp.sum(square, axis=0, keepdims=True)
    pair = jnp.where(iota((2, cy), 0) == 0, along, square)
    sums_out[...] = jnp.broadcast_to(pair[None], sums_out.shape)


def after_kernel(sums_ref, z_ref, residual_ref, update_hbm, residual_hbm, update_out, sem, sems):
    copy = pltpu.make_async_copy(residual_ref, residual_hbm, sem)
    copy.start()
    pair = jnp.sum(sums_ref[...], axis=0)
    both = jnp.sum(pair, axis=1, keepdims=True)
    step = both[0:1] / both[1:2]
    copies = []
    for c in range(3):
        update_out[c] = z_ref[c] * step[None]
        copies.append(pltpu.make_async_copy(update_out.at[c], update_hbm.at[c], sems.at[c]))
        copies[-1].start()
    for each in [copy, *copies]:
        each.wait()


def other_pair(device, count_x, count_y):
    x, y = divmod(device, count_y)
    near = y + 1 if y % 2 else y - 1
    if 0 <= near < count_y:
        return x * count_y + near
    return (x ^ 1) * count_y + y if count_x % 2 == 0 else device


def body(
    pressure,
    saturation,
    saturation_old,
    pore_volume,
    permeability,
    jac_diag,
    jac_off,
    perf_cell,
    perf_well,
    perf_index,
    well_rate,
):
    count_x, count_y = lax.axis_size("gx"), lax.axis_size("gy")
    devices = count_x * count_y
    cx, nz, cy = pressure.shape
    wells = well_rate.shape[1] * count_y
    layers = 1 if count_x == 2 else 2
    columns_at, tiles = sent_tiles(cx, layers)[-2:]
    groups = -(-SEAM * 2 * cx // cy)
    offsets = window(count_x, cx)
    width = len(offsets)
    shape = jax.ShapeDtypeStruct
    whole = pl.BlockSpec(memory_space=pltpu.VMEM)
    anywhere = pl.BlockSpec(memory_space=pltpu.HBM)
    params = pltpu.CompilerParams(vmem_limit_bytes=32 * 1024 * 1024)

    fields = (pressure, saturation, saturation_old, pore_volume, permeability, jac_diag)
    perforations = (perf_cell, perf_well, perf_index, well_rate)
    wells_part, block, own, ya, yb, dinv, diag, off = pl.pallas_call(
        functools.partial(before_kernel, count_x, count_y),
        in_specs=[anywhere] * 11,
        out_specs=[anywhere, *[whole] * 7],
        out_shape=[
            pltpu.HBM((devices, 2, wells), f32),
            shape((tiles, nz, cy), f32),
            shape((BULK * cx + 2, nz, cy), f32),
            shape((cx + 1 + groups, nz, cy), f32),
            shape((max(cx + 1 + groups, 2 * cx), nz, cy), f32),
            shape((9, cx, nz, cy), f32),
            shape(jac_diag.shape, f32),
            shape(jac_off.shape, f32),
        ],
        scratch_shapes=[
            *[pltpu.VMEM(v.shape, v.dtype) for v in fields[:5]],
            *[pltpu.VMEM(v.shape, v.dtype) for v in perforations],
            pltpu.VMEM((devices, 2, wells), f32),
            pltpu.SemaphoreType.DMA((13,)),
        ],
        compiler_params=params,
        name="before",
    )(*[pltpu.with_memory_space_constraint(v, pltpu.HBM) for v in (*fields, jac_off, *perforations)])

    pairs = [(i, i ^ 1) for i in range(count_y)]
    others = [(i, other_pair(i, count_x, count_y)) for i in range(devices)]

    def from_x(values, offset):
        return lax.ppermute(
            values, "gx", [((i + offset) % count_x, i) for i in range(count_x)]
        )

    ya_got = lax.ppermute(ya, "gy", pairs)
    yb_got = lax.ppermute(yb, ("gx", "gy"), others)
    blocks = [from_x(block, o) for o in offsets[1:]]
    wells_all = lax.all_to_all(wells_part, ("gx", "gy"), 0, 0)
    ya_all = [ya_got] + [lax.ppermute(v[columns_at:], "gy", pairs) for v in blocks]
    yb_all = [yb_got] + [from_x(yb_got, o) for o in offsets[1:]]

    residual, direction, sums = pl.pallas_call(
        functools.partial(main_kernel, count_x, count_y, tuple(offsets)),
        in_specs=[whole] * (4 + 3 * width),
        out_specs=[whole] * 3,
        out_shape=[
            shape((3, cx, nz, cy), f32),
            shape((3, cx, nz, cy), f32),
            shape((devices, 2, cy), f32),
        ],
        compiler_params=params,
        name="main",
    )(wells_all, diag, off, dinv, own, *blocks, *ya_all, *yb_all)

    sums_all = lax.all_to_all(sums, ("gx", "gy"), 0, 0)
    update, residual = pl.pallas_call(
        after_kernel,
        in_specs=[whole] * 3,
        out_specs=[anywhere] * 2,
        out_shape=[pltpu.HBM((3, cx, nz, cy), f32)] * 2,
        scratch_shapes=[
            pltpu.VMEM((3, cx, nz, cy), f32),
            pltpu.SemaphoreType.DMA,
            pltpu.SemaphoreType.DMA((3,)),
        ],
        compiler_params=params,
        name="after",
    )(sums_all, direction, residual)
    return (residual, update)


def solution(mesh):
    placed = (
        P("gx", None, "gy"),
        P(None, "gx", None, "gy"),
        P(None, "gx", None, "gy"),
        P("gx", None, "gy"),
        P("gx", None, "gy"),
        P(None, None, "gx", None, "gy"),
        P(None, None, None, "gx", None, "gy"),
        P("gx", "gy"),
        P("gx", "gy"),
        P("gx", "gy"),
        P("gx", "gy"),
    )
    return jax.shard_map(
        body,
        mesh=mesh,
        in_specs=placed,
        out_specs=(P(None, "gx", None, "gy"), P(None, "gx", None, "gy")),
        check_vma=False,
    )
```

```python
import functools

import jax
import jax.numpy as jnp
from jax import lax
from jax.experimental import pallas as pl
from jax.experimental.pallas import tpu as pltpu
from jax.sharding import PartitionSpec as P

SWEEPS = 4
WIDE = SWEEPS + 1

viscosity = (1.0, 2.0, 0.2)
vertical_ratio = 0.1
f32 = jnp.float32

PRESS, MOB, PERM, PART, INV, COEF = 0, 1, 4, 5, 8, 9
BULK = 15
FACE = 5
DINV, DCOL, OFFC, EPART, EPRESS, EPERM, EWATER, EGAS = 0, 9, 12, 30, 33, 34, 35, 36
EDGE = 37
SEAM = 30
BORDER_AT = (BULK * WIDE + 1) // 2 * 2
SUM, INNER = 7, 8
TINY = 1e-30
NT = (((1,), (1,)), ((), ()))
NN = (((1,), (0,)), ((), ()))


def iota(shape, axis):
    return lax.broadcasted_iota(jnp.int32, shape, axis)


def split_dot(values, hot, dims):
    rows = values.shape[0]
    high = values.astype(jnp.bfloat16)
    rest = values - high.astype(f32)
    mid = rest.astype(jnp.bfloat16)
    low = (rest - mid.astype(f32)).astype(jnp.bfloat16)
    parts = jnp.concatenate([high, mid, low], axis=0)
    out = lax.dot_general(parts, hot, dims, preferred_element_type=f32)
    return out[:rows] + (out[rows : 2 * rows] + out[2 * rows :])


def total_of(terms):
    while len(terms) > 1:
        paired = [a + b for a, b in zip(terms[::2], terms[1::2])]
        terms = paired + terms[len(terms) - len(terms) % 2 :]
    return terms[0]


def hot_of(condition):
    return jnp.where(condition, 1.0, 0.0).astype(jnp.bfloat16)


def sent_tiles(cx, layers):
    edges = INNER * (cx - layers)
    borders = edges + EDGE * layers
    return edges, borders, borders + 1, borders + 2, borders + 3 + cx


def mobilities(water, gas):
    oil = 1.0 - water - gas
    return [
        water * water / viscosity[0],
        oil * oil / viscosity[1],
        gas * gas / viscosity[2],
    ]


def face_flows(here, there, weight):
    conduct = weight * here[PERM] * there[PERM] / (here[PERM] + there[PERM] + TINY)
    drop = here[PRESS] - there[PRESS]
    flow = conduct * drop
    return [
        flow * jnp.where(drop >= 0.0, here[MOB + c], there[MOB + c]) for c in range(3)
    ]


def window(count, cx):
    reach = -(-WIDE // cx)
    if count <= 2 * reach + 1:
        return list(range(count))
    return list(range(reach + 1)) + list(range(-reach, 0))


def before_kernel(
    count_x,
    count_y,
    *refs,
):
    sources, (wells_hbm, block_out, own_out, ya_out, yb_out, dinv_out) = refs[:11], refs[11:17]
    diag_ref, off_ref = refs[17:19]
    press_ref, sat_ref, old_ref, pore_ref, perm_ref = refs[19:24]
    cell_ref, well_ref, index_ref, rate_ref, wells_out, sems = refs[24:]
    targets = (*refs[19:24], diag_ref, off_ref, *refs[24:28])
    copies = []
    for i in (1, 0, 7, 9, 8, 10, 4, 2, 3, 5, 6):
        copies.append(pltpu.make_async_copy(sources[i], targets[i], sems.at[i]))
        copies[-1].start()
    for copy in copies[:6]:
        copy.wait()
    cx, nz, cy = press_ref.shape
    at_x = lax.axis_index("gx")
    at_y = lax.axis_index("gy")
    layers = 1 if count_x == 2 else 2
    edge_at, border_at, last, columns_at, _ = sent_tiles(cx, layers)

    press = press_ref[...]
    water, gas = sat_ref[0], sat_ref[1]
    mobile = mobilities(water, gas)

    cells = cell_ref[...]
    perfs = cells.shape[1]
    spot_xz = lax.div(cells, cy)
    spot_y = lax.rem(cells, cy)
    stacked = jnp.concatenate([v.reshape(cx * nz, cy) for v in (water, gas, press)], axis=0)
    hot_y = hot_of(iota((cy, perfs), 0) == spot_y)
    picked = split_dot(stacked, hot_y, NN).reshape(3, cx * nz, perfs)
    on_xz = iota((cx * nz, perfs), 0) == spot_xz
    water_at, gas_at, press_at = (
        jnp.sum(jnp.where(on_xz, picked[i], 0.0), axis=0, keepdims=True) for i in range(3)
    )
    at_perf = [*mobilities(water_at, gas_at), press_at]
    index_vals = index_ref[...]
    parts = [index_vals * at_perf[i] for i in range(3)]
    strength = index_vals * (at_perf[0] + at_perf[1] + at_perf[2])
    weighted = strength * at_perf[3]
    row = iota((16, perfs), 0)
    both = jnp.where(row == 0, strength, jnp.where(row == 1, weighted, 0.0))
    wells = wells_out.shape[2]
    sums = split_dot(both, hot_of(iota((wells, perfs), 0) == well_ref[...]), NT)
    owned = rate_ref.shape[1]
    square = jnp.broadcast_to(rate_ref[...], (owned, owned))
    column = jnp.sum(
        jnp.where(iota((owned, owned), 0) == iota((owned, owned), 1), square, 0.0),
        axis=1,
        keepdims=True,
    )
    mine = iota((owned, wells), 1) == at_y * owned + iota((owned, wells), 0)
    rates = jnp.sum(jnp.where(mine, column, 0.0), axis=0, keepdims=True)
    pair = sums[:2] - jnp.where(iota((2, wells), 0) == 1, rates, 0.0)
    wells_out[...] = jnp.broadcast_to(pair[None], wells_out.shape)
    part_size = wells_out.shape[0] // 2
    wells_copies = [
        pltpu.make_async_copy(
            wells_out.at[pl.ds(i * part_size, part_size)],
            wells_hbm.at[pl.ds(i * part_size, part_size)],
            sems.at[11 + i],
        )
        for i in range(2)
    ]
    for each in wells_copies:
        each.start()

    perf_rows = [
        spot_xz.astype(f32),
        spot_y.astype(f32),
        well_ref[...].astype(f32),
        *parts,
        at_perf[3],
        jnp.zeros_like(at_perf[3]),
    ]
    for r, values in enumerate(perf_rows):
        block_out[last, r : r + 1, :] = values
        block_out[columns_at + cx, r : r + 1, :] = values
        own_out[BULK * cx, r : r + 1, :] = values
        ya_out[cx, r : r + 1, :] = values
        yb_out[cx, r : r + 1, :] = values

    for copy in copies[6:9]:
        copy.wait()
    perm = perm_ref[...]
    old_water, old_gas = old_ref[0], old_ref[1]
    oil, old_oil = 1.0 - water - gas, 1.0 - old_water - old_gas
    pore = pore_ref[...]
    part = [pore * (water - old_water), pore * (oil - old_oil), pore * (gas - old_gas)]
    layer_at = iota((cx, nz, cy), 1)
    lane_at = iota((cx, nz, cy), 2)
    cells_here = [press, *mobile, perm]
    flows = face_flows([v[:-1] for v in cells_here], [v[1:] for v in cells_here], 2.0)
    none = jnp.zeros((1, nz, cy), f32)
    for c in range(3):
        part[c] = part[c] + jnp.concatenate([flows[c], none], axis=0)
        part[c] = part[c] - jnp.concatenate([none, flows[c]], axis=0)
    for axis, weight, inside in (
        (2, 2.0, lane_at < cy - 1),
        (1, 2.0 * vertical_ratio, layer_at < nz - 1),
    ):
        size = cells_here[0].shape[axis]
        flows = face_flows(
            cells_here, [pltpu.roll(v, size - 1, axis) for v in cells_here], weight
        )
        for c in range(3):
            flow = jnp.where(inside, flows[c], 0.0)
            part[c] = part[c] + flow - pltpu.roll(flow, 1, axis)

    lane = iota((nz, cy), 1)
    to_left = [jnp.zeros((nz, cy), f32) for _ in range(cx)]
    to_right = [jnp.zeros((nz, cy), f32) for _ in range(cx)]
    beside = [jnp.zeros((nz, cy), f32) for _ in range(0, SEAM, cy // (2 * cx))]

    def put_bulk(f, values):
        own_out[f * cx : (f + 1) * cx] = values
        shift = f * WIDE
        on_left = (lane >= shift) & (lane < shift + WIDE)
        start = (shift - WIDE) % cy
        on_right = (lane >= start) & (lane < start + WIDE)
        for x in range(cx):
            turned = pltpu.roll(values[x], shift, 1) if shift else values[x]
            to_left[x] = jnp.where(on_left, turned, to_left[x])
            to_right[x] = jnp.where(on_right, turned, to_right[x])

    def put_edge(e, values):
        if layers == 1:
            block_out[edge_at + e] = jnp.where(at_x == 0, values[cx - 1], values[0])
        else:
            block_out[edge_at + e] = values[0]
            block_out[edge_at + EDGE + e] = values[cx - 1]
        if e < SEAM:
            group, place = divmod(e, cy // (2 * cx))
            for x in range(cx):
                at = 2 * (place * cx + x) + 1
                here = (lane == at - 1) | (lane == at)
                beside[group] = jnp.where(here, pltpu.roll(values[x], at, 1), beside[group])

    def put_inner(i, values):
        for x in range(cx - layers):
            at = i * (cx - layers) + x
            if layers == 1:
                block_out[at] = jnp.where(at_x == 0, values[x], values[x + 1])
            else:
                block_out[at] = values[x + 1]

    border = jnp.zeros((nz, cy), f32)
    for f in range(FACE):
        for x in range(cx):
            at = BORDER_AT + 2 * (f * cx + x) + 1
            first = pltpu.roll(cells_here[f][x], at - 1, 1)
            second = pltpu.roll(cells_here[f][x], at + 1, 1)
            border = jnp.where(lane == at - 1, first, jnp.where(lane == at, second, border))
    block_out[border_at] = border
    own_out[BULK * cx + 1] = border
    to_left[0] = to_right[0] = border
    for f, values in enumerate([*cells_here, *part]):
        put_bulk(f, values)
    for e, values in enumerate([*part, press, perm, water, gas]):
        put_edge(EPART + e, values)
    put_inner(SUM, part[0] + part[1] + part[2])

    copies[9].wait()
    copies[10].wait()
    diag = [[diag_ref[a, b] for b in range(3)] for a in range(3)]
    inverse = 1.0 / (diag[0][0] + diag[1][0] + diag[2][0])
    put_bulk(INV, inverse)
    put_inner(6, inverse)

    def cofactor(a, b):
        return (
            diag[(a + 1) % 3][(b + 1) % 3] * diag[(a + 2) % 3][(b + 2) % 3]
            - diag[(a + 1) % 3][(b + 2) % 3] * diag[(a + 2) % 3][(b + 1) % 3]
        )

    cofactors = [[cofactor(a, b) for b in range(3)] for a in range(3)]
    over = 1.0 / (
        diag[0][0] * cofactors[0][0] + diag[0][1] * cofactors[0][1] + diag[0][2] * cofactors[0][2]
    )
    for a in range(3):
        put_edge(DCOL + a, diag[a][0])
        for b in range(3):
            solve = cofactors[b][a] * over
            dinv_out[3 * a + b] = solve
            put_edge(DINV + 3 * a + b, solve)

    for q in range(6):
        columns = [off_ref[q, c, 0] for c in range(3)]
        if q == 4:
            columns = [jnp.where(layer_at > 0, v, 0.0) for v in columns]
        if q == 5:
            columns = [jnp.where(layer_at < nz - 1, v, 0.0) for v in columns]
        coef = (columns[0] + columns[1] + columns[2]) * inverse
        put_bulk(COEF + q, coef)
        put_inner(q, coef)
        for c in range(3):
            put_edge(OFFC + 3 * q + c, columns[c])

    even = lax.rem(at_y, 2) == 0
    for x in range(cx):
        ya_out[x] = jnp.where(even, to_right[x], to_left[x])
        yb_out[x] = jnp.where(even, to_left[x], to_right[x])
        block_out[columns_at + x] = ya_out[x]
    for t, values in enumerate(beside):
        ya_out[cx + 1 + t] = values
        yb_out[cx + 1 + t] = values
    for spare in range(cx + 1 + len(beside), yb_out.shape[0]):
        yb_out[spare] = jnp.zeros((nz, cy), f32)
    for each in wells_copies:
        each.wait()


def main_kernel(count_x, count_y, offsets, *refs):
    width = len(offsets)
    (wells_ref, diag_ref, off_ref, dinv_ref, own_ref), refs = refs[:5], refs[5:]
    blocks, refs = (None, *refs[: width - 1]), refs[width - 1 :]
    ya_refs, refs = refs[:width], refs[width:]
    yb_refs, refs = refs[:width], refs[width:]
    residual_out, z_out, sums_out = refs

    cx, nz, cy = residual_out.shape[1:]
    total = width * cx
    at_x = lax.axis_index("gx")
    at_y = lax.axis_index("gy")
    even = lax.rem(at_y, 2) == 0
    has_left = jnp.where(at_y > 0, 1.0, 0.0).astype(f32)
    has_right = jnp.where(at_y < count_y - 1, 1.0, 0.0).astype(f32)
    layers = 1 if count_x == 2 else 2
    edge_at, border_at, last, columns_at, _ = sent_tiles(cx, layers)
    index_x = [lax.rem(at_x + (o % count_x), count_x) for o in offsets]
    joined = [
        jnp.where(index_x[(j + 1) % width] == index_x[j] + 1, 1.0, 0.0).astype(f32)
        for j in range(width)
    ]

    from_left, from_right = [], []
    for j in range(width):
        first, second = ya_refs[j][: cx + 1], yb_refs[j][: cx + 1]
        from_right.append(jnp.where(even, first, second) * has_right)
        from_left.append(jnp.where(even, second, first) * has_left)
    lane = iota((nz, cy), 1)

    merged = []
    for parity in range(2):
        of_right = lane < 0
        for f in range(parity, BULK, 2):
            of_right = of_right | ((lane >= f * WIDE) & (lane < (f + 1) * WIDE))
        merged.append(
            [
                jnp.where(of_right, from_right[j][x], from_left[j][x])
                for j in range(width)
                for x in range(cx)
            ]
        )

    def halo(f, x):
        tile = merged[f % 2][x]
        return pltpu.roll(tile, cy - f * WIDE, 1) if f else tile

    def arranged(edges, inner):
        if layers == 2:
            return jnp.stack([edges[0], *inner, edges[1]])
        first = [edges[0], *inner]
        second = [*inner, edges[0]]
        return jnp.stack([jnp.where(at_x == 0, a, b) for a, b in zip(first, second)])

    def received(j):
        block = blocks[j]
        edges = [
            [block[edge_at + side * EDGE + e] for e in range(EDGE)] for side in range(layers)
        ]
        inner = [
            [block[i * (cx - layers) + x] for x in range(cx - layers)] for i in range(INNER)
        ]
        zero = jnp.zeros((nz, cy), f32)
        part = [
            arranged(
                [edge[EPART + c] for edge in edges], inner[SUM] if c == 0 else [zero] * (cx - layers)
            )
            for c in range(3)
        ]
        scale = [1.0 / (edge[DCOL] + edge[DCOL + 1] + edge[DCOL + 2]) for edge in edges]
        coefs = [
            arranged(
                [
                    (edge[OFFC + 3 * q] + edge[OFFC + 3 * q + 1] + edge[OFFC + 3 * q + 2]) * by
                    for edge, by in zip(edges, scale)
                ],
                inner[q],
            )
            for q in range(6)
        ]
        return dict(enumerate([*part, arranged(scale, inner[6]), *coefs], start=PART))

    others = [received(j) for j in range(1, width)]

    def extended(f):
        own = jnp.concatenate(
            [own_ref[f * cx : (f + 1) * cx], *[other[f] for other in others]], axis=0
        )
        side = jnp.stack([halo(f, x) for x in range(total)])
        return jnp.concatenate([own, side], axis=2)

    lanes = 2 * cy
    level = iota((total, nz, lanes), 1)

    def next_x(v):
        return jnp.concatenate([v[1:], v[:1]], axis=0)

    def last_x(v):
        return jnp.concatenate([v[-1:], v[:-1]], axis=0)

    def next_y(v):
        return pltpu.roll(v, v.shape[2] - 1, 2)

    def last_y(v):
        return pltpu.roll(v, 1, 2)

    def next_z(v):
        return pltpu.roll(v, nz - 1, 1)

    def last_z(v):
        return pltpu.roll(v, 1, 1)

    def seam_after(v):
        rows = [v[i] for i in range(total)]
        for j in range(width):
            rows[j * cx + cx - 1] = rows[j * cx + cx - 1] * joined[j]
        return jnp.stack(rows)

    def seam_before(v):
        rows = [v[i] for i in range(total)]
        for j in range(width):
            at = ((j + 1) % width) * cx
            rows[at] = rows[at] * joined[j]
        return jnp.stack(rows)

    resid = [extended(PART + c) for c in range(3)]
    rows = [[resid[c][x] for x in range(total)] for c in range(3)]
    sides = {}

    def side_of(f, x):
        if (f, x) not in sides:
            sides[f, x] = halo(f, x)
        return sides[f, x]

    even_lane = lane % 2 == 0
    ends = (lane == 0) | (lane == cy - 1)
    for j in range(width):
        border = blocks[j][border_at] if j else own_ref[BULK * cx + 1]
        beyond = jnp.where(
            even_lane, pltpu.roll(from_left[j][0], cy - 1, 1), pltpu.roll(from_right[j][0], 1, 1)
        )
        backs = [cy - BORDER_AT - 2 * f * cx for f in range(FACE)]
        flows = face_flows(
            [pltpu.roll(beyond, back, 1) for back in backs],
            [pltpu.roll(border, back, 1) for back in backs],
            2.0,
        )
        for c in range(3):
            flow = jnp.where(lane < 2 * cx, flows[c], 0.0)
            swapped = jnp.where(even_lane, pltpu.roll(flow, cy - 1, 1), pltpu.roll(flow, 1, 1))
            for x in range(cx):
                back = cy - 2 * x - 1
                inward = jnp.where(ends, pltpu.roll(swapped, back, 1), 0.0)
                outward = jnp.where(ends, pltpu.roll(flow, back, 1), 0.0)
                at = j * cx + x
                rows[c][at] = rows[c][at] + jnp.concatenate([-inward, outward], axis=1)

    def edge_cells(j, last_layer):
        x = cx - 1 if last_layer else 0
        if j == 0:
            inside = [own_ref[f * cx + x] for f in range(FACE)]
        else:
            at = edge_at + (EDGE if last_layer and layers == 2 else 0)
            water, gas = blocks[j][at + EWATER], blocks[j][at + EGAS]
            inside = [
                blocks[j][at + EPRESS],
                *mobilities(water, gas),
                blocks[j][at + EPERM],
            ]
        return [
            jnp.concatenate([inside[f], side_of(f, j * cx + x)], axis=1) for f in range(FACE)
        ]

    for j in range(width):
        after = (j + 1) % width
        flows = face_flows(edge_cells(j, True), edge_cells(after, False), 2.0 * joined[j])
        for c in range(3):
            near_x, far_x = j * cx + cx - 1, after * cx
            rows[c][near_x] = rows[c][near_x] + flows[c]
            rows[c][far_x] = rows[c][far_x] - flows[c]
    resid = [jnp.stack(rows[c]) for c in range(3)]

    wells = wells_ref.shape[2]
    perfs = own_ref.shape[2]
    added = [[] for _ in range(3)]
    holes = jnp.zeros((16, wells), f32)
    lists = []
    for j in range(width):
        pair = jnp.sum(wells_ref[pl.ds(index_x[j] * count_y, count_y)], axis=0)
        holes = jnp.where(iota((16, wells), 0) == j, pair[1:2] / pair[0:1], holes)
        lists += [
            blocks[j][last] if j else own_ref[BULK * cx],
            from_left[j][cx],
            from_right[j][cx],
        ]
    listed = jnp.concatenate(lists, axis=1)
    number = iota((wells, perfs), 0).astype(f32)
    holes_at = jnp.concatenate(
        [split_dot(holes, hot_of(number == v[2:3]), NN) for v in lists], axis=1
    )
    for j in range(width):
        tiles = listed[:, 3 * perfs * j : 3 * perfs * (j + 1)]
        spot_xz, spot_y = tiles[0:1], tiles[1:2]
        fall = tiles[6:7] - holes_at[j : j + 1, 3 * perfs * j : 3 * perfs * (j + 1)]
        on_xz = iota((cx * nz, 3 * perfs), 0).astype(f32) == spot_xz
        spread = jnp.concatenate(
            [jnp.where(on_xz, tiles[3 + c : 4 + c] * fall, 0.0) for c in range(3)], axis=0
        )
        hot_y = iota((cy, 3 * perfs), 0).astype(f32) == spot_y
        nearby = iota((cy, 3 * perfs), 0)
        source = iota((cy, 3 * perfs), 1)
        kept = jnp.where(
            source < 2 * perfs, jnp.where(nearby >= cy - WIDE, 1, 0), jnp.where(nearby < WIDE, 1, 0)
        )
        hot_side = hot_of(hot_y & (kept == 1))
        inner = split_dot(spread[:, :perfs], hot_of(hot_y[:, :perfs]), NT)
        inner = inner.reshape(3, cx, nz, cy)
        aside = spread[:, perfs:]
        if j:
            aside = aside.reshape(3, cx * nz, 2 * perfs)
            aside = aside[0] + aside[1] + aside[2]
        outer = split_dot(aside, hot_side[:, perfs:], NT).reshape(-1, cx, nz, cy)
        for c in range(3):
            side = outer[c] if c < outer.shape[0] else jnp.zeros_like(outer[0])
            added[c].append(jnp.concatenate([inner[c], side], axis=2))
    start = [-(resid[c] + jnp.concatenate(added[c], axis=0)) for c in range(3)]
    for c in range(3):
        residual_out[c] = -start[c][:cx, :, :cy]

    coefs = [extended(COEF + q) for q in range(6)]
    coefs[0] = seam_before(coefs[0])
    coefs[1] = seam_after(coefs[1])
    scaled = (start[0] + start[1] + start[2]) * extended(INV)
    steps = (last_x, next_x, last_y, next_y, last_z, next_z)
    part = scaled
    for _ in range(1, SWEEPS):
        along_x, along_y, along_z = (
            coefs[q] * steps[q](part) + coefs[q + 1] * steps[q + 1](part) for q in (0, 2, 4)
        )
        part = (scaled - along_x) - (along_z + along_y)

    near = [step(part) for step in steps]
    near[0] = seam_before(near[0])
    near[1] = seam_after(near[1])
    near[4] = jnp.where(level > 0, near[4], 0.0)
    near[5] = jnp.where(level < nz - 1, near[5], 0.0)

    def direction(edge_of, here, around, initial):
        rest = []
        for c in range(3):
            coupled = [edge_of(OFFC + 3 * q + c) * beyond for q, beyond in enumerate(around)]
            rest.append(initial[c] - total_of([edge_of(DCOL + c) * here, *coupled]))
        solved = []
        for a in range(3):
            value = edge_of(DINV + 3 * a) * rest[0]
            value = value + edge_of(DINV + 3 * a + 1) * rest[1]
            solved.append(value + edge_of(DINV + 3 * a + 2) * rest[2])
        solved[0] = solved[0] + here
        return solved

    def edge_own(e):
        if e < DCOL:
            return dinv_ref[e]
        if e < OFFC:
            return diag_ref[e - DCOL, 0]
        return off_ref[(e - OFFC) // 3, (e - OFFC) % 3, 0]

    beside = []
    for t in range(cx + 1, cx + 1 - (-SEAM * 2 * cx // cy)):
        one, two = ya_refs[0][t], yb_refs[0][t]
        left, right = jnp.where(even, two, one) * has_left, jnp.where(even, one, two) * has_right
        beside.append(jnp.where(even_lane, left, right))

    def edge_side(e):
        tile, place = divmod(2 * cx * e, cy)
        return pltpu.roll(beside[tile], cy - place, 1) if place else beside[tile]

    def packed(tiles, shift):
        result = jnp.zeros((nz, cy), f32)
        for x in range(cx):
            turned = pltpu.roll(tiles[x], (2 * x + shift) % cy, 1)
            result = jnp.where((lane >= 2 * x) & (lane < 2 * x + 2), turned, result)
        return result

    inside = [part[x, :, :cy] for x in range(cx)]
    outside = [part[x, :, cy:] for x in range(cx)]
    here = packed(outside, 1)
    depth = iota((nz, cy), 0)
    z_side = direction(
        edge_side,
        here,
        [
            packed([part[total - 1, :, cy:] * joined[width - 1], *outside[:-1]], 1),
            packed([*outside[1:], part[cx % total, :, cy:] * joined[0]], 1),
            packed([jnp.where(lane == cy - 1, a, b) for a, b in zip(inside, outside)], 2),
            packed([jnp.where(lane == 0, a, b) for a, b in zip(inside, outside)], 0),
            jnp.where(depth > 0, pltpu.roll(here, 1, 0), 0.0),
            jnp.where(depth < nz - 1, pltpu.roll(here, nz - 1, 0), 0.0),
        ],
        [packed([start[c][x, :, cy:] for x in range(cx)], 1) for c in range(3)],
    )

    def direction_at(edge_of, where):
        return direction(
            edge_of, where(part), [where(v) for v in near], [where(v) for v in start]
        )

    after, before = 1 % width, width - 1
    z_own = direction_at(edge_own, lambda v: v[:cx, :, :cy])
    if layers == 1:
        z_next = z_last = direction_at(
            lambda e: blocks[after][edge_at + e],
            lambda v: jnp.where(at_x == 0, v[cx, :, :cy], v[total - 1, :, :cy]),
        )
    else:
        z_next = direction_at(
            lambda e: blocks[after][edge_at + e], lambda v: v[after * cx, :, :cy]
        )
        z_last = direction_at(
            lambda e: blocks[before][edge_at + EDGE + e],
            lambda v: v[before * cx + cx - 1, :, :cy],
        )
    level_own = iota((cx, nz, cy), 1)
    around = []
    for k in range(3):
        z_out[k] = z_own[k]
        before_y, after_y = [], []
        for x in range(cx):
            left = pltpu.roll(z_side[k], (cy - 2 * x) % cy, 1) if x else z_side[k]
            right = pltpu.roll(z_side[k], (cy - 2 - 2 * x) % cy, 1)
            before_y.append(jnp.where(lane == 0, left, pltpu.roll(z_own[k][x], 1, 1)))
            after_y.append(
                jnp.where(lane == cy - 1, right, pltpu.roll(z_own[k][x], cy - 1, 1))
            )
        around.append(
            [
                jnp.concatenate([(z_last[k] * joined[width - 1])[None], z_own[k][:-1]], axis=0),
                jnp.concatenate([z_own[k][1:], (z_next[k] * joined[0])[None]], axis=0),
                jnp.stack(before_y),
                jnp.stack(after_y),
                jnp.where(level_own > 0, last_z(z_own[k]), 0.0),
                jnp.where(level_own < nz - 1, next_z(z_own[k]), 0.0),
            ]
        )
    along = jnp.zeros((nz, cy), f32)
    square = jnp.zeros((nz, cy), f32)
    for c in range(3):
        terms = [diag_ref[c, k] * z_own[k] for k in range(3)]
        terms += [off_ref[q, c, k] * around[k][q] for q in range(6) for k in range(3)]
        mapped = total_of(terms)
        along = along + jnp.sum(mapped * start[c][:cx, :, :cy], axis=0)
        square = square + jnp.sum(mapped * mapped, axis=0)
    along = jnp.sum(along, axis=0, keepdims=True)
    square = jnp.sum(square, axis=0, keepdims=True)
    pair = jnp.where(iota((2, cy), 0) == 0, along, square)
    sums_out[...] = jnp.broadcast_to(pair[None], sums_out.shape)


def after_kernel(sums_ref, z_ref, residual_ref, update_hbm, residual_hbm, update_out, sem, sems):
    copy = pltpu.make_async_copy(residual_ref, residual_hbm, sem)
    pair = jnp.sum(sums_ref[...], axis=0)
    both = jnp.sum(pair, axis=1, keepdims=True)
    step = both[0:1] / both[1:2]
    copies = []
    for c in range(3):
        update_out[c] = z_ref[c] * step[None]
        copies.append(pltpu.make_async_copy(update_out.at[c], update_hbm.at[c], sems.at[c]))
        copies[-1].start()
    copy.start()
    for each in [copy, *copies]:
        each.wait()


def other_pair(device, count_x, count_y):
    x, y = divmod(device, count_y)
    near = y + 1 if y % 2 else y - 1
    if 0 <= near < count_y:
        return x * count_y + near
    return (x ^ 1) * count_y + y if count_x % 2 == 0 else device


def body(
    pressure,
    saturation,
    saturation_old,
    pore_volume,
    permeability,
    jac_diag,
    jac_off,
    perf_cell,
    perf_well,
    perf_index,
    well_rate,
):
    count_x, count_y = lax.axis_size("gx"), lax.axis_size("gy")
    devices = count_x * count_y
    cx, nz, cy = pressure.shape
    wells = well_rate.shape[1] * count_y
    layers = 1 if count_x == 2 else 2
    columns_at, tiles = sent_tiles(cx, layers)[-2:]
    groups = -(-SEAM * 2 * cx // cy)
    offsets = window(count_x, cx)
    width = len(offsets)
    shape = jax.ShapeDtypeStruct
    whole = pl.BlockSpec(memory_space=pltpu.VMEM)
    anywhere = pl.BlockSpec(memory_space=pltpu.HBM)
    params = pltpu.CompilerParams(vmem_limit_bytes=32 * 1024 * 1024)

    fields = (pressure, saturation, saturation_old, pore_volume, permeability, jac_diag)
    perforations = (perf_cell, perf_well, perf_index, well_rate)
    wells_part, block, own, ya, yb, dinv, diag, off = pl.pallas_call(
        functools.partial(before_kernel, count_x, count_y),
        in_specs=[anywhere] * 11,
        out_specs=[anywhere, *[whole] * 7],
        out_shape=[
            pltpu.HBM((devices, 2, wells), f32),
            shape((tiles, nz, cy), f32),
            shape((BULK * cx + 2, nz, cy), f32),
            shape((cx + 1 + groups, nz, cy), f32),
            shape((max(cx + 1 + groups, 2 * cx), nz, cy), f32),
            shape((9, cx, nz, cy), f32),
            shape(jac_diag.shape, f32),
            shape(jac_off.shape, f32),
        ],
        scratch_shapes=[
            *[pltpu.VMEM(v.shape, v.dtype) for v in fields[:5]],
            *[pltpu.VMEM(v.shape, v.dtype) for v in perforations],
            pltpu.VMEM((devices, 2, wells), f32),
            pltpu.SemaphoreType.DMA((13,)),
        ],
        compiler_params=params,
        name="before",
    )(*[pltpu.with_memory_space_constraint(v, pltpu.HBM) for v in (*fields, jac_off, *perforations)])

    pairs = [(i, i ^ 1) for i in range(count_y)]
    others = [(i, other_pair(i, count_x, count_y)) for i in range(devices)]

    def from_x(values, offset):
        return lax.ppermute(
            values, "gx", [((i + offset) % count_x, i) for i in range(count_x)]
        )

    ya_got = lax.ppermute(ya, "gy", pairs)
    yb_got = lax.ppermute(yb, ("gx", "gy"), others)
    blocks = [from_x(block, o) for o in offsets[1:]]
    wells_all = lax.all_to_all(wells_part, ("gx", "gy"), 0, 0)
    ya_all = [ya_got] + [lax.ppermute(v[columns_at:], "gy", pairs) for v in blocks]
    yb_all = [yb_got] + [from_x(yb_got, o) for o in offsets[1:]]

    residual, direction, sums = pl.pallas_call(
        functools.partial(main_kernel, count_x, count_y, tuple(offsets)),
        in_specs=[whole] * (4 + 3 * width),
        out_specs=[whole] * 3,
        out_shape=[
            shape((3, cx, nz, cy), f32),
            shape((3, cx, nz, cy), f32),
            shape((devices, 2, cy), f32),
        ],
        compiler_params=params,
        name="main",
    )(wells_all, diag, off, dinv, own, *blocks, *ya_all, *yb_all)

    sums_all = lax.all_to_all(sums, ("gx", "gy"), 0, 0)
    update, residual = pl.pallas_call(
        after_kernel,
        in_specs=[whole] * 3,
        out_specs=[anywhere] * 2,
        out_shape=[pltpu.HBM((3, cx, nz, cy), f32)] * 2,
        scratch_shapes=[
            pltpu.VMEM((3, cx, nz, cy), f32),
            pltpu.SemaphoreType.DMA,
            pltpu.SemaphoreType.DMA((3,)),
        ],
        compiler_params=params,
        name="after",
    )(sums_all, direction, residual)
    return (residual, update)


def solution(mesh):
    placed = (
        P("gx", None, "gy"),
        P(None, "gx", None, "gy"),
        P(None, "gx", None, "gy"),
        P("gx", None, "gy"),
        P("gx", None, "gy"),
        P(None, None, "gx", None, "gy"),
        P(None, None, None, "gx", None, "gy"),
        P("gx", "gy"),
        P("gx", "gy"),
        P("gx", "gy"),
        P("gx", "gy"),
    )
    return jax.shard_map(
        body,
        mesh=mesh,
        in_specs=placed,
        out_specs=(P(None, "gx", None, "gy"), P(None, "gx", None, "gy")),
        check_vma=False,
    )
```
